32 devices in a mesh: groups: 2 (over y), vocab: 8 (over z, x), rows: 2 (over core).
Axes of the slice: x: 2, y: 2, z: 4, core: 2. Of those that a mesh axis runs over, the one named last changes fastest.
Arguments:
- teacher_hidden: bfloat16 [64, 4608], P(('groups', 'vocab', 'rows')), parts along dimension 0, may hold values from -140 to 140
- student_hidden: bfloat16 [64, 3584], P(('groups', 'vocab', 'rows')), parts along dimension 0, may hold values from -140 to 140
- teacher_head: bfloat16 [4608, 1024], P(None, 'vocab'), may hold values from -0.176776695 to 0.176776695
- student_head: bfloat16 [3584, 1024], P(None, 'vocab'), may hold values from -0.20044593 to 0.20044593
- labels: int32 [64], P(('groups', 'vocab', 'rows')), parts along dimension 0, may hold values from 0 to 1023
Outputs:
- token_loss: float32 [64], P(('groups', 'vocab', 'rows')), parts along dimension 0
- hidden_grad: float32 [64, 3584], P(('groups', 'vocab', 'rows')), parts along dimension 0
- head_grad: float32 [7168, 1024], P('groups', 'vocab'), parts along dimension 0
The draws below stay inside these ranges and needn't reach their ends.
There are 2 independent parts, one for each index of `groups`. The reference program is written for one: setup_inputs(seed, part) draws one part's arguments, and reference() takes and returns one part's arrays. A program takes and returns all parts, laid end to end along the dimension named above; an argument that names none is the same for every part. Nothing has to cross between parts.
All inputs are finite; a program needn't handle non-finite values.
Results may differ from the reference program's by a relative error of at most 0.0021.
Values may be sent and summed in bfloat16 or wider, within the bound.
No kernel may reach another device: no remote copies, remote signals or barrier semaphores. Data moves between devices by JAX's collectives and lax.ppermute only.
A program may use at most 64 MiB of HBM per device.

```python
import math
import jax
import jax.numpy as jnp
import numpy as np
from jax import lax

DT = 4608
DS = 3584
VOCAB = 1024
TOKENS = 32


def column_rise():
    columns = lax.broadcasted_iota(jnp.float32, (1, VOCAB), 1)
    return jnp.exp(math.log(1.45) * columns / VOCAB)


def draw_teacher_hidden(key, part):
    key = jax.random.fold_in(key, 11)
    base_key, scale_key = jax.random.split(key, 2)
    values = jax.random.truncated_normal(base_key, -6.0, 6.0, (TOKENS, DT), jnp.float32)
    scales = 1.2 * jnp.exp(jax.random.uniform(scale_key, (TOKENS, 1), jnp.float32, 0.0, 0.69))
    return (values * scales).astype(jnp.bfloat16)


def draw_student_hidden(key, part):
    key = jax.random.fold_in(key, 23)
    base_key, scale_key = jax.random.split(key, 2)
    values = jax.random.truncated_normal(base_key, -6.0, 6.0, (TOKENS, DS), jnp.float32)
    scales = 1.2 * jnp.exp(jax.random.uniform(scale_key, (TOKENS, 1), jnp.float32, 0.0, 0.69))
    return (values * scales).astype(jnp.bfloat16)


def draw_teacher_head(key, part):
    key = jax.random.fold_in(key, 37)
    base_key, scale_key, common_key = jax.random.split(key, 3)
    common = 0.6 * jax.random.uniform(common_key, (DT, 1), jnp.float32, -1.0, 1.0)
    values = jax.random.truncated_normal(base_key, -6.0, 6.0, (DT, VOCAB), jnp.float32)
    scales = jnp.exp(jax.random.uniform(scale_key, (1, VOCAB), jnp.float32, -0.3, 0.3))
    return ((values * scales * column_rise() + common) / math.sqrt(DT)).astype(jnp.bfloat16)


def draw_student_head(key, part):
    key = jax.random.fold_in(key, 53)
    base_key, scale_key, common_key = jax.random.split(key, 3)
    common = 0.6 * jax.random.uniform(common_key, (DS, 1), jnp.float32, -1.0, 1.0)
    values = jax.random.truncated_normal(base_key, -6.0, 6.0, (DS, VOCAB), jnp.float32)
    scales = jnp.exp(jax.random.uniform(scale_key, (1, VOCAB), jnp.float32, -0.3, 0.3))
    return ((values * scales * column_rise() + common) / math.sqrt(DS)).astype(jnp.bfloat16)


def plant(result, stream_key, smallest, high):
    extent = result.shape
    place = [jax.random.randint(jax.random.fold_in(stream_key, axis), (), 0, extent[axis]) for axis in range(len(extent))]
    result = result.at[tuple(place)].set(smallest)
    longest = extent.index(max(extent))
    place[longest] = (place[longest] + 1) % extent[longest]
    return result.at[tuple(place)].set(high)


def cumulative_ranks(number_of, skew):
    loads = [(1 << 20) // math.isqrt(grade ** skew) + 1 for grade in range(1, number_of + 1)]
    width = 1 + sum(loads) // (1 << 30)
    return np.cumsum(np.array([max(1, weight // width) for weight in loads]))


def skewed_ids(stream_key, extent, count, slope):
    listing = cumulative_ranks(count, slope)
    lot = jax.random.randint(jax.random.fold_in(stream_key, 1), extent, 0, int(listing[count - 1]))
    grade = jnp.searchsorted(jnp.asarray(listing, jnp.int32), lot, side="right")
    return jax.random.permutation(jax.random.fold_in(stream_key, 2), count)[grade].astype(jnp.int32)


def setup_inputs(seed: int = 0, part: int = 0) -> dict:
    splits = jax.random.split(jax.random.key(seed), 6)
    part_keys = jax.random.split(jax.random.fold_in(splits[5], part), 6)
    return {
        "teacher_hidden": draw_teacher_hidden(jax.random.fold_in(jax.random.fold_in(splits[5], part), 71), part),
        "student_hidden": draw_student_hidden(jax.random.fold_in(jax.random.fold_in(splits[5], part), 71), part),
        "teacher_head": draw_teacher_head(jax.random.fold_in(splits[5], 71), part),
        "student_head": draw_student_head(jax.random.fold_in(splits[5], 71), part),
        "labels": plant(skewed_ids(part_keys[4], (TOKENS,), VOCAB, 2), jax.random.fold_in(part_keys[4], 3), 0, VOCAB - 1).astype(jnp.int32),
    }


def reference(teacher_hidden, student_hidden, teacher_head, student_head, labels):
    teacher_logits = jnp.dot(teacher_hidden, teacher_head, preferred_element_type=jnp.float32)
    student_logits = jnp.dot(student_hidden, student_head, preferred_element_type=jnp.float32)
    top_teacher = jnp.max(teacher_logits, axis=1)
    scaled = jnp.exp(teacher_logits - top_teacher[:, None])
    mass_teacher = jnp.sum(scaled, axis=1)
    cross_term = jnp.sum(scaled * (teacher_logits - student_logits), axis=1)
    top_student = jnp.max(student_logits, axis=1)
    student_scaled = jnp.exp(student_logits - top_student[:, None])
    mass_student = jnp.sum(student_scaled, axis=1)
    columns = lax.broadcasted_iota(jnp.int32, student_logits.shape, 1)
    target = labels.astype(jnp.int32)[:, None] == columns
    picked = jnp.sum(jnp.where(target, student_logits, jnp.zeros_like(student_logits)), axis=1)
    token_loss = cross_term / mass_teacher - top_teacher - jnp.log(mass_teacher) + 2.0 * (top_student + jnp.log(mass_student)) - picked
    teacher_prob = scaled / mass_teacher[:, None]
    student_prob = student_scaled / mass_student[:, None]
    logit_grad = (2.0 * student_prob - teacher_prob - target.astype(jnp.float32)).astype(jnp.bfloat16)
    hidden_grad = jnp.dot(logit_grad, student_head.T, preferred_element_type=jnp.float32)
    head_grad = jnp.dot(student_hidden.T, logit_grad, preferred_element_type=jnp.float32)
    return token_loss, hidden_grad, head_grad
```

```python
import jax
import jax.numpy as jnp
from jax import lax
from jax.sharding import PartitionSpec as P

F32 = jnp.float32
BF16 = jnp.bfloat16
CODE = 128


def spread(block, axis, size):
    copies = jnp.broadcast_to(block[None], (size,) + block.shape)
    return lax.all_to_all(copies, axis, split_axis=0, concat_axis=0, tiled=True)


def on_device(teacher_hidden, student_hidden, teacher_head, student_head, labels, *, shards):
    own, teacher_width = teacher_hidden.shape
    student_width = student_hidden.shape[1]
    columns_here = student_head.shape[1]
    first_column = lax.axis_index("vocab") * columns_here
    lanes = lax.broadcasted_iota(jnp.int32, (own, CODE), 1)
    digits = jnp.where(lanes == 0, (labels // 128)[:, None], (labels % 128)[:, None])
    payload = jnp.concatenate([teacher_hidden, student_hidden, digits.astype(BF16)], axis=1)
    rows = spread(payload, "vocab", shards).reshape(shards * own, -1)
    teacher_rows = rows[:, :teacher_width]
    student_rows = rows[:, teacher_width : teacher_width + student_width]
    code = rows[:, teacher_width + student_width :].astype(jnp.int32)
    label_rows = code[:, 0] * 128 + code[:, 1]
    other = [(0, 1), (1, 0)]
    student_other = lax.ppermute(student_rows, "rows", other)

    teacher_logits = jnp.dot(teacher_rows, teacher_head, preferred_element_type=F32)
    student_logits = jnp.dot(student_rows, student_head, preferred_element_type=F32)
    columns = lax.broadcasted_iota(jnp.int32, student_logits.shape, 1)
    target = (label_rows - first_column)[:, None] == columns
    top_t = jnp.max(teacher_logits, axis=1, keepdims=True)
    exp_t = jnp.exp(teacher_logits - top_t)
    top_s = jnp.max(student_logits, axis=1, keepdims=True)
    exp_s = jnp.exp(student_logits - top_s)
    stats = jnp.concatenate(
        [
            top_t,
            jnp.sum(exp_t, axis=1, keepdims=True),
            jnp.sum(exp_t * (teacher_logits - student_logits), axis=1, keepdims=True),
            top_s,
            jnp.sum(exp_s, axis=1, keepdims=True),
            jnp.sum(jnp.where(target, student_logits, 0.0), axis=1, keepdims=True),
        ],
        axis=1,
    )
    every = spread(stats, "vocab", shards)
    all_top_t = jnp.max(every[:, :, 0], axis=0)
    factor_t = jnp.exp(every[:, :, 0] - all_top_t[None])
    all_top_s = jnp.max(every[:, :, 3], axis=0)
    factor_s = jnp.exp(every[:, :, 3] - all_top_s[None])
    mass_t = jnp.sum(every[:, :, 1] * factor_t, axis=0)
    cross = jnp.sum(every[:, :, 2] * factor_t, axis=0)
    mass_s = jnp.sum(every[:, :, 4] * factor_s, axis=0)
    picked = jnp.sum(every[:, :, 5], axis=0)
    loss = cross / mass_t - all_top_t - jnp.log(mass_t) + 2.0 * (all_top_s + jnp.log(mass_s)) - picked
    token_loss = lax.dynamic_slice_in_dim(loss, lax.axis_index("vocab") * own, own, 0)

    teacher_prob = jnp.exp(teacher_logits - all_top_t[:, None]) / mass_t[:, None]
    student_prob = jnp.exp(student_logits - all_top_s[:, None]) / mass_s[:, None]
    grad_rows = (2.0 * student_prob - teacher_prob - target.astype(F32)).astype(BF16)
    grad_other = lax.ppermute(grad_rows, "rows", other)
    partial = lax.dot_general(grad_rows, student_head, (((1,), (1,)), ((), ())), preferred_element_type=F32)
    arrived = lax.all_to_all(partial.reshape(shards, own, student_width), "vocab", split_axis=0, concat_axis=0, tiled=True)
    hidden_grad = jnp.sum(arrived, axis=0)
    head_grad = lax.dot_general(
        jnp.concatenate([student_rows, student_other], axis=0),
        jnp.concatenate([grad_rows, grad_other], axis=0),
        (((0,), (0,)), ((), ())),
        preferred_element_type=F32,
    )
    return (token_loss, hidden_grad, head_grad)


def solution(mesh):
    tokens = ("groups", "vocab", "rows")
    in_specs = (P(tokens, None), P(tokens, None), P(None, "vocab"), P(None, "vocab"), P(tokens))
    out_specs = (P(tokens), P(tokens, None), P("groups", "vocab"))

    def body(*arrays):
        return on_device(*arrays, shards=mesh.shape["vocab"])

    return jax.shard_map(body, mesh=mesh, in_specs=in_specs, out_specs=out_specs, check_vma=False)
```

```python
import jax
import jax.numpy as jnp
from jax import lax
from jax.sharding import PartitionSpec as P

F32 = jnp.float32
BF16 = jnp.bfloat16
CODE = 128
DIRECT = 16


def spread(block, shards):
    copies = jnp.broadcast_to(block[None], (shards,) + block.shape)
    return lax.all_to_all(copies, "vocab", split_axis=0, concat_axis=0, tiled=True)


def from_peers(blocks, shards):
    return [blocks[0]] + [
        lax.ppermute(blocks[k], "vocab", [(i, i ^ k) for i in range(shards)]) for k in range(1, shards)
    ]


def gather_tokens(block, shards):
    if shards <= DIRECT:
        return jnp.concatenate(from_peers([block] * shards, shards), axis=0)
    return spread(block, shards).reshape(shards * block.shape[0], -1)


def gather_stats(stats, shards):
    if shards > DIRECT:
        return spread(stats, shards)
    own = stats.shape[0] // shards
    return jnp.stack(
        [
            jnp.concatenate([block[(i ^ k) * own : (i ^ k) * own + own] for i in range(shards)], axis=0)
            for k, block in enumerate(from_peers([stats] * shards, shards))
        ]
    )


def own_tokens(array, shards):
    own = array.shape[0] // shards
    if shards <= DIRECT:
        return array[:own]
    return lax.dynamic_slice_in_dim(array, lax.axis_index("vocab") * own, own, 0)


def sum_to_owner(partial, shards):
    own = partial.shape[0] // shards
    if shards > DIRECT:
        blocks = partial.reshape(shards, own, -1)
        return jnp.sum(lax.all_to_all(blocks, "vocab", split_axis=0, concat_axis=0, tiled=True), axis=0)
    arrived = from_peers([partial[k * own : k * own + own] for k in range(shards)], shards)
    total = arrived[0]
    for block in arrived[1:]:
        total = total + block
    return total


def on_device(teacher_hidden, student_hidden, teacher_head, student_head, labels, *, shards):
    own, teacher_width = teacher_hidden.shape
    student_width = student_hidden.shape[1]
    columns_here = student_head.shape[1]
    first_column = lax.axis_index("vocab") * columns_here
    lanes = lax.broadcasted_iota(jnp.int32, (own, CODE), 1)
    digits = jnp.where(lanes == 0, (labels // 128)[:, None], (labels % 128)[:, None])
    payload = jnp.concatenate([teacher_hidden, student_hidden, digits.astype(BF16)], axis=1)
    rows = gather_tokens(payload, shards)
    teacher_rows = rows[:, :teacher_width]
    student_rows = rows[:, teacher_width : teacher_width + student_width]
    code = rows[:, teacher_width + student_width :].astype(jnp.int32)
    label_rows = code[:, 0] * 128 + code[:, 1]
    other = [(0, 1), (1, 0)]
    student_other = lax.ppermute(student_rows, "rows", other)

    teacher_logits = jnp.dot(teacher_rows, teacher_head, preferred_element_type=F32)
    student_logits = jnp.dot(student_rows, student_head, preferred_element_type=F32)
    columns = lax.broadcasted_iota(jnp.int32, student_logits.shape, 1)
    target = (label_rows - first_column)[:, None] == columns
    top_t = jnp.max(teacher_logits, axis=1, keepdims=True)
    exp_t = jnp.exp(teacher_logits - top_t)
    top_s = jnp.max(student_logits, axis=1, keepdims=True)
    exp_s = jnp.exp(student_logits - top_s)
    stats = jnp.concatenate(
        [
            top_t,
            jnp.sum(exp_t, axis=1, keepdims=True),
            jnp.sum(exp_t * (teacher_logits - student_logits), axis=1, keepdims=True),
            top_s,
            jnp.sum(exp_s, axis=1, keepdims=True),
            jnp.sum(jnp.where(target, student_logits, 0.0), axis=1, keepdims=True),
        ],
        axis=1,
    )
    every = gather_stats(stats, shards)
    all_top_t = jnp.max(every[:, :, 0], axis=0)
    factor_t = jnp.exp(every[:, :, 0] - all_top_t[None])
    all_top_s = jnp.max(every[:, :, 3], axis=0)
    factor_s = jnp.exp(every[:, :, 3] - all_top_s[None])
    mass_t = jnp.sum(every[:, :, 1] * factor_t, axis=0)
    cross = jnp.sum(every[:, :, 2] * factor_t, axis=0)
    mass_s = jnp.sum(every[:, :, 4] * factor_s, axis=0)
    picked = jnp.sum(every[:, :, 5], axis=0)
    loss = cross / mass_t - all_top_t - jnp.log(mass_t) + 2.0 * (all_top_s + jnp.log(mass_s)) - picked
    token_loss = own_tokens(loss, shards)

    teacher_prob = jnp.exp(teacher_logits - all_top_t[:, None]) / mass_t[:, None]
    student_prob = jnp.exp(student_logits - all_top_s[:, None]) / mass_s[:, None]
    grad_rows = (2.0 * student_prob - teacher_prob - target.astype(F32)).astype(BF16)
    grad_other = lax.ppermute(grad_rows, "rows", other)
    partial = lax.dot_general(grad_rows, student_head, (((1,), (1,)), ((), ())), preferred_element_type=F32)
    hidden_grad = sum_to_owner(partial, shards)
    head_grad = lax.dot_general(
        jnp.concatenate([student_rows, student_other], axis=0),
        jnp.concatenate([grad_rows, grad_other], axis=0),
        (((0,), (0,)), ((), ())),
        preferred_element_type=F32,
    )
    return (token_loss, hidden_grad, head_grad)


def solution(mesh):
    tokens = ("groups", "vocab", "rows")
    in_specs = (P(tokens, None), P(tokens, None), P(None, "vocab"), P(None, "vocab"), P(tokens))
    out_specs = (P(tokens), P(tokens, None), P("groups", "vocab"))

    def body(*arrays):
        return on_device(*arrays, shards=mesh.shape["vocab"])

    return jax.shard_map(body, mesh=mesh, in_specs=in_specs, out_specs=out_specs, check_vma=False)
```

```python
import jax
import jax.numpy as jnp
from jax import lax
from jax.sharding import PartitionSpec as P

F32 = jnp.float32
BF16 = jnp.bfloat16
CODE = 128


def spread(block, axis, size):
    copies = jnp.broadcast_to(block[None], (size,) + block.shape)
    return lax.all_to_all(copies, axis, split_axis=0, concat_axis=0, tiled=True)


def on_device(teacher_hidden, student_hidden, teacher_head, student_head, labels, *, shards):
    own, teacher_width = teacher_hidden.shape
    student_width = student_hidden.shape[1]
    columns_here = student_head.shape[1]
    first_column = lax.axis_index("vocab") * columns_here
    lanes = lax.broadcasted_iota(jnp.int32, (own, CODE), 1)
    digits = jnp.where(lanes == 0, (labels // 128)[:, None], (labels % 128)[:, None])
    payload = jnp.concatenate([teacher_hidden, student_hidden, digits.astype(BF16)], axis=1)
    rows = spread(payload, "vocab", shards).reshape(shards * own, -1)
    teacher_rows = rows[:, :teacher_width]
    student_rows = rows[:, teacher_width : teacher_width + student_width]
    code = rows[:, teacher_width + student_width :].astype(jnp.int32)
    label_rows = code[:, 0] * 128 + code[:, 1]
    other = [(0, 1), (1, 0)]
    student_other = lax.ppermute(student_rows, "rows", other)

    teacher_logits = jnp.dot(teacher_rows, teacher_head, preferred_element_type=F32)
    student_logits = jnp.dot(student_rows, student_head, preferred_element_type=F32)
    columns = lax.broadcasted_iota(jnp.int32, student_logits.shape, 1)
    target = (label_rows - first_column)[:, None] == columns
    top_t = jnp.max(teacher_logits, axis=1, keepdims=True)
    exp_t = jnp.exp(teacher_logits - top_t)
    top_s = jnp.max(student_logits, axis=1, keepdims=True)
    exp_s = jnp.exp(student_logits - top_s)
    stats = jnp.concatenate(
        [
            top_t,
            jnp.sum(exp_t, axis=1, keepdims=True),
            jnp.sum(exp_t * (teacher_logits - student_logits), axis=1, keepdims=True),
            top_s,
            jnp.sum(exp_s, axis=1, keepdims=True),
            jnp.sum(jnp.where(target, student_logits, 0.0), axis=1, keepdims=True),
        ],
        axis=1,
    )
    here = lax.axis_index("vocab")
    flat = stats.T.reshape(1, -1)
    mine = lax.broadcasted_iota(jnp.int32, (shards, 1), 0) == here
    every = lax.psum(jnp.where(mine, flat, 0.0), "vocab").reshape(shards, 6, shards * own)
    all_top_t = jnp.max(every[:, 0], axis=0)
    factor_t = jnp.exp(every[:, 0] - all_top_t[None])
    all_top_s = jnp.max(every[:, 3], axis=0)
    factor_s = jnp.exp(every[:, 3] - all_top_s[None])
    mass_t = jnp.sum(every[:, 1] * factor_t, axis=0)
    cross = jnp.sum(every[:, 2] * factor_t, axis=0)
    mass_s = jnp.sum(every[:, 4] * factor_s, axis=0)
    picked = jnp.sum(every[:, 5], axis=0)
    loss = cross / mass_t - all_top_t - jnp.log(mass_t) + 2.0 * (all_top_s + jnp.log(mass_s)) - picked
    token_loss = lax.dynamic_slice_in_dim(loss, lax.axis_index("vocab") * own, own, 0)

    teacher_prob = jnp.exp(teacher_logits - all_top_t[:, None]) / mass_t[:, None]
    student_prob = jnp.exp(student_logits - all_top_s[:, None]) / mass_s[:, None]
    grad_rows = (2.0 * student_prob - teacher_prob - target.astype(F32)).astype(BF16)
    grad_other = lax.ppermute(grad_rows, "rows", other)
    partial = lax.dot_general(grad_rows, student_head, (((1,), (1,)), ((), ())), preferred_element_type=F32)
    arrived = lax.all_to_all(
        partial.astype(BF16).reshape(shards, own, student_width), "vocab", split_axis=0, concat_axis=0, tiled=True
    )
    own_partial = lax.dynamic_slice_in_dim(partial, here * own, own, 0)
    hidden_grad = own_partial + jnp.sum(jnp.where(mine[:, :, None], 0.0, arrived.astype(F32)), axis=0)
    head_grad = lax.dot_general(
        jnp.concatenate([student_rows, student_other], axis=0),
        jnp.concatenate([grad_rows, grad_other], axis=0),
        (((0,), (0,)), ((), ())),
        preferred_element_type=F32,
    )
    return (token_loss, hidden_grad, head_grad)


def solution(mesh):
    tokens = ("groups", "vocab", "rows")
    in_specs = (P(tokens, None), P(tokens, None), P(None, "vocab"), P(None, "vocab"), P(tokens))
    out_specs = (P(tokens), P(tokens, None), P("groups", "vocab"))

    def body(*arrays):
        return on_device(*arrays, shards=mesh.shape["vocab"])

    return jax.shard_map(body, mesh=mesh, in_specs=in_specs, out_specs=out_specs, check_vma=False)
```

```python
import jax
import jax.numpy as jnp
from jax import lax
from jax.experimental import pallas as pl
from jax.experimental.pallas import tpu as pltpu
from jax.sharding import PartitionSpec as P

F32 = jnp.float32
BF16 = jnp.bfloat16
CODE = 128


UNROLL = 16
SMEM = pl.BlockSpec(memory_space=pltpu.SMEM)
VMEM = pl.BlockSpec(memory_space=pltpu.VMEM)


def over_shards(shards, body):
    if shards <= UNROLL:
        for shard in range(shards):
            body(shard)
    else:
        pl.loop(0, shards)(body)


def swap(blocks):
    return lax.all_to_all(blocks, "vocab", split_axis=0, concat_axis=0, tiled=True)


def payload_kernel(labels_ref, teacher_ref, student_ref, out_ref):
    shards, own, _ = out_ref.shape
    teacher_width, student_width = teacher_ref.shape[1], student_ref.shape[1]
    row = lax.broadcasted_iota(jnp.int32, (own, CODE), 0)
    lane = lax.broadcasted_iota(jnp.int32, (own, CODE), 1)
    digits = jnp.zeros((own, CODE), jnp.int32)
    for token in range(own):
        label = labels_ref[token]
        pair = jnp.where(lane == 0, label >> 7, label & 127)
        digits = jnp.where(row == token, pair, digits)
    teacher = teacher_ref[...]
    student = student_ref[...]
    code = digits.astype(F32).astype(BF16)

    def write(shard):
        out_ref[shard, :, :teacher_width] = teacher
        out_ref[shard, :, teacher_width : teacher_width + student_width] = student
        out_ref[shard, :, teacher_width + student_width :] = code

    over_shards(shards, write)


def partial_kernel(here_ref, grad_ref, head_ref, out_ref, own_ref, total_ref):
    shards, own, _ = out_ref.shape
    total_ref[...] = lax.dot_general(
        grad_ref[...], head_ref[...], (((1,), (1,)), ((), ())), preferred_element_type=F32
    )

    together = 8 // own

    def write(group):
        start = group * 8 if isinstance(group, int) else pl.multiple_of(group * 8, 8)
        rows = total_ref[pl.ds(start, 8), :]
        for place in range(together):
            shard = group * together + place
            block = rows[place * own : place * own + own]
            out_ref[shard] = block.astype(BF16)

            @pl.when(shard == here_ref[0])
            def _():
                own_ref[...] = block

    over_shards(shards // together, write)


def sum_kernel(here_ref, arrived_ref, own_ref, out_ref):
    out_ref[...] = own_ref[...]

    def add(shard):
        block = arrived_ref[shard].astype(F32)
        out_ref[...] += jnp.where(shard == here_ref[0], jnp.zeros_like(block), block)

    over_shards(arrived_ref.shape[0], add)


def on_device(teacher_hidden, student_hidden, teacher_head, student_head, labels, *, shards):
    own, teacher_width = teacher_hidden.shape
    student_width = student_hidden.shape[1]
    columns_here = student_head.shape[1]
    first_column = lax.axis_index("vocab") * columns_here
    here = lax.axis_index("vocab").astype(jnp.int32)[None]
    payload = pl.pallas_call(
        payload_kernel,
        out_shape=jax.ShapeDtypeStruct((shards, own, teacher_width + student_width + CODE), BF16),
        in_specs=[SMEM, VMEM, VMEM],
        out_specs=VMEM,
    )(labels, teacher_hidden, student_hidden)
    rows = swap(payload).reshape(shards * own, -1)
    teacher_rows = rows[:, :teacher_width]
    student_rows = rows[:, teacher_width : teacher_width + student_width]
    code = rows[:, teacher_width + student_width :].astype(jnp.int32)
    label_rows = code[:, 0] * 128 + code[:, 1]
    other = [(0, 1), (1, 0)]
    student_other = lax.ppermute(student_rows, "rows", other)

    teacher_logits = jnp.dot(teacher_rows, teacher_head, preferred_element_type=F32)
    student_logits = jnp.dot(student_rows, student_head, preferred_element_type=F32)
    columns = lax.broadcasted_iota(jnp.int32, student_logits.shape, 1)
    target = (label_rows - first_column)[:, None] == columns
    top_t = jnp.max(teacher_logits, axis=1, keepdims=True)
    exp_t = jnp.exp(teacher_logits - top_t)
    top_s = jnp.max(student_logits, axis=1, keepdims=True)
    exp_s = jnp.exp(student_logits - top_s)
    stats = jnp.stack(
        [
            top_t[:, 0],
            jnp.sum(exp_t, axis=1),
            jnp.sum(exp_t * (teacher_logits - student_logits), axis=1),
            top_s[:, 0],
            jnp.sum(exp_s, axis=1),
            jnp.sum(jnp.where(target, student_logits, 0.0), axis=1),
        ]
    )
    lanes = -(-shards * own // 128) * 128
    stats = jnp.pad(stats, ((0, 2), (0, lanes - shards * own)))
    every = swap(jnp.broadcast_to(stats[None], (shards,) + stats.shape))[:, :, : shards * own]
    all_top_t = jnp.max(every[:, 0], axis=0)
    factor_t = jnp.exp(every[:, 0] - all_top_t[None])
    all_top_s = jnp.max(every[:, 3], axis=0)
    factor_s = jnp.exp(every[:, 3] - all_top_s[None])
    mass_t = jnp.sum(every[:, 1] * factor_t, axis=0)
    cross = jnp.sum(every[:, 2] * factor_t, axis=0)
    mass_s = jnp.sum(every[:, 4] * factor_s, axis=0)
    picked = jnp.sum(every[:, 5], axis=0)
    loss = cross / mass_t - all_top_t - jnp.log(mass_t) + 2.0 * (all_top_s + jnp.log(mass_s)) - picked
    token_loss = lax.dynamic_slice_in_dim(loss, lax.axis_index("vocab") * own, own, 0)

    teacher_prob = jnp.exp(teacher_logits - all_top_t[:, None]) / mass_t[:, None]
    student_prob = jnp.exp(student_logits - all_top_s[:, None]) / mass_s[:, None]
    grad_rows = (2.0 * student_prob - teacher_prob - target.astype(F32)).astype(BF16)
    grad_other = lax.ppermute(grad_rows, "rows", other)
    block = (shards, own, student_width)
    partials, own_partial = pl.pallas_call(
        partial_kernel,
        out_shape=(jax.ShapeDtypeStruct(block, BF16), jax.ShapeDtypeStruct(block[1:], F32)),
        in_specs=[SMEM, VMEM, VMEM],
        out_specs=(VMEM, VMEM),
        scratch_shapes=[pltpu.VMEM((shards * own, student_width), F32)],
    )(here, grad_rows, student_head)
    hidden_grad = pl.pallas_call(
        sum_kernel,
        out_shape=jax.ShapeDtypeStruct(block[1:], F32),
        in_specs=[SMEM, VMEM, VMEM],
        out_specs=VMEM,
    )(here, swap(partials), own_partial)
    head_grad = lax.dot_general(
        jnp.concatenate([student_rows, student_other], axis=0),
        jnp.concatenate([grad_rows, grad_other], axis=0),
        (((0,), (0,)), ((), ())),
        preferred_element_type=F32,
    )
    return (token_loss, hidden_grad, head_grad)


def solution(mesh):
    tokens = ("groups", "vocab", "rows")
    in_specs = (P(tokens, None), P(tokens, None), P(None, "vocab"), P(None, "vocab"), P(tokens))
    out_specs = (P(tokens), P(tokens, None), P("groups", "vocab"))

    def body(*arrays):
        return on_device(*arrays, shards=mesh.shape["vocab"])

    return jax.shard_map(body, mesh=mesh, in_specs=in_specs, out_specs=out_specs, check_vma=False)
```

```python
import jax
import jax.numpy as jnp
from jax import lax
from jax.experimental import pallas as pl
from jax.experimental.pallas import tpu as pltpu
from jax.sharding import PartitionSpec as P

F32 = jnp.float32
BF16 = jnp.bfloat16
CODE = 128


UNROLL = 16
SMEM = pl.BlockSpec(memory_space=pltpu.SMEM)
VMEM = pl.BlockSpec(memory_space=pltpu.VMEM)


def over_shards(shards, body):
    if shards <= UNROLL:
        for shard in range(shards):
            body(shard)
    else:
        pl.loop(0, shards)(body)


def swap(blocks):
    return lax.all_to_all(blocks, "vocab", split_axis=0, concat_axis=0, tiled=True)


def payload_kernel(labels_ref, teacher_ref, student_ref, out_ref):
    shards, own, _ = out_ref.shape
    teacher_width, student_width = teacher_ref.shape[1], student_ref.shape[1]
    row = lax.broadcasted_iota(jnp.int32, (own, CODE), 0)
    lane = lax.broadcasted_iota(jnp.int32, (own, CODE), 1)
    digits = jnp.zeros((own, CODE), jnp.int32)
    for token in range(own):
        label = labels_ref[token]
        pair = jnp.where(lane == 0, label >> 7, label & 127)
        digits = jnp.where(row == token, pair, digits)
    teacher = teacher_ref[...]
    student = student_ref[...]
    code = digits.astype(F32).astype(BF16)

    def write(shard):
        out_ref[shard, :, :teacher_width] = teacher
        out_ref[shard, :, teacher_width : teacher_width + student_width] = student
        out_ref[shard, :, teacher_width + student_width :] = code

    over_shards(shards, write)


def gather_stats(block, shards):
    held = block[None]
    bit = 1
    while bit < shards:
        arrived = lax.ppermute(held, "vocab", [(i, i ^ bit) for i in range(shards)])
        held = jnp.concatenate([held, arrived], axis=0)
        bit *= 2
    return held


def on_device(teacher_hidden, student_hidden, teacher_head, student_head, labels, *, shards):
    own, teacher_width = teacher_hidden.shape
    student_width = student_hidden.shape[1]
    columns_here = student_head.shape[1]
    first_column = lax.axis_index("vocab") * columns_here
    here = lax.axis_index("vocab").astype(jnp.int32)[None]
    payload = pl.pallas_call(
        payload_kernel,
        out_shape=jax.ShapeDtypeStruct((shards, own, teacher_width + student_width + CODE), BF16),
        in_specs=[SMEM, VMEM, VMEM],
        out_specs=VMEM,
    )(labels, teacher_hidden, student_hidden)
    rows = swap(payload).reshape(shards * own, -1)
    teacher_rows = rows[:, :teacher_width]
    student_rows = rows[:, teacher_width : teacher_width + student_width]
    code = rows[:, teacher_width + student_width :].astype(jnp.int32)
    label_rows = code[:, 0] * 128 + code[:, 1]
    other = [(0, 1), (1, 0)]
    student_other = lax.ppermute(student_rows, "rows", other)

    teacher_logits = jnp.dot(teacher_rows, teacher_head, preferred_element_type=F32)
    student_logits = jnp.dot(student_rows, student_head, preferred_element_type=F32)
    columns = lax.broadcasted_iota(jnp.int32, student_logits.shape, 1)
    target = (label_rows - first_column)[:, None] == columns
    top_t = jnp.max(teacher_logits, axis=1, keepdims=True)
    exp_t = jnp.exp(teacher_logits - top_t)
    top_s = jnp.max(student_logits, axis=1, keepdims=True)
    exp_s = jnp.exp(student_logits - top_s)
    stats = jnp.stack(
        [
            top_t[:, 0],
            jnp.sum(exp_t, axis=1),
            jnp.sum(exp_t * (teacher_logits - student_logits), axis=1),
            top_s[:, 0],
            jnp.sum(exp_s, axis=1),
            jnp.sum(jnp.where(target, student_logits, 0.0), axis=1),
        ]
    )
    lanes = -(-shards * own // 128) * 128
    stats = jnp.pad(stats, ((0, 2), (0, lanes - shards * own)))
    every = gather_stats(stats, shards)[:, :, : shards * own]
    all_top_t = jnp.max(every[:, 0], axis=0)
    factor_t = jnp.exp(every[:, 0] - all_top_t[None])
    all_top_s = jnp.max(every[:, 3], axis=0)
    factor_s = jnp.exp(every[:, 3] - all_top_s[None])
    mass_t = jnp.sum(every[:, 1] * factor_t, axis=0)
    cross = jnp.sum(every[:, 2] * factor_t, axis=0)
    mass_s = jnp.sum(every[:, 4] * factor_s, axis=0)
    picked = jnp.sum(every[:, 5], axis=0)
    loss = cross / mass_t - all_top_t - jnp.log(mass_t) + 2.0 * (all_top_s + jnp.log(mass_s)) - picked
    token_loss = lax.dynamic_slice_in_dim(loss, lax.axis_index("vocab") * own, own, 0)

    teacher_prob = jnp.exp(teacher_logits - all_top_t[:, None]) / mass_t[:, None]
    student_prob = jnp.exp(student_logits - all_top_s[:, None]) / mass_s[:, None]
    grad_rows = (2.0 * student_prob - teacher_prob - target.astype(F32)).astype(BF16)
    grad_other = lax.ppermute(grad_rows, "rows", other)
    partial = lax.dot_general(grad_rows, student_head, (((1,), (1,)), ((), ())), preferred_element_type=F32)
    arrived = swap(partial.astype(BF16).reshape(shards, own, student_width)).astype(F32)
    own_grad = lax.dynamic_slice_in_dim(grad_rows, here[0] * own, own, 0)
    own_partial = lax.dot_general(own_grad, student_head, (((1,), (1,)), ((), ())), preferred_element_type=F32)
    others = lax.broadcasted_iota(jnp.int32, (shards, 1, 1), 0) != here[0]
    hidden_grad = own_partial + jnp.sum(jnp.where(others, arrived, 0.0), axis=0)
    head_grad = lax.dot_general(
        jnp.concatenate([student_rows, student_other], axis=0),
        jnp.concatenate([grad_rows, grad_other], axis=0),
        (((0,), (0,)), ((), ())),
        preferred_element_type=F32,
    )
    return (token_loss, hidden_grad, head_grad)


def solution(mesh):
    tokens = ("groups", "vocab", "rows")
    in_specs = (P(tokens, None), P(tokens, None), P(None, "vocab"), P(None, "vocab"), P(tokens))
    out_specs = (P(tokens), P(tokens, None), P("groups", "vocab"))

    def body(*arrays):
        return on_device(*arrays, shards=mesh.shape["vocab"])

    return jax.shard_map(body, mesh=mesh, in_specs=in_specs, out_specs=out_specs, check_vma=False)
```

```python
import jax
import jax.numpy as jnp
from jax import lax
from jax.experimental import pallas as pl
from jax.experimental.pallas import tpu as pltpu
from jax.sharding import PartitionSpec as P

F32 = jnp.float32
BF16 = jnp.bfloat16
CODE = 128


UNROLL = 16
SMEM = pl.BlockSpec(memory_space=pltpu.SMEM)
VMEM = pl.BlockSpec(memory_space=pltpu.VMEM)


def over_shards(shards, body):
    if shards <= UNROLL:
        for shard in range(shards):
            body(shard)
    else:
        pl.loop(0, shards)(body)


def swap(blocks):
    return lax.all_to_all(blocks, "vocab", split_axis=0, concat_axis=0, tiled=True)


def payload_kernel(labels_ref, teacher_ref, student_ref, out_ref):
    shards, own, _ = out_ref.shape
    teacher_width, student_width = teacher_ref.shape[1], student_ref.shape[1]
    row = lax.broadcasted_iota(jnp.int32, (own, CODE), 0)
    lane = lax.broadcasted_iota(jnp.int32, (own, CODE), 1)
    digits = jnp.zeros((own, CODE), jnp.int32)
    for token in range(own):
        label = labels_ref[token]
        pair = jnp.where(lane == 0, label >> 7, label & 127)
        digits = jnp.where(row == token, pair, digits)
    teacher = teacher_ref[...]
    student = student_ref[...]
    code = digits.astype(F32).astype(BF16)

    def write(shard):
        out_ref[shard, :, :teacher_width] = teacher
        out_ref[shard, :, teacher_width : teacher_width + student_width] = student
        out_ref[shard, :, teacher_width + student_width :] = code

    over_shards(shards, write)


def on_device(teacher_hidden, student_hidden, teacher_head, student_head, labels, *, shards):
    own, teacher_width = teacher_hidden.shape
    student_width = student_hidden.shape[1]
    columns_here = student_head.shape[1]
    first_column = lax.axis_index("vocab") * columns_here
    here = lax.axis_index("vocab").astype(jnp.int32)[None]
    payload = pl.pallas_call(
        payload_kernel,
        out_shape=jax.ShapeDtypeStruct((shards, own, teacher_width + student_width + CODE), BF16),
        in_specs=[SMEM, VMEM, VMEM],
        out_specs=VMEM,
    )(labels, teacher_hidden, student_hidden)
    rows = swap(payload).reshape(shards * own, -1)
    teacher_rows = rows[:, :teacher_width]
    student_rows = rows[:, teacher_width : teacher_width + student_width]
    code = rows[:, teacher_width + student_width :].astype(jnp.int32)
    label_rows = code[:, 0] * 128 + code[:, 1]
    other = [(0, 1), (1, 0)]
    student_other = lax.ppermute(student_rows, "rows", other)

    teacher_logits = jnp.dot(teacher_rows, teacher_head, preferred_element_type=F32)
    student_logits = jnp.dot(student_rows, student_head, preferred_element_type=F32)
    columns = lax.broadcasted_iota(jnp.int32, student_logits.shape, 1)
    target = (label_rows - first_column)[:, None] == columns
    top_t = jnp.max(teacher_logits, axis=1, keepdims=True)
    exp_t = jnp.exp(teacher_logits - top_t)
    top_s = jnp.max(student_logits, axis=1, keepdims=True)
    exp_s = jnp.exp(student_logits - top_s)
    stats = jnp.concatenate(
        [
            top_t,
            jnp.sum(exp_t, axis=1, keepdims=True),
            jnp.sum(exp_t * (teacher_logits - student_logits), axis=1, keepdims=True),
            top_s,
            jnp.sum(exp_s, axis=1, keepdims=True),
            jnp.sum(jnp.where(target, student_logits, 0.0), axis=1, keepdims=True),
        ],
        axis=1,
    )
    every = swap(jnp.broadcast_to(stats[None], (shards,) + stats.shape))
    all_top_t = jnp.max(every[:, :, 0], axis=0)
    factor_t = jnp.exp(every[:, :, 0] - all_top_t[None])
    all_top_s = jnp.max(every[:, :, 3], axis=0)
    factor_s = jnp.exp(every[:, :, 3] - all_top_s[None])
    mass_t = jnp.sum(every[:, :, 1] * factor_t, axis=0)
    cross = jnp.sum(every[:, :, 2] * factor_t, axis=0)
    mass_s = jnp.sum(every[:, :, 4] * factor_s, axis=0)
    picked = jnp.sum(every[:, :, 5], axis=0)
    loss = cross / mass_t - all_top_t - jnp.log(mass_t) + 2.0 * (all_top_s + jnp.log(mass_s)) - picked
    token_loss = lax.dynamic_slice_in_dim(loss, lax.axis_index("vocab") * own, own, 0)

    teacher_prob = jnp.exp(teacher_logits - all_top_t[:, None]) / mass_t[:, None]
    student_prob = jnp.exp(student_logits - all_top_s[:, None]) / mass_s[:, None]
    grad_rows = (2.0 * student_prob - teacher_prob - target.astype(F32)).astype(BF16)
    grad_other = lax.ppermute(grad_rows, "rows", other)
    partial = lax.dot_general(grad_rows, student_head, (((1,), (1,)), ((), ())), preferred_element_type=F32)
    arrived = swap(partial.astype(BF16).reshape(shards, own, student_width))
    hidden_grad = jnp.sum(arrived.astype(F32), axis=0)
    head_grad = lax.dot_general(
        jnp.concatenate([student_rows, student_other], axis=0),
        jnp.concatenate([grad_rows, grad_other], axis=0),
        (((0,), (0,)), ((), ())),
        preferred_element_type=F32,
    )
    return (token_loss, hidden_grad, head_grad)


def solution(mesh):
    tokens = ("groups", "vocab", "rows")
    in_specs = (P(tokens, None), P(tokens, None), P(None, "vocab"), P(None, "vocab"), P(tokens))
    out_specs = (P(tokens), P(tokens, None), P("groups", "vocab"))

    def body(*arrays):
        return on_device(*arrays, shards=mesh.shape["vocab"])

    return jax.shard_map(body, mesh=mesh, in_specs=in_specs, out_specs=out_specs, check_vma=False)
```

```python
import jax
import jax.numpy as jnp
from jax import lax
from jax.experimental import pallas as pl
from jax.experimental.pallas import tpu as pltpu
from jax.sharding import PartitionSpec as P

F32 = jnp.float32
BF16 = jnp.bfloat16
CODE = 128


UNROLL = 16
SMEM = pl.BlockSpec(memory_space=pltpu.SMEM)
VMEM = pl.BlockSpec(memory_space=pltpu.VMEM)


def over_shards(shards, body):
    if shards <= UNROLL:
        for shard in range(shards):
            body(shard)
    else:
        pl.loop(0, shards)(body)


def swap(blocks):
    return lax.all_to_all(blocks, "vocab", split_axis=0, concat_axis=0, tiled=True)


def payload_kernel(labels_ref, teacher_ref, student_ref, out_ref):
    shards, own, _ = out_ref.shape
    teacher_width, student_width = teacher_ref.shape[1], student_ref.shape[1]
    row = lax.broadcasted_iota(jnp.int32, (own, CODE), 0)
    lane = lax.broadcasted_iota(jnp.int32, (own, CODE), 1)
    digits = jnp.zeros((own, CODE), jnp.int32)
    for token in range(own):
        label = labels_ref[token]
        pair = jnp.where(lane == 0, label >> 7, label & 127)
        digits = jnp.where(row == token, pair, digits)
    teacher = teacher_ref[...]
    student = student_ref[...]
    code = digits.astype(F32).astype(BF16)

    def write(shard):
        out_ref[shard, :, :teacher_width] = teacher
        out_ref[shard, :, teacher_width : teacher_width + student_width] = student
        out_ref[shard, :, teacher_width + student_width :] = code

    over_shards(shards, write)


def gather_tokens(teacher_hidden, student_hidden, labels, shards):
    own, teacher_width = teacher_hidden.shape
    student_width = student_hidden.shape[1]
    payload = pl.pallas_call(
        payload_kernel,
        out_shape=jax.ShapeDtypeStruct((shards, own, teacher_width + student_width + CODE), BF16),
        in_specs=[SMEM, VMEM, VMEM],
        out_specs=VMEM,
    )(labels, teacher_hidden, student_hidden)
    rows = swap(payload).reshape(shards * own, -1)
    return (
        rows[:, :teacher_width],
        rows[:, teacher_width : teacher_width + student_width],
        rows[:, teacher_width + student_width :],
    )


def round_bf16(array):
    return lax.reduce_precision(array, exponent_bits=8, mantissa_bits=7)


def three_parts(array):
    high = round_bf16(array)
    middle = round_bf16(array - high)
    return [part.astype(BF16) for part in (high, middle, array - high - middle)]


def raw_partial_kernel(first_ref, teacher_ref, student_ref, code_ref, stats_ref, head_ref, out_ref):
    shards, _, _ = out_ref.shape
    tokens, columns = student_ref.shape
    width = head_ref.shape[0]
    rows = 4 * tokens

    def iota(shape, dim):
        return lax.broadcasted_iota(jnp.int32, shape, dim)

    def dot(left, right, dims):
        return lax.dot_general(left, right, (dims, ((), ())), preferred_element_type=F32)

    teacher = teacher_ref[...]
    student = student_ref[...]
    exp_t = jnp.exp(teacher - jnp.max(teacher, axis=1, keepdims=True))
    exp_s = jnp.exp(student - jnp.max(student, axis=1, keepdims=True))
    code = code_ref[...].astype(F32)
    lane = iota(code.shape, 1)
    label = jnp.sum(jnp.where(lane == 0, code * 128.0, jnp.where(lane == 1, code, 0.0)), axis=1, keepdims=True)
    target = (label.astype(jnp.int32) - first_ref[0] == iota((tokens, columns), 1)).astype(F32)
    high_t = exp_t.astype(BF16).astype(F32)
    high_s = exp_s.astype(BF16).astype(F32)
    members = 3 * tokens
    spread_shape = (rows, members)
    row, column = iota(spread_shape, 0), iota(spread_shape, 1)
    pick = jnp.zeros(spread_shape, F32)
    for j in range(3):
        pick += ((row % 4 == j) & (column == row // 4 + j * tokens)).astype(F32)
    pick = pick.astype(BF16)
    high = jnp.concatenate([high_s, high_t, target], axis=0).astype(BF16)
    low = jnp.concatenate([exp_s - high_s, exp_t - high_t, jnp.zeros_like(target)], axis=0).astype(BF16)
    left_high = dot(pick, high, ((1,), (0,))).astype(BF16)
    left_low = dot(pick, low, ((1,), (0,))).astype(BF16)
    mix_shape = (tokens, rows)
    token, place = iota(mix_shape, 0), iota(mix_shape, 1)
    scale_s = 2.0 / jnp.sum(exp_s, axis=1, keepdims=True)
    scale_t = 1.0 / jnp.sum(exp_t, axis=1, keepdims=True)
    mix = jnp.where(place == 4 * token, scale_s, jnp.where(place == 4 * token + 1, -scale_t, 0.0))
    put = (iota((rows, tokens), 0) == 4 * iota((rows, tokens), 1) + 3).astype(F32).astype(BF16)
    mix = dot(put, mix.astype(BF16), ((1,), (0,))).astype(BF16)
    step = 512
    for start in range(0, width, step):
        head = head_ref[pl.ds(start, step), :]
        exact = dot(left_high, head, ((1,), (1,))) + dot(left_low, head, ((1,), (1,)))
        sent = exact.astype(BF16).astype(F32)
        residue = (exact - sent).astype(BF16)
        sent += dot(mix, residue, ((1,), (0,)))
        for shard in range(shards):
            out_ref[shard, :, pl.ds(start, step)] = sent[8 * shard : 8 * shard + 8].astype(BF16)
    stats = stats_ref[...]
    for shard in range(shards):
        out_ref[shard, :, width:] = stats


def two_exchanges(teacher_hidden, student_hidden, teacher_head, student_head, labels, *, shards):
    own = labels.shape[0]
    width = student_hidden.shape[1]
    columns_here = student_head.shape[1]
    tokens = shards * own
    here = lax.axis_index("vocab").astype(jnp.int32)
    first_column = here * columns_here
    teacher_rows, student_rows, code = gather_tokens(teacher_hidden, student_hidden, labels, shards)
    other = [(0, 1), (1, 0)]
    student_other = lax.ppermute(student_rows, "rows", other)

    teacher_logits = jnp.dot(teacher_rows, teacher_head, preferred_element_type=F32)
    student_logits = jnp.dot(student_rows, student_head, preferred_element_type=F32)
    label_rows = code[:, 0].astype(jnp.int32) * 128 + code[:, 1].astype(jnp.int32)
    columns = lax.broadcasted_iota(jnp.int32, student_logits.shape, 1)
    target = (label_rows - first_column)[:, None] == columns
    top_t = jnp.max(teacher_logits, axis=1)
    exp_t = jnp.exp(teacher_logits - top_t[:, None])
    top_s = jnp.max(student_logits, axis=1)
    exp_s = jnp.exp(student_logits - top_s[:, None])
    stats = jnp.stack(
        [
            top_t,
            jnp.sum(exp_t, axis=1),
            jnp.sum(exp_t * (teacher_logits - student_logits), axis=1),
            top_s,
            jnp.sum(exp_s, axis=1),
            jnp.sum(jnp.where(target, student_logits, 0.0), axis=1),
            jnp.sum(jnp.where(target, teacher_logits, 0.0), axis=1),
            jnp.zeros_like(top_t),
        ]
    )
    stats = jnp.pad(stats, ((0, 0), (0, 128 - tokens)))
    payload = pl.pallas_call(
        raw_partial_kernel,
        out_shape=jax.ShapeDtypeStruct((shards, 8, width + 3 * 128), BF16),
        in_specs=[SMEM, VMEM, VMEM, VMEM, VMEM, VMEM],
        out_specs=VMEM,
    )(first_column[None], teacher_logits, student_logits, code, jnp.concatenate(three_parts(stats), axis=1), student_head)
    arrived = swap(payload)

    tail = arrived[:, :, width:].astype(F32)
    every = tail[:, :, :128] + tail[:, :, 128:256] + tail[:, :, 256:]

    def fold(part):
        top_t = jnp.max(part[:, 0], axis=0)
        factor_t = jnp.exp(part[:, 0] - top_t)
        top_s = jnp.max(part[:, 3], axis=0)
        factor_s = jnp.exp(part[:, 3] - top_s)
        mass_t = jnp.sum(part[:, 1] * factor_t, axis=0)
        mass_s = jnp.sum(part[:, 4] * factor_s, axis=0)
        return top_t, factor_t, mass_t, top_s, factor_s, mass_s

    top_t, _, mass_t, top_s, _, mass_s = fold(every[:, :, :tokens])
    teacher_prob = jnp.exp(teacher_logits - top_t[:, None]) / mass_t[:, None]
    student_prob = jnp.exp(student_logits - top_s[:, None]) / mass_s[:, None]
    grad_rows = (2.0 * student_prob - teacher_prob - target.astype(F32)).astype(BF16)
    grad_other = lax.ppermute(grad_rows, "rows", other)

    mine = lax.dynamic_slice_in_dim(every, here * own, own, 2)
    top_t, factor_t, mass_t, top_s, factor_s, mass_s = fold(mine)
    cross = jnp.sum(mine[:, 2] * factor_t, axis=0)
    picked = jnp.sum(mine[:, 5], axis=0)
    picked_t = jnp.sum(mine[:, 6], axis=0)
    token_loss = cross / mass_t - top_t - jnp.log(mass_t) + 2.0 * (top_s + jnp.log(mass_s)) - picked
    label_grad = 2.0 * jnp.exp(picked - top_s) / mass_s - jnp.exp(picked_t - top_t) / mass_t - 1.0
    label_weight = round_bf16(label_grad) - label_grad - 1.0
    weight_s = factor_s / mass_s
    weight_t = factor_t / mass_t
    share = 0.8 * weight_s * mine[:, 4] + 0.2 * weight_t * mine[:, 1]
    weights = jnp.stack(
        [2.0 * weight_s, -weight_t, jnp.broadcast_to(label_weight, weight_s.shape), share], axis=2
    ).reshape(shards, 4 * own, 1)
    by_row = jnp.sum(weights * arrived[:, :, :width].astype(F32), axis=0)
    hidden_grad = jnp.sum(by_row.reshape(own, 4, width), axis=1)
    head_grad = lax.dot_general(
        jnp.concatenate([student_rows, student_other], axis=0),
        jnp.concatenate([grad_rows, grad_other], axis=0),
        (((0,), (0,)), ((), ())),
        preferred_element_type=F32,
    )
    return (token_loss, hidden_grad, head_grad)


def three_exchanges(teacher_hidden, student_hidden, teacher_head, student_head, labels, *, shards):
    own = labels.shape[0]
    student_width = student_hidden.shape[1]
    columns_here = student_head.shape[1]
    first_column = lax.axis_index("vocab") * columns_here
    teacher_rows, student_rows, code = gather_tokens(teacher_hidden, student_hidden, labels, shards)
    code = code.astype(jnp.int32)
    label_rows = code[:, 0] * 128 + code[:, 1]
    other = [(0, 1), (1, 0)]
    student_other = lax.ppermute(student_rows, "rows", other)

    teacher_logits = jnp.dot(teacher_rows, teacher_head, preferred_element_type=F32)
    student_logits = jnp.dot(student_rows, student_head, preferred_element_type=F32)
    columns = lax.broadcasted_iota(jnp.int32, student_logits.shape, 1)
    target = (label_rows - first_column)[:, None] == columns
    top_t = jnp.max(teacher_logits, axis=1, keepdims=True)
    exp_t = jnp.exp(teacher_logits - top_t)
    top_s = jnp.max(student_logits, axis=1, keepdims=True)
    exp_s = jnp.exp(student_logits - top_s)
    stats = jnp.concatenate(
        [
            top_t,
            jnp.sum(exp_t, axis=1, keepdims=True),
            jnp.sum(exp_t * (teacher_logits - student_logits), axis=1, keepdims=True),
            top_s,
            jnp.sum(exp_s, axis=1, keepdims=True),
            jnp.sum(jnp.where(target, student_logits, 0.0), axis=1, keepdims=True),
        ],
        axis=1,
    )
    every = swap(jnp.broadcast_to(stats[None], (shards,) + stats.shape))
    all_top_t = jnp.max(every[:, :, 0], axis=0)
    factor_t = jnp.exp(every[:, :, 0] - all_top_t[None])
    all_top_s = jnp.max(every[:, :, 3], axis=0)
    factor_s = jnp.exp(every[:, :, 3] - all_top_s[None])
    mass_t = jnp.sum(every[:, :, 1] * factor_t, axis=0)
    cross = jnp.sum(every[:, :, 2] * factor_t, axis=0)
    mass_s = jnp.sum(every[:, :, 4] * factor_s, axis=0)
    picked = jnp.sum(every[:, :, 5], axis=0)
    loss = cross / mass_t - all_top_t - jnp.log(mass_t) + 2.0 * (all_top_s + jnp.log(mass_s)) - picked
    token_loss = lax.dynamic_slice_in_dim(loss, lax.axis_index("vocab") * own, own, 0)

    teacher_prob = jnp.exp(teacher_logits - all_top_t[:, None]) / mass_t[:, None]
    student_prob = jnp.exp(student_logits - all_top_s[:, None]) / mass_s[:, None]
    grad_rows = (2.0 * student_prob - teacher_prob - target.astype(F32)).astype(BF16)
    grad_other = lax.ppermute(grad_rows, "rows", other)
    partial = lax.dot_general(grad_rows, student_head, (((1,), (1,)), ((), ())), preferred_element_type=F32)
    arrived = swap(partial.astype(BF16).reshape(shards, own, student_width))
    hidden_grad = jnp.sum(arrived.astype(F32), axis=0)
    head_grad = lax.dot_general(
        jnp.concatenate([student_rows, student_other], axis=0),
        jnp.concatenate([grad_rows, grad_other], axis=0),
        (((0,), (0,)), ((), ())),
        preferred_element_type=F32,
    )
    return (token_loss, hidden_grad, head_grad)


def solution(mesh):
    tokens = ("groups", "vocab", "rows")
    in_specs = (P(tokens, None), P(tokens, None), P(None, "vocab"), P(None, "vocab"), P(tokens))
    out_specs = (P(tokens), P(tokens, None), P("groups", "vocab"))

    def body(*arrays):
        shards = mesh.shape["vocab"]
        tokens_here = shards * arrays[4].shape[0]
        small = shards <= UNROLL and tokens_here <= 128 and arrays[4].shape[0] == 2
        return (two_exchanges if small else three_exchanges)(*arrays, shards=shards)

    return jax.shard_map(body, mesh=mesh, in_specs=in_specs, out_specs=out_specs, check_vma=False)
```

```python
import jax
import jax.numpy as jnp
from jax import lax
from jax.experimental import pallas as pl
from jax.experimental.pallas import tpu as pltpu
from jax.sharding import PartitionSpec as P

F32 = jnp.float32
BF16 = jnp.bfloat16
CODE = 128


UNROLL = 16
SMEM = pl.BlockSpec(memory_space=pltpu.SMEM)
VMEM = pl.BlockSpec(memory_space=pltpu.VMEM)


def over_shards(shards, body):
    if shards <= UNROLL:
        for shard in range(shards):
            body(shard)
    else:
        pl.loop(0, shards)(body)


def swap(blocks):
    return lax.all_to_all(blocks, "vocab", split_axis=0, concat_axis=0, tiled=True)


def payload_kernel(labels_ref, teacher_ref, student_ref, out_ref):
    shards, own, _ = out_ref.shape
    teacher_width, student_width = teacher_ref.shape[1], student_ref.shape[1]
    row = lax.broadcasted_iota(jnp.int32, (own, CODE), 0)
    lane = lax.broadcasted_iota(jnp.int32, (own, CODE), 1)
    digits = jnp.zeros((own, CODE), jnp.int32)
    for token in range(own):
        label = labels_ref[token]
        pair = jnp.where(lane == 0, label >> 7, label & 127)
        digits = jnp.where(row == token, pair, digits)
    teacher = teacher_ref[...]
    student = student_ref[...]
    code = digits.astype(F32).astype(BF16)

    def write(shard):
        out_ref[shard, :, :teacher_width] = teacher
        out_ref[shard, :, teacher_width : teacher_width + student_width] = student
        out_ref[shard, :, teacher_width + student_width :] = code

    over_shards(shards, write)


def gather_tokens(teacher_hidden, student_hidden, labels, shards):
    own, teacher_width = teacher_hidden.shape
    student_width = student_hidden.shape[1]
    payload = pl.pallas_call(
        payload_kernel,
        out_shape=jax.ShapeDtypeStruct((shards, own, teacher_width + student_width + CODE), BF16),
        in_specs=[SMEM, VMEM, VMEM],
        out_specs=VMEM,
    )(labels, teacher_hidden, student_hidden)
    return swap(payload)


def round_bf16(array):
    return lax.reduce_precision(array, exponent_bits=8, mantissa_bits=7)


def raw_partial_kernel(first_ref, rows_ref, teacher_head_ref, head_ref, out_ref, teacher_ref, student_ref, target_ref):
    shards, own, _ = rows_ref.shape
    tokens = shards * own
    wide = 8 * shards
    columns = head_ref.shape[1]
    teacher_width, width = teacher_head_ref.shape[0], head_ref.shape[0]
    quarter = width // 4

    def iota(shape, dim):
        return lax.broadcasted_iota(jnp.int32, shape, dim)

    def dot(left, right, dims):
        return lax.dot_general(left, right, (dims, ((), ())), preferred_element_type=F32)

    def rows_of(start, size):
        return jnp.concatenate([rows_ref[shard, :, start : start + size] for shard in range(shards)], axis=0)

    student = dot(rows_of(teacher_width, width), head_ref[...], ((1,), (0,)))
    teacher = dot(rows_of(0, teacher_width), teacher_head_ref[...], ((1,), (0,)))
    code = rows_of(teacher_width + width, CODE).astype(F32)
    lane = iota(code.shape, 1)
    label = jnp.sum(jnp.where(lane == 0, code * 128.0, jnp.where(lane == 1, code, 0.0)), axis=1, keepdims=True)
    target = (label.astype(jnp.int32) - first_ref[0] == iota((tokens, columns), 1)).astype(F32)
    teacher_ref[...] = teacher
    student_ref[...] = student
    target_ref[...] = target

    def total(array):
        return jnp.sum(array, axis=1, keepdims=True)

    top_t = jnp.max(teacher, axis=1, keepdims=True)
    top_s = jnp.max(student, axis=1, keepdims=True)
    exp_t = jnp.exp(teacher - top_t)
    exp_s = jnp.exp(student - top_s)
    mass_t, mass_s = total(exp_t), total(exp_s)
    combined = exp_s * (2.0 / mass_s) - exp_t / mass_t
    kappa = (total(target * combined) > 0.5).astype(F32)
    stats = [
        top_t,
        mass_t,
        total(exp_t * (teacher - student)),
        top_s,
        mass_s,
        total(target * student),
        total(target * teacher),
        2.0 * kappa + total(target),
    ]
    lane = iota((tokens, 128), 1)
    table = jnp.zeros((tokens, 128), F32)
    for k, stat in enumerate(stats):
        table = jnp.where(lane % 8 == k, stat, table)
    first = table.astype(BF16).astype(F32)
    second = (table - first).astype(BF16).astype(F32)
    part = (lane % 32) // 8
    parts = jnp.where(
        part == 0, first, jnp.where(part == 1, second, jnp.where(part == 2, table - first - second, 0.0))
    ).astype(BF16)

    row, column = iota((wide, tokens), 0), iota((wide, tokens), 1)
    of_token = (column == (row // 8) * 2 + row % 2).astype(F32).astype(BF16)
    by_row = dot(of_token, parts, ((1,), (0,)))

    def stat_by_row(k):
        picked = by_row[:, k : k + 1] + by_row[:, 8 + k : 9 + k] + by_row[:, 16 + k : 17 + k]
        return picked

    members = jnp.concatenate([exp_s, exp_t, kappa * combined * total(target) - target], axis=0)
    member_high = members.astype(BF16)
    member_low = (members - member_high.astype(F32)).astype(BF16)
    row, column = iota((wide, 3 * tokens), 0), iota((wide, 3 * tokens), 1)
    place = row % 8
    token = (row // 8) * 2 + row % 2
    picks = [((place < 6) & (column == (place // 2) * tokens + token)).astype(F32)]
    for j in range(3):
        picks.append(((place >= 6) & (column == j * tokens + token)).astype(F32))
    pick = jnp.concatenate(picks, axis=0).astype(BF16)
    left_high = dot(pick, member_high, ((1,), (0,))).astype(BF16)
    left_low = dot(pick, member_low, ((1,), (0,))).astype(BF16)
    left = jnp.concatenate([left_high[:wide], left_low[:wide]], axis=0)
    left_last = jnp.concatenate([left_high[wide:], left_low[wide:]], axis=0)

    place = iota((wide, 1), 0) % 8
    has_label = stat_by_row(7) > 0.5
    scale_s = jnp.where(has_label, 0.0, 2.0 / stat_by_row(4))
    scale_t = jnp.where(has_label, 0.0, -1.0 / stat_by_row(1))
    scale = jnp.where(place < 2, scale_s, jnp.where(place < 4, scale_t, 0.0))
    in_third = ((place == 4) | (place == 5)).astype(F32)
    scale_s = jnp.where(place >= 6, scale_s, 0.0)
    scale_t = jnp.where(place >= 6, scale_t, 0.0)
    last = dot(left_last, head_ref[3 * quarter :, :], ((1,), (1,)))
    correction = jnp.zeros((wide, quarter), F32)
    for j in range(3):
        both = dot(left, head_ref[j * quarter : (j + 1) * quarter, :], ((1,), (1,)))
        exact = both[:wide] + both[wide:] + last[j * wide : (j + 1) * wide] + last[(3 + j) * wide : (4 + j) * wide]
        sent = exact.astype(BF16).astype(F32)
        residue = exact - sent
        if j < 2:
            correction += residue * (scale_s, scale_t)[j]
        else:
            sent += correction
        scaled = residue * scale
        sent += in_third * (pltpu.roll(scaled, 4, 0) + pltpu.roll(scaled, 2, 0))
        for shard in range(shards):
            out_ref[shard, :, j * quarter : (j + 1) * quarter] = sent[8 * shard : 8 * shard + 8].astype(BF16)
    lane = iota((8, 128), 1)
    shared = jnp.zeros((8, 128), F32)
    wide_parts = parts.astype(F32)
    for group in range(tokens // 8):
        shared = jnp.where(lane // 32 == group + 1, wide_parts[8 * group : 8 * group + 8], shared)
    for shard in range(shards):
        block = jnp.where(lane < 32, by_row[8 * shard : 8 * shard + 8], shared)
        out_ref[shard, :, 3 * quarter :] = block.astype(BF16)


def two_exchanges(teacher_hidden, student_hidden, teacher_head, student_head, labels, *, shards):
    own = labels.shape[0]
    teacher_width, width = teacher_hidden.shape[1], student_hidden.shape[1]
    columns_here = student_head.shape[1]
    tokens = shards * own
    quarter = width // 4
    here = lax.axis_index("vocab").astype(jnp.int32)
    rows = gather_tokens(teacher_hidden, student_hidden, labels, shards)
    student_rows = rows[:, :, teacher_width : teacher_width + width].reshape(tokens, width)
    other = [(0, 1), (1, 0)]
    student_other = lax.ppermute(student_rows, "rows", other)

    square = jax.ShapeDtypeStruct((tokens, columns_here), F32)
    payload, teacher_logits, student_logits, target = pl.pallas_call(
        raw_partial_kernel,
        out_shape=(jax.ShapeDtypeStruct((shards, 8, 3 * quarter + 128), BF16), square, square, square),
        in_specs=[SMEM, VMEM, VMEM, VMEM],
        out_specs=(VMEM, VMEM, VMEM, VMEM),
        compiler_params=pltpu.CompilerParams(vmem_limit_bytes=24 * 1024 * 1024),
    )((here * columns_here)[None], rows, teacher_head, student_head)
    arrived = swap(payload)
    tail = arrived[:, :, 3 * quarter :].astype(F32)

    def statistics(lane):
        return tail[:, :, lane : lane + 8] + tail[:, :, lane + 8 : lane + 16] + tail[:, :, lane + 16 : lane + 24]

    def fold(stats):
        top_t = jnp.max(stats[:, :, 0:1], axis=0)
        factor_t = jnp.exp(stats[:, :, 0:1] - top_t)
        top_s = jnp.max(stats[:, :, 3:4], axis=0)
        factor_s = jnp.exp(stats[:, :, 3:4] - top_s)
        mass_t = jnp.sum(stats[:, :, 1:2] * factor_t, axis=0)
        mass_s = jnp.sum(stats[:, :, 4:5] * factor_s, axis=0)
        return top_t, factor_t, mass_t, top_s, factor_s, mass_s

    folded = [fold(statistics(32 * group + 32)) for group in range(tokens // 8)]
    top_t, _, mass_t, top_s, _, mass_s = [jnp.concatenate([f[i] for f in folded], axis=-2) for i in range(6)]
    grad_rows = (
        2.0 * (jnp.exp(student_logits - top_s) / mass_s) - jnp.exp(teacher_logits - top_t) / mass_t - target
    ).astype(BF16)
    grad_other = lax.ppermute(grad_rows, "rows", other)

    mine = statistics(0)
    top_t, factor_t, mass_t, top_s, factor_s, mass_s = fold(mine)
    cross = jnp.sum(mine[:, :, 2:3] * factor_t, axis=0)
    picked = jnp.sum(mine[:, :, 5:6], axis=0)
    picked_t = jnp.sum(mine[:, :, 6:7], axis=0)
    loss = cross / mass_t - top_t - jnp.log(mass_t) + 2.0 * (top_s + jnp.log(mass_s)) - picked
    token_loss = loss[:own, 0]
    label_grad = 2.0 * (jnp.exp(picked - top_s) / mass_s) - jnp.exp(picked_t - top_t) / mass_t - 1.0
    rounding = round_bf16(label_grad) - label_grad
    weight_s = factor_s / mass_s
    weight_t = factor_t / mass_t
    share_s = weight_s * mine[:, :, 4:5]
    share_t = weight_t * mine[:, :, 1:2]
    kappa = (mine[:, :, 7:8] > 2.0).astype(F32)
    weight_l = jnp.where(mine[:, :, 7:8] > 0.5, 1.0 - (1.0 - kappa) * rounding, 0.8 * share_s + 0.2 * share_t)
    weight_s = 2.0 * (weight_s - kappa / mine[:, :, 4:5])
    weight_t = kappa / mine[:, :, 1:2] - weight_t
    place = lax.broadcasted_iota(jnp.int32, (1, 8, 1), 1)
    pieces = []
    for j, weight_last in enumerate((weight_s, weight_t, weight_l)):
        weight = jnp.where(
            place < 2, weight_s, jnp.where(place < 4, weight_t, jnp.where(place < 6, weight_l, weight_last))
        )
        pieces.append(jnp.sum(weight * arrived[:, :, j * quarter : (j + 1) * quarter].astype(F32), axis=0))
    hidden_grad = jnp.concatenate(
        [piece[0:2] + piece[2:4] + piece[4:6] for piece in pieces] + [sum(piece[6:8] for piece in pieces)], axis=1
    )
    head_grad = lax.dot_general(
        jnp.concatenate([student_rows, student_other], axis=0),
        jnp.concatenate([grad_rows, grad_other], axis=0),
        (((0,), (0,)), ((), ())),
        preferred_element_type=F32,
    )
    return (token_loss, hidden_grad, head_grad)


def three_exchanges(teacher_hidden, student_hidden, teacher_head, student_head, labels, *, shards):
    own = labels.shape[0]
    student_width = student_hidden.shape[1]
    columns_here = student_head.shape[1]
    first_column = lax.axis_index("vocab") * columns_here
    rows = gather_tokens(teacher_hidden, student_hidden, labels, shards).reshape(shards * own, -1)
    teacher_width = teacher_hidden.shape[1]
    teacher_rows = rows[:, :teacher_width]
    student_rows = rows[:, teacher_width : teacher_width + student_width]
    code = rows[:, teacher_width + student_width :].astype(jnp.int32)
    label_rows = code[:, 0] * 128 + code[:, 1]
    other = [(0, 1), (1, 0)]
    student_other = lax.ppermute(student_rows, "rows", other)

    teacher_logits = jnp.dot(teacher_rows, teacher_head, preferred_element_type=F32)
    student_logits = jnp.dot(student_rows, student_head, preferred_element_type=F32)
    columns = lax.broadcasted_iota(jnp.int32, student_logits.shape, 1)
    target = (label_rows - first_column)[:, None] == columns
    top_t = jnp.max(teacher_logits, axis=1, keepdims=True)
    exp_t = jnp.exp(teacher_logits - top_t)
    top_s = jnp.max(student_logits, axis=1, keepdims=True)
    exp_s = jnp.exp(student_logits - top_s)
    stats = jnp.concatenate(
        [
            top_t,
            jnp.sum(exp_t, axis=1, keepdims=True),
            jnp.sum(exp_t * (teacher_logits - student_logits), axis=1, keepdims=True),
            top_s,
            jnp.sum(exp_s, axis=1, keepdims=True),
            jnp.sum(jnp.where(target, student_logits, 0.0), axis=1, keepdims=True),
        ],
        axis=1,
    )
    every = swap(jnp.broadcast_to(stats[None], (shards,) + stats.shape))
    all_top_t = jnp.max(every[:, :, 0], axis=0)
    factor_t = jnp.exp(every[:, :, 0] - all_top_t[None])
    all_top_s = jnp.max(every[:, :, 3], axis=0)
    factor_s = jnp.exp(every[:, :, 3] - all_top_s[None])
    mass_t = jnp.sum(every[:, :, 1] * factor_t, axis=0)
    cross = jnp.sum(every[:, :, 2] * factor_t, axis=0)
    mass_s = jnp.sum(every[:, :, 4] * factor_s, axis=0)
    picked = jnp.sum(every[:, :, 5], axis=0)
    loss = cross / mass_t - all_top_t - jnp.log(mass_t) + 2.0 * (all_top_s + jnp.log(mass_s)) - picked
    token_loss = lax.dynamic_slice_in_dim(loss, lax.axis_index("vocab") * own, own, 0)

    teacher_prob = jnp.exp(teacher_logits - all_top_t[:, None]) / mass_t[:, None]
    student_prob = jnp.exp(student_logits - all_top_s[:, None]) / mass_s[:, None]
    grad_rows = (2.0 * student_prob - teacher_prob - target.astype(F32)).astype(BF16)
    grad_other = lax.ppermute(grad_rows, "rows", other)
    partial = lax.dot_general(grad_rows, student_head, (((1,), (1,)), ((), ())), preferred_element_type=F32)
    arrived = swap(partial.astype(BF16).reshape(shards, own, student_width))
    hidden_grad = jnp.sum(arrived.astype(F32), axis=0)
    head_grad = lax.dot_general(
        jnp.concatenate([student_rows, student_other], axis=0),
        jnp.concatenate([grad_rows, grad_other], axis=0),
        (((0,), (0,)), ((), ())),
        preferred_element_type=F32,
    )
    return (token_loss, hidden_grad, head_grad)


def solution(mesh):
    tokens = ("groups", "vocab", "rows")
    in_specs = (P(tokens, None), P(tokens, None), P(None, "vocab"), P(None, "vocab"), P(tokens))
    out_specs = (P(tokens), P(tokens, None), P("groups", "vocab"))

    def body(*arrays):
        shards = mesh.shape["vocab"]
        own = arrays[4].shape[0]
        small = own == 2 and shards % 4 == 0 and shards * own <= 24
        return (two_exchanges if small else three_exchanges)(*arrays, shards=shards)

    return jax.shard_map(body, mesh=mesh, in_specs=in_specs, out_specs=out_specs, check_vma=False)
```

```python
import jax
import jax.numpy as jnp
from jax import lax
from jax.experimental import pallas as pl
from jax.experimental.pallas import tpu as pltpu
from jax.sharding import PartitionSpec as P

F32 = jnp.float32
BF16 = jnp.bfloat16
CODE = 128


UNROLL = 16
SMEM = pl.BlockSpec(memory_space=pltpu.SMEM)
VMEM = pl.BlockSpec(memory_space=pltpu.VMEM)
SMALL = pltpu.CompilerParams(vmem_limit_bytes=16 * 1024 * 1024)


def over_shards(shards, body):
    if shards <= UNROLL:
        for shard in range(shards):
            body(shard)
    else:
        pl.loop(0, shards)(body)


def swap(blocks):
    return lax.all_to_all(blocks, "vocab", split_axis=0, concat_axis=0, tiled=True)


def payload_kernel(labels_ref, teacher_ref, student_ref, out_ref):
    shards, own, _ = out_ref.shape
    teacher_width, student_width = teacher_ref.shape[1], student_ref.shape[1]
    row = lax.broadcasted_iota(jnp.int32, (own, CODE), 0)
    lane = lax.broadcasted_iota(jnp.int32, (own, CODE), 1)
    digits = jnp.zeros((own, CODE), jnp.int32)
    for token in range(own):
        label = labels_ref[token]
        pair = jnp.where(lane == 0, label >> 7, label & 127)
        digits = jnp.where(row == token, pair, digits)
    teacher = teacher_ref[...]
    student = student_ref[...]
    code = digits.astype(F32).astype(BF16)

    def write(shard):
        out_ref[shard, :, :teacher_width] = teacher
        out_ref[shard, :, teacher_width : teacher_width + student_width] = student
        out_ref[shard, :, teacher_width + student_width :] = code

    over_shards(shards, write)


def gather_tokens(teacher_hidden, student_hidden, labels, shards):
    own, teacher_width = teacher_hidden.shape
    student_width = student_hidden.shape[1]
    payload = pl.pallas_call(
        payload_kernel,
        out_shape=jax.ShapeDtypeStruct((shards, own, teacher_width + student_width + CODE), BF16),
        in_specs=[SMEM, VMEM, VMEM],
        out_specs=VMEM,
        compiler_params=SMALL,
    )(labels, teacher_hidden, student_hidden)
    return swap(payload)


def raw_partial_kernel(first_ref, rows_ref, heads_ref, out_ref, teacher_ref, student_ref, target_ref):
    shards, own, _ = rows_ref.shape
    tokens = shards * own
    wide = 8 * shards
    columns = heads_ref.shape[1]
    quarter = (out_ref.shape[2] - 128) // 3
    width = 4 * quarter
    teacher_width = heads_ref.shape[0] - width

    def iota(shape, dim):
        return lax.broadcasted_iota(jnp.int32, shape, dim)

    def dot(left, right, dims):
        return lax.dot_general(left, right, (dims, ((), ())), preferred_element_type=F32)

    def rows_of(start, size):
        return jnp.concatenate([rows_ref[shard, :, start : start + size] for shard in range(shards)], axis=0)

    student = dot(rows_of(teacher_width, width), heads_ref[teacher_width:, :], ((1,), (0,)))
    teacher = dot(rows_of(0, teacher_width), heads_ref[:teacher_width, :], ((1,), (0,)))
    code = rows_of(teacher_width + width, CODE).astype(F32)
    lane = iota(code.shape, 1)
    label = jnp.sum(jnp.where(lane == 0, code * 128.0, jnp.where(lane == 1, code, 0.0)), axis=1, keepdims=True)
    target = (label.astype(jnp.int32) - first_ref[0] == iota((tokens, columns), 1)).astype(F32)
    teacher_ref[...] = teacher
    student_ref[...] = student
    target_ref[...] = target

    def total(array):
        return jnp.sum(array, axis=1, keepdims=True)

    top_t = jnp.max(teacher, axis=1, keepdims=True)
    top_s = jnp.max(student, axis=1, keepdims=True)
    exp_t = jnp.exp(teacher - top_t)
    exp_s = jnp.exp(student - top_s)
    mass_t, mass_s = total(exp_t), total(exp_s)
    combined = exp_s * (2.0 / mass_s) - exp_t / mass_t
    kappa = (total(target * combined) > 0.5).astype(F32)
    stats = [
        top_t,
        mass_t,
        total(exp_t * (teacher - student)),
        top_s,
        mass_s,
        total(target * student),
        total(target * teacher),
        2.0 * kappa + total(target),
    ]
    lane = iota((tokens, 128), 1)
    table = jnp.zeros((tokens, 128), F32)
    for k, stat in enumerate(stats):
        table = jnp.where(lane % 8 == k, stat, table)
    first = table.astype(BF16).astype(F32)
    second = (table - first).astype(BF16).astype(F32)
    part = (lane % 32) // 8
    parts = jnp.where(
        part == 0, first, jnp.where(part == 1, second, jnp.where(part == 2, table - first - second, 0.0))
    ).astype(BF16)

    row, column = iota((wide, tokens), 0), iota((wide, tokens), 1)
    of_token = (column == (row // 8) * 2 + row % 2).astype(F32).astype(BF16)
    by_row = dot(of_token, parts, ((1,), (0,)))

    def stat_by_row(k):
        picked = by_row[:, k : k + 1] + by_row[:, 8 + k : 9 + k] + by_row[:, 16 + k : 17 + k]
        return picked

    members = jnp.concatenate([exp_s, exp_t, kappa * combined * total(target) - target], axis=0)
    member_high = members.astype(BF16)
    member_low = (members - member_high.astype(F32)).astype(BF16)
    row, column = iota((wide, 3 * tokens), 0), iota((wide, 3 * tokens), 1)
    place = row % 8
    token = (row // 8) * 2 + row % 2
    picks = [((place < 6) & (column == (place // 2) * tokens + token)).astype(F32)]
    for j in range(3):
        picks.append(((place >= 6) & (column == j * tokens + token)).astype(F32))
    pick = jnp.concatenate(picks, axis=0).astype(BF16)
    left_high = dot(pick, member_high, ((1,), (0,))).astype(BF16)
    left_low = dot(pick, member_low, ((1,), (0,))).astype(BF16)
    left = jnp.concatenate([left_high[:wide], left_low[:wide]], axis=0)
    left_last = jnp.concatenate([left_high[wide:], left_low[wide:]], axis=0)

    place = iota((wide, 1), 0) % 8
    has_label = stat_by_row(7) > 0.5
    scale_s = jnp.where(has_label, 0.0, 2.0 / stat_by_row(4))
    scale_t = jnp.where(has_label, 0.0, -1.0 / stat_by_row(1))
    scale = jnp.where(place < 2, scale_s, jnp.where(place < 4, scale_t, 0.0))
    in_third = ((place == 4) | (place == 5)).astype(F32)
    scale_s = jnp.where(place >= 6, scale_s, 0.0)
    scale_t = jnp.where(place >= 6, scale_t, 0.0)
    last = dot(left_last, heads_ref[teacher_width + 3 * quarter :, :], ((1,), (1,)))
    correction = jnp.zeros((wide, quarter), F32)
    for j in range(3):
        both = dot(left, heads_ref[teacher_width + j * quarter : teacher_width + (j + 1) * quarter, :], ((1,), (1,)))
        exact = both[:wide] + both[wide:] + last[j * wide : (j + 1) * wide] + last[(3 + j) * wide : (4 + j) * wide]
        sent = exact.astype(BF16).astype(F32)
        residue = exact - sent
        if j < 2:
            correction += residue * (scale_s, scale_t)[j]
        else:
            sent += correction
        scaled = residue * scale
        sent += in_third * (pltpu.roll(scaled, 4, 0) + pltpu.roll(scaled, 2, 0))
        for shard in range(shards):
            out_ref[shard, :, j * quarter : (j + 1) * quarter] = sent[8 * shard : 8 * shard + 8].astype(BF16)
    lane = iota((8, 128), 1)
    shared = jnp.zeros((8, 128), F32)
    wide_parts = parts.astype(F32)
    for group in range(tokens // 8):
        shared = jnp.where(lane // 32 == group + 1, wide_parts[8 * group : 8 * group + 8], shared)
    for shard in range(shards):
        block = jnp.where(lane < 32, by_row[8 * shard : 8 * shard + 8], shared)
        out_ref[shard, :, 3 * quarter :] = block.astype(BF16)


def sum_parts(tail):
    shards = tail.shape[0]
    flat = tail.astype(F32).reshape(shards * 8, 128)
    return flat + pltpu.roll(flat, 120, 1) + pltpu.roll(flat, 112, 1)


def fold(flat, lane):
    shards = flat.shape[0] // 8
    stats = [flat[:, lane + k : lane + k + 1].reshape(shards, 8, 1) for k in range(8)]
    top_t = jnp.max(stats[0], axis=0)
    factor_t = jnp.exp(stats[0] - top_t)
    top_s = jnp.max(stats[3], axis=0)
    factor_s = jnp.exp(stats[3] - top_s)
    mass_t = jnp.sum(stats[1] * factor_t, axis=0)
    mass_s = jnp.sum(stats[4] * factor_s, axis=0)
    return stats, top_t, factor_t, mass_t, top_s, factor_s, mass_s


def logit_grad_kernel(tail_ref, teacher_ref, student_ref, target_ref, out_ref):
    flat = sum_parts(tail_ref[...])
    folded = [fold(flat, 32 * group + 32) for group in range(out_ref.shape[0] // 8)]
    top_t, mass_t, top_s, mass_s = [jnp.concatenate([f[i] for f in folded], axis=0) for i in (1, 3, 4, 6)]
    teacher_prob = jnp.exp(teacher_ref[...] - top_t) / mass_t
    student_prob = jnp.exp(student_ref[...] - top_s) / mass_s
    out_ref[...] = (2.0 * student_prob - teacher_prob - target_ref[...]).astype(BF16)


def owner_kernel(arrived_ref, out_ref, loss_ref):
    shards, _, lanes = arrived_ref.shape
    quarter = (lanes - 128) // 3
    stats, top_t, factor_t, mass_t, top_s, factor_s, mass_s = fold(sum_parts(arrived_ref[:, :, 3 * quarter :]), 0)
    cross = jnp.sum(stats[2] * factor_t, axis=0)
    picked = jnp.sum(stats[5], axis=0)
    picked_t = jnp.sum(stats[6], axis=0)
    loss = cross / mass_t - top_t - jnp.log(mass_t) + 2.0 * (top_s + jnp.log(mass_s)) - picked
    square = (8, 128)
    same = lax.broadcasted_iota(jnp.int32, square, 0) == lax.broadcasted_iota(jnp.int32, square, 1)
    loss_ref[...] = jnp.sum(jnp.where(same, loss, 0.0), axis=0, keepdims=True)
    label_grad = 2.0 * (jnp.exp(picked - top_s) / mass_s) - jnp.exp(picked_t - top_t) / mass_t - 1.0
    rounding = label_grad.astype(BF16).astype(F32) - label_grad
    weight_s = factor_s / mass_s
    weight_t = factor_t / mass_t
    share = 0.8 * weight_s * stats[4] + 0.2 * weight_t * stats[1]
    kappa = jnp.where(stats[7] > 2.0, 1.0, 0.0)
    weight_l = jnp.where(stats[7] > 0.5, 1.0 - (1.0 - kappa) * rounding, share)
    weight_s = 2.0 * (weight_s - kappa / stats[4])
    weight_t = kappa / stats[1] - weight_t
    place = lax.broadcasted_iota(jnp.int32, (shards, 8, 1), 1)
    last = jnp.zeros((8, quarter), F32)
    for j, weight_last in enumerate((weight_s, weight_t, weight_l)):
        weight = jnp.where(
            place < 2, weight_s, jnp.where(place < 4, weight_t, jnp.where(place < 6, weight_l, weight_last))
        )
        piece = jnp.zeros((8, quarter), F32)
        for shard in range(shards):
            piece += weight[shard] * arrived_ref[shard, :, j * quarter : (j + 1) * quarter].astype(F32)
        last += piece
        out_ref[:, j * quarter : (j + 1) * quarter] = piece[0:2] + piece[2:4] + piece[4:6]
    out_ref[:, 3 * quarter :] = last[6:8]


def two_exchanges(teacher_hidden, student_hidden, teacher_head, student_head, labels, *, shards):
    own = labels.shape[0]
    teacher_width, width = teacher_hidden.shape[1], student_hidden.shape[1]
    columns_here = student_head.shape[1]
    tokens = shards * own
    quarter = width // 4
    here = lax.axis_index("vocab").astype(jnp.int32)
    rows = gather_tokens(teacher_hidden, student_hidden, labels, shards)
    student_rows = rows[:, :, teacher_width : teacher_width + width].reshape(tokens, width)
    other = [(0, 1), (1, 0)]
    student_other = lax.ppermute(student_rows, "rows", other)

    square = jax.ShapeDtypeStruct((tokens, columns_here), F32)
    payload, teacher_logits, student_logits, target = pl.pallas_call(
        raw_partial_kernel,
        out_shape=(jax.ShapeDtypeStruct((shards, 8, 3 * quarter + 128), BF16), square, square, square),
        in_specs=[SMEM, VMEM, VMEM],
        out_specs=(VMEM, VMEM, VMEM, VMEM),
        compiler_params=SMALL,
    )((here * columns_here)[None], rows, jnp.concatenate([teacher_head, student_head], axis=0))
    arrived = swap(payload)
    grad_rows = pl.pallas_call(
        logit_grad_kernel,
        out_shape=jax.ShapeDtypeStruct((tokens, columns_here), BF16),
        in_specs=[VMEM] * 4,
        out_specs=VMEM,
        compiler_params=SMALL,
    )(arrived[:, :, 3 * quarter :], teacher_logits, student_logits, target)
    grad_other = lax.ppermute(grad_rows, "rows", other)
    hidden_grad, loss = pl.pallas_call(
        owner_kernel,
        out_shape=(jax.ShapeDtypeStruct((own, width), F32), jax.ShapeDtypeStruct((1, 128), F32)),
        in_specs=[VMEM],
        out_specs=(VMEM, VMEM),
        compiler_params=SMALL,
    )(arrived)
    token_loss = loss[0, :own]
    head_grad = lax.dot_general(
        jnp.concatenate([student_rows, student_other], axis=0),
        jnp.concatenate([grad_rows, grad_other], axis=0),
        (((0,), (0,)), ((), ())),
        preferred_element_type=F32,
    )
    return (token_loss, hidden_grad, head_grad)


def three_exchanges(teacher_hidden, student_hidden, teacher_head, student_head, labels, *, shards):
    own = labels.shape[0]
    student_width = student_hidden.shape[1]
    columns_here = student_head.shape[1]
    first_column = lax.axis_index("vocab") * columns_here
    rows = gather_tokens(teacher_hidden, student_hidden, labels, shards).reshape(shards * own, -1)
    teacher_width = teacher_hidden.shape[1]
    teacher_rows = rows[:, :teacher_width]
    student_rows = rows[:, teacher_width : teacher_width + student_width]
    code = rows[:, teacher_width + student_width :].astype(jnp.int32)
    label_rows = code[:, 0] * 128 + code[:, 1]
    other = [(0, 1), (1, 0)]
    student_other = lax.ppermute(student_rows, "rows", other)

    teacher_logits = jnp.dot(teacher_rows, teacher_head, preferred_element_type=F32)
    student_logits = jnp.dot(student_rows, student_head, preferred_element_type=F32)
    columns = lax.broadcasted_iota(jnp.int32, student_logits.shape, 1)
    target = (label_rows - first_column)[:, None] == columns
    top_t = jnp.max(teacher_logits, axis=1, keepdims=True)
    exp_t = jnp.exp(teacher_logits - top_t)
    top_s = jnp.max(student_logits, axis=1, keepdims=True)
    exp_s = jnp.exp(student_logits - top_s)
    stats = jnp.concatenate(
        [
            top_t,
            jnp.sum(exp_t, axis=1, keepdims=True),
            jnp.sum(exp_t * (teacher_logits - student_logits), axis=1, keepdims=True),
            top_s,
            jnp.sum(exp_s, axis=1, keepdims=True),
            jnp.sum(jnp.where(target, student_logits, 0.0), axis=1, keepdims=True),
        ],
        axis=1,
    )
    every = swap(jnp.broadcast_to(stats[None], (shards,) + stats.shape))
    all_top_t = jnp.max(every[:, :, 0], axis=0)
    factor_t = jnp.exp(every[:, :, 0] - all_top_t[None])
    all_top_s = jnp.max(every[:, :, 3], axis=0)
    factor_s = jnp.exp(every[:, :, 3] - all_top_s[None])
    mass_t = jnp.sum(every[:, :, 1] * factor_t, axis=0)
    cross = jnp.sum(every[:, :, 2] * factor_t, axis=0)
    mass_s = jnp.sum(every[:, :, 4] * factor_s, axis=0)
    picked = jnp.sum(every[:, :, 5], axis=0)
    loss = cross / mass_t - all_top_t - jnp.log(mass_t) + 2.0 * (all_top_s + jnp.log(mass_s)) - picked
    token_loss = lax.dynamic_slice_in_dim(loss, lax.axis_index("vocab") * own, own, 0)

    teacher_prob = jnp.exp(teacher_logits - all_top_t[:, None]) / mass_t[:, None]
    student_prob = jnp.exp(student_logits - all_top_s[:, None]) / mass_s[:, None]
    grad_rows = (2.0 * student_prob - teacher_prob - target.astype(F32)).astype(BF16)
    grad_other = lax.ppermute(grad_rows, "rows", other)
    partial = lax.dot_general(grad_rows, student_head, (((1,), (1,)), ((), ())), preferred_element_type=F32)
    arrived = swap(partial.astype(BF16).reshape(shards, own, student_width))
    hidden_grad = jnp.sum(arrived.astype(F32), axis=0)
    head_grad = lax.dot_general(
        jnp.concatenate([student_rows, student_other], axis=0),
        jnp.concatenate([grad_rows, grad_other], axis=0),
        (((0,), (0,)), ((), ())),
        preferred_element_type=F32,
    )
    return (token_loss, hidden_grad, head_grad)


def solution(mesh):
    tokens = ("groups", "vocab", "rows")
    in_specs = (P(tokens, None), P(tokens, None), P(None, "vocab"), P(None, "vocab"), P(tokens))
    out_specs = (P(tokens), P(tokens, None), P("groups", "vocab"))

    def body(*arrays):
        shards = mesh.shape["vocab"]
        own = arrays[4].shape[0]
        small = own == 2 and shards % 4 == 0 and shards * own <= 24
        return (two_exchanges if small else three_exchanges)(*arrays, shards=shards)

    return jax.shard_map(body, mesh=mesh, in_specs=in_specs, out_specs=out_specs, check_vma=False)
```

```python
import jax
import jax.numpy as jnp
from jax import lax
from jax.experimental import pallas as pl
from jax.experimental.pallas import tpu as pltpu
from jax.sharding import PartitionSpec as P

F32 = jnp.float32
BF16 = jnp.bfloat16
CODE = 128


UNROLL = 16
PIECES = 4
SMEM = pl.BlockSpec(memory_space=pltpu.SMEM)
VMEM = pl.BlockSpec(memory_space=pltpu.VMEM)
SMALL = pltpu.CompilerParams(vmem_limit_bytes=16 * 1024 * 1024)


def over_shards(shards, body):
    if shards <= UNROLL:
        for shard in range(shards):
            body(shard)
    else:
        pl.loop(0, shards)(body)


def swap(blocks):
    return lax.all_to_all(blocks, "vocab", split_axis=0, concat_axis=0, tiled=True)


def payload_kernel(labels_ref, teacher_ref, student_ref, out_ref):
    shards, own, _ = out_ref.shape
    teacher_width, student_width = teacher_ref.shape[1], student_ref.shape[1]
    row = lax.broadcasted_iota(jnp.int32, (own, CODE), 0)
    lane = lax.broadcasted_iota(jnp.int32, (own, CODE), 1)
    digits = jnp.zeros((own, CODE), jnp.int32)
    for token in range(own):
        label = labels_ref[token]
        pair = jnp.where(lane == 0, label >> 7, label & 127)
        digits = jnp.where(row == token, pair, digits)
    teacher = teacher_ref[...]
    student = student_ref[...]
    code = digits.astype(F32).astype(BF16)

    def write(shard):
        out_ref[shard, :, :teacher_width] = teacher
        out_ref[shard, :, teacher_width : teacher_width + student_width] = student
        out_ref[shard, :, teacher_width + student_width :] = code

    over_shards(shards, write)


def gather_tokens(teacher_hidden, student_hidden, labels, shards):
    own, teacher_width = teacher_hidden.shape
    student_width = student_hidden.shape[1]
    payload = pl.pallas_call(
        payload_kernel,
        out_shape=jax.ShapeDtypeStruct((shards, own, teacher_width + student_width + CODE), BF16),
        in_specs=[SMEM, VMEM, VMEM],
        out_specs=VMEM,
    )(labels, teacher_hidden, student_hidden)
    return swap(payload)


def raw_partial_kernel(first_ref, rows_ref, heads_ref, out_ref, teacher_ref, student_ref, target_ref):
    shards, own, _ = rows_ref.shape
    tokens = shards * own
    wide = 8 * shards
    columns = heads_ref.shape[1]
    quarter = (out_ref.shape[2] - 128) // 3
    width = 4 * quarter
    teacher_width = heads_ref.shape[0] - width

    def iota(shape, dim):
        return lax.broadcasted_iota(jnp.int32, shape, dim)

    def dot(left, right, dims):
        return lax.dot_general(left, right, (dims, ((), ())), preferred_element_type=F32)

    def rows_of(start, size):
        return jnp.concatenate([rows_ref[shard, :, start : start + size] for shard in range(shards)], axis=0)

    student = dot(rows_of(teacher_width, width), heads_ref[teacher_width:, :], ((1,), (0,)))
    teacher = dot(rows_of(0, teacher_width), heads_ref[:teacher_width, :], ((1,), (0,)))
    code = rows_of(teacher_width + width, CODE).astype(F32)
    lane = iota(code.shape, 1)
    label = jnp.sum(jnp.where(lane == 0, code * 128.0, jnp.where(lane == 1, code, 0.0)), axis=1, keepdims=True)
    target = (label.astype(jnp.int32) - first_ref[0] == iota((tokens, columns), 1)).astype(F32)
    teacher_ref[...] = teacher
    student_ref[...] = student
    target_ref[...] = target

    def total(array):
        return jnp.sum(array, axis=1, keepdims=True)

    top_t = jnp.max(teacher, axis=1, keepdims=True)
    top_s = jnp.max(student, axis=1, keepdims=True)
    exp_t = jnp.exp(teacher - top_t)
    exp_s = jnp.exp(student - top_s)
    mass_t, mass_s = total(exp_t), total(exp_s)
    combined = exp_s * (2.0 / mass_s) - exp_t / mass_t
    kappa = (total(target * combined) > 0.5).astype(F32)
    stats = [
        top_t,
        mass_t,
        total(exp_t * (teacher - student)),
        top_s,
        mass_s,
        total(target * student),
        total(target * teacher),
        2.0 * kappa + total(target),
    ]
    lane = iota((tokens, 128), 1)
    table = jnp.zeros((tokens, 128), F32)
    for k, stat in enumerate(stats):
        table = jnp.where(lane % 8 == k, stat, table)
    first = table.astype(BF16).astype(F32)
    second = (table - first).astype(BF16).astype(F32)
    part = (lane % 32) // 8
    parts = jnp.where(
        part == 0, first, jnp.where(part == 1, second, jnp.where(part == 2, table - first - second, 0.0))
    ).astype(BF16)

    row, column = iota((wide, tokens), 0), iota((wide, tokens), 1)
    of_token = (column == (row // 8) * 2 + row % 2).astype(F32).astype(BF16)
    by_row = dot(of_token, parts, ((1,), (0,)))

    def stat_by_row(k):
        picked = by_row[:, k : k + 1] + by_row[:, 8 + k : 9 + k] + by_row[:, 16 + k : 17 + k]
        return picked

    members = jnp.concatenate([exp_s, exp_t, kappa * combined * total(target) - target], axis=0)
    member_high = members.astype(BF16)
    member_low = (members - member_high.astype(F32)).astype(BF16)
    row, column = iota((wide, 3 * tokens), 0), iota((wide, 3 * tokens), 1)
    place = row % 8
    token = (row // 8) * 2 + row % 2
    picks = [((place < 6) & (column == (place // 2) * tokens + token)).astype(F32)]
    for j in range(3):
        picks.append(((place >= 6) & (column == j * tokens + token)).astype(F32))
    pick = jnp.concatenate(picks, axis=0).astype(BF16)
    left_high = dot(pick, member_high, ((1,), (0,))).astype(BF16)
    left_low = dot(pick, member_low, ((1,), (0,))).astype(BF16)
    left = jnp.concatenate([left_high[:wide], left_low[:wide]], axis=0)
    left_last = jnp.concatenate([left_high[wide:], left_low[wide:]], axis=0)

    place = iota((wide, 1), 0) % 8
    has_label = stat_by_row(7) > 0.5
    scale_s = jnp.where(has_label, 0.0, 2.0 / stat_by_row(4))
    scale_t = jnp.where(has_label, 0.0, -1.0 / stat_by_row(1))
    scale = jnp.where(place < 2, scale_s, jnp.where(place < 4, scale_t, 0.0))
    in_third = ((place == 4) | (place == 5)).astype(F32)
    scale_s = jnp.where(place >= 6, scale_s, 0.0)
    scale_t = jnp.where(place >= 6, scale_t, 0.0)
    last = dot(left_last, heads_ref[teacher_width + 3 * quarter :, :], ((1,), (1,)))
    correction = jnp.zeros((wide, quarter), F32)
    for j in range(3):
        both = dot(left, heads_ref[teacher_width + j * quarter : teacher_width + (j + 1) * quarter, :], ((1,), (1,)))
        exact = both[:wide] + both[wide:] + last[j * wide : (j + 1) * wide] + last[(3 + j) * wide : (4 + j) * wide]
        sent = exact.astype(BF16).astype(F32)
        residue = exact - sent
        if j < 2:
            correction += residue * (scale_s, scale_t)[j]
        else:
            sent += correction
        scaled = residue * scale
        sent += in_third * (pltpu.roll(scaled, 4, 0) + pltpu.roll(scaled, 2, 0))
        for shard in range(shards):
            out_ref[shard, :, j * quarter : (j + 1) * quarter] = sent[8 * shard : 8 * shard + 8].astype(BF16)
    lane = iota((8, 128), 1)
    shared = jnp.zeros((8, 128), F32)
    wide_parts = parts.astype(F32)
    for group in range(tokens // 8):
        shared = jnp.where(lane // 32 == group + 1, wide_parts[8 * group : 8 * group + 8], shared)
    for shard in range(shards):
        block = jnp.where(lane < 32, by_row[8 * shard : 8 * shard + 8], shared)
        out_ref[shard, :, 3 * quarter :] = block.astype(BF16)


def sum_parts(tail):
    shards = tail.shape[0]
    flat = tail.astype(F32).reshape(shards * 8, 128)
    return flat + pltpu.roll(flat, 120, 1) + pltpu.roll(flat, 112, 1)


def fold(flat, lane):
    shards = flat.shape[0] // 8
    stats = [flat[:, lane + k : lane + k + 1].reshape(shards, 8, 1) for k in range(8)]
    top_t = jnp.max(stats[0], axis=0)
    factor_t = jnp.exp(stats[0] - top_t)
    top_s = jnp.max(stats[3], axis=0)
    factor_s = jnp.exp(stats[3] - top_s)
    mass_t = jnp.sum(stats[1] * factor_t, axis=0)
    mass_s = jnp.sum(stats[4] * factor_s, axis=0)
    return stats, top_t, factor_t, mass_t, top_s, factor_s, mass_s


def logit_grad_kernel(tail_ref, teacher_ref, student_ref, target_ref, out_ref):
    flat = sum_parts(tail_ref[...])
    folded = [fold(flat, 32 * group + 32) for group in range(out_ref.shape[0] // 8)]
    top_t, mass_t, top_s, mass_s = [jnp.concatenate([f[i] for f in folded], axis=0) for i in (1, 3, 4, 6)]
    teacher_prob = jnp.exp(teacher_ref[...] - top_t) / mass_t
    student_prob = jnp.exp(student_ref[...] - top_s) / mass_s
    out_ref[...] = (2.0 * student_prob - teacher_prob - target_ref[...]).astype(BF16)


def owner_kernel(arrived_ref, out_ref, loss_ref):
    shards, _, lanes = arrived_ref.shape
    quarter = (lanes - 128) // 3
    stats, top_t, factor_t, mass_t, top_s, factor_s, mass_s = fold(sum_parts(arrived_ref[:, :, 3 * quarter :]), 0)
    cross = jnp.sum(stats[2] * factor_t, axis=0)
    picked = jnp.sum(stats[5], axis=0)
    picked_t = jnp.sum(stats[6], axis=0)
    loss = cross / mass_t - top_t - jnp.log(mass_t) + 2.0 * (top_s + jnp.log(mass_s)) - picked
    token = lax.broadcasted_iota(jnp.int32, (8, 1), 0)
    for t in range(out_ref.shape[0]):
        loss_ref[t] = jnp.sum(jnp.where(token == t, loss, 0.0))
    label_grad = 2.0 * (jnp.exp(picked - top_s) / mass_s) - jnp.exp(picked_t - top_t) / mass_t - 1.0
    rounding = label_grad.astype(BF16).astype(F32) - label_grad
    weight_s = factor_s / mass_s
    weight_t = factor_t / mass_t
    share = 0.8 * weight_s * stats[4] + 0.2 * weight_t * stats[1]
    kappa = jnp.where(stats[7] > 2.0, 1.0, 0.0)
    weight_l = jnp.where(stats[7] > 0.5, 1.0 - (1.0 - kappa) * rounding, share)
    weight_s = 2.0 * (weight_s - kappa / stats[4])
    weight_t = kappa / stats[1] - weight_t
    place = lax.broadcasted_iota(jnp.int32, (shards, 8, 1), 1)
    last = jnp.zeros((8, quarter), F32)
    for j, weight_last in enumerate((weight_s, weight_t, weight_l)):
        weight = jnp.where(
            place < 2, weight_s, jnp.where(place < 4, weight_t, jnp.where(place < 6, weight_l, weight_last))
        )
        piece = jnp.zeros((8, quarter), F32)
        for shard in range(shards):
            piece += weight[shard] * arrived_ref[shard, :, j * quarter : (j + 1) * quarter].astype(F32)
        last += piece
        out_ref[:, j * quarter : (j + 1) * quarter] = piece[0:2] + piece[2:4] + piece[4:6]
    out_ref[:, 3 * quarter :] = last[6:8]


def head_grad_kernel(hidden_ref, grad_ref, other_ref, out_ref, total_ref, sems):
    grads = jnp.concatenate([grad_ref[...], other_ref[...]], axis=0)
    size = hidden_ref.shape[0] // PIECES
    copies = []
    for piece in range(PIECES):
        rows = pl.ds(piece * size, size)
        total_ref[rows, :] = jnp.dot(hidden_ref[rows, :], grads, preferred_element_type=F32)
        copies.append(pltpu.make_async_copy(total_ref.at[rows, :], out_ref.at[rows, :], sems.at[piece]))
        copies[-1].start()
    for copy in copies:
        copy.wait()


def two_exchanges(teacher_hidden, student_hidden, teacher_head, student_head, labels, *, shards):
    own = labels.shape[0]
    teacher_width, width = teacher_hidden.shape[1], student_hidden.shape[1]
    columns_here = student_head.shape[1]
    tokens = shards * own
    quarter = width // 4
    here = lax.axis_index("vocab").astype(jnp.int32)
    rows = gather_tokens(teacher_hidden, student_hidden, labels, shards)
    student_rows = rows[:, :, teacher_width : teacher_width + width].reshape(tokens, width)
    other = [(0, 1), (1, 0)]
    student_other = lax.ppermute(student_rows, "rows", other)

    square = jax.ShapeDtypeStruct((tokens, columns_here), F32)
    payload, teacher_logits, student_logits, target = pl.pallas_call(
        raw_partial_kernel,
        out_shape=(jax.ShapeDtypeStruct((shards, 8, 3 * quarter + 128), BF16), square, square, square),
        in_specs=[SMEM, VMEM, VMEM],
        out_specs=(VMEM, VMEM, VMEM, VMEM),
        compiler_params=SMALL,
    )((here * columns_here)[None], rows, jnp.concatenate([teacher_head, student_head], axis=0))
    arrived = swap(payload)
    grad_rows = pl.pallas_call(
        logit_grad_kernel,
        out_shape=jax.ShapeDtypeStruct((tokens, columns_here), BF16),
        in_specs=[VMEM] * 4,
        out_specs=VMEM,
        compiler_params=SMALL,
    )(arrived[:, :, 3 * quarter :], teacher_logits, student_logits, target)
    grad_other = lax.ppermute(grad_rows, "rows", other)
    hidden_grad, token_loss = pl.pallas_call(
        owner_kernel,
        out_shape=(jax.ShapeDtypeStruct((own, width), F32), jax.ShapeDtypeStruct((own,), F32)),
        in_specs=[VMEM],
        out_specs=(VMEM, SMEM),
        compiler_params=SMALL,
    )(arrived)
    head_grad = pl.pallas_call(
        head_grad_kernel,
        out_shape=jax.ShapeDtypeStruct((width, columns_here), F32),
        in_specs=[VMEM] * 3,
        out_specs=pl.BlockSpec(memory_space=pl.ANY),
        scratch_shapes=[pltpu.VMEM((width, columns_here), F32), pltpu.SemaphoreType.DMA((PIECES,))],
        compiler_params=SMALL,
    )(jnp.concatenate([student_rows, student_other], axis=0).T, grad_rows, grad_other)
    return (token_loss, hidden_grad, head_grad)


def three_exchanges(teacher_hidden, student_hidden, teacher_head, student_head, labels, *, shards):
    own = labels.shape[0]
    student_width = student_hidden.shape[1]
    columns_here = student_head.shape[1]
    first_column = lax.axis_index("vocab") * columns_here
    rows = gather_tokens(teacher_hidden, student_hidden, labels, shards).reshape(shards * own, -1)
    teacher_width = teacher_hidden.shape[1]
    teacher_rows = rows[:, :teacher_width]
    student_rows = rows[:, teacher_width : teacher_width + student_width]
    code = rows[:, teacher_width + student_width :].astype(jnp.int32)
    label_rows = code[:, 0] * 128 + code[:, 1]
    other = [(0, 1), (1, 0)]
    student_other = lax.ppermute(student_rows, "rows", other)

    teacher_logits = jnp.dot(teacher_rows, teacher_head, preferred_element_type=F32)
    student_logits = jnp.dot(student_rows, student_head, preferred_element_type=F32)
    columns = lax.broadcasted_iota(jnp.int32, student_logits.shape, 1)
    target = (label_rows - first_column)[:, None] == columns
    top_t = jnp.max(teacher_logits, axis=1, keepdims=True)
    exp_t = jnp.exp(teacher_logits - top_t)
    top_s = jnp.max(student_logits, axis=1, keepdims=True)
    exp_s = jnp.exp(student_logits - top_s)
    stats = jnp.concatenate(
        [
            top_t,
            jnp.sum(exp_t, axis=1, keepdims=True),
            jnp.sum(exp_t * (teacher_logits - student_logits), axis=1, keepdims=True),
            top_s,
            jnp.sum(exp_s, axis=1, keepdims=True),
            jnp.sum(jnp.where(target, student_logits, 0.0), axis=1, keepdims=True),
        ],
        axis=1,
    )
    every = swap(jnp.broadcast_to(stats[None], (shards,) + stats.shape))
    all_top_t = jnp.max(every[:, :, 0], axis=0)
    factor_t = jnp.exp(every[:, :, 0] - all_top_t[None])
    all_top_s = jnp.max(every[:, :, 3], axis=0)
    factor_s = jnp.exp(every[:, :, 3] - all_top_s[None])
    mass_t = jnp.sum(every[:, :, 1] * factor_t, axis=0)
    cross = jnp.sum(every[:, :, 2] * factor_t, axis=0)
    mass_s = jnp.sum(every[:, :, 4] * factor_s, axis=0)
    picked = jnp.sum(every[:, :, 5], axis=0)
    loss = cross / mass_t - all_top_t - jnp.log(mass_t) + 2.0 * (all_top_s + jnp.log(mass_s)) - picked
    token_loss = lax.dynamic_slice_in_dim(loss, lax.axis_index("vocab") * own, own, 0)

    teacher_prob = jnp.exp(teacher_logits - all_top_t[:, None]) / mass_t[:, None]
    student_prob = jnp.exp(student_logits - all_top_s[:, None]) / mass_s[:, None]
    grad_rows = (2.0 * student_prob - teacher_prob - target.astype(F32)).astype(BF16)
    grad_other = lax.ppermute(grad_rows, "rows", other)
    partial = lax.dot_general(grad_rows, student_head, (((1,), (1,)), ((), ())), preferred_element_type=F32)
    arrived = swap(partial.astype(BF16).reshape(shards, own, student_width))
    hidden_grad = jnp.sum(arrived.astype(F32), axis=0)
    head_grad = lax.dot_general(
        jnp.concatenate([student_rows, student_other], axis=0),
        jnp.concatenate([grad_rows, grad_other], axis=0),
        (((0,), (0,)), ((), ())),
        preferred_element_type=F32,
    )
    return (token_loss, hidden_grad, head_grad)


def solution(mesh):
    tokens = ("groups", "vocab", "rows")
    in_specs = (P(tokens, None), P(tokens, None), P(None, "vocab"), P(None, "vocab"), P(tokens))
    out_specs = (P(tokens), P(tokens, None), P("groups", "vocab"))

    def body(*arrays):
        shards = mesh.shape["vocab"]
        own = arrays[4].shape[0]
        small = own == 2 and shards % 4 == 0 and shards * own <= 24
        return (two_exchanges if small else three_exchanges)(*arrays, shards=shards)

    return jax.shard_map(body, mesh=mesh, in_specs=in_specs, out_specs=out_specs, check_vma=False)
```

```python
import jax
import jax.numpy as jnp
from jax import lax
from jax.experimental import pallas as pl
from jax.experimental.pallas import tpu as pltpu
from jax.sharding import PartitionSpec as P

F32 = jnp.float32
BF16 = jnp.bfloat16
CODE = 128


UNROLL = 16
PIECES = 4
SMEM = pl.BlockSpec(memory_space=pltpu.SMEM)
VMEM = pl.BlockSpec(memory_space=pltpu.VMEM)
ANY = pl.BlockSpec(memory_space=pl.ANY)
SMALL = pltpu.CompilerParams(vmem_limit_bytes=16 * 1024 * 1024)


def over_shards(shards, body):
    if shards <= UNROLL:
        for shard in range(shards):
            body(shard)
    else:
        pl.loop(0, shards)(body)


def swap(blocks):
    return lax.all_to_all(blocks, "vocab", split_axis=0, concat_axis=0, tiled=True)


def payload_kernel(labels_ref, teacher_ref, student_ref, out_ref):
    shards, own, _ = out_ref.shape
    teacher_width, student_width = teacher_ref.shape[1], student_ref.shape[1]
    teacher = teacher_ref[...]
    student = student_ref[...]
    code = label_digits(labels_ref, own)

    def write(shard):
        out_ref[shard, :, :teacher_width] = teacher
        out_ref[shard, :, teacher_width : teacher_width + student_width] = student
        out_ref[shard, :, teacher_width + student_width :] = code

    over_shards(shards, write)


def label_digits(labels_ref, own):
    row = lax.broadcasted_iota(jnp.int32, (own, CODE), 0)
    lane = lax.broadcasted_iota(jnp.int32, (own, CODE), 1)
    digits = jnp.zeros((own, CODE), jnp.int32)
    for token in range(own):
        label = labels_ref[token]
        pair = jnp.where(lane == 0, label >> 7, label & 127)
        digits = jnp.where(row == token, pair, digits)
    return digits.astype(F32).astype(BF16)


def payload_copy_kernel(labels_hbm, teacher_hbm, student_hbm, out_hbm, labels_ref, code_ref, label_sem, sems):
    shards, own, _ = out_hbm.shape
    teacher_width, width = teacher_hbm.shape[1], student_hbm.shape[1]
    labels_in = pltpu.make_async_copy(labels_hbm, labels_ref, label_sem)
    labels_in.start()
    copies = []

    def copy_out(source, start, size):
        for shard in range(shards):
            target = out_hbm.at[shard, :, pl.ds(start, size)]
            copies.append(pltpu.make_async_copy(source, target, sems.at[len(copies)]))
            copies[-1].start()

    copy_out(teacher_hbm, 0, teacher_width)
    copy_out(student_hbm, teacher_width, width)
    labels_in.wait()
    code_ref[...] = label_digits(labels_ref, own)
    copy_out(code_ref, teacher_width + width, CODE)
    for copy in copies:
        copy.wait()


def gather_tokens(teacher_hidden, student_hidden, labels, shards):
    own, teacher_width = teacher_hidden.shape
    student_width = student_hidden.shape[1]
    out_shape = jax.ShapeDtypeStruct((shards, own, teacher_width + student_width + CODE), BF16)
    if shards <= UNROLL:
        payload = pl.pallas_call(
            payload_copy_kernel,
            out_shape=out_shape,
            in_specs=[ANY] * 3,
            out_specs=ANY,
            scratch_shapes=[
                pltpu.SMEM((own,), jnp.int32),
                pltpu.VMEM((own, CODE), BF16),
                pltpu.SemaphoreType.DMA,
                pltpu.SemaphoreType.DMA((3 * shards,)),
            ],
        )(labels, teacher_hidden, student_hidden)
    else:
        payload = pl.pallas_call(
            payload_kernel,
            out_shape=out_shape,
            in_specs=[SMEM, VMEM, VMEM],
            out_specs=VMEM,
        )(labels, teacher_hidden, student_hidden)
    return swap(payload)


def raw_partial_kernel(
    first_ref, rows_ref, heads_ref, out_hbm, teacher_ref, student_ref, target_ref, out_ref, sems
):
    shards, own, _ = rows_ref.shape
    tokens = shards * own
    wide = 8 * shards
    columns = heads_ref.shape[1]
    quarter = (out_ref.shape[2] - 128) // 3
    width = 4 * quarter
    teacher_width = heads_ref.shape[0] - width

    def iota(shape, dim):
        return lax.broadcasted_iota(jnp.int32, shape, dim)

    def dot(left, right, dims):
        return lax.dot_general(left, right, (dims, ((), ())), preferred_element_type=F32)

    copies = []

    def send_out(piece, start, size):
        lanes = pl.ds(start, size)
        copies.append(pltpu.make_async_copy(out_ref.at[:, :, lanes], out_hbm.at[:, :, lanes], sems.at[piece]))
        copies[-1].start()

    def rows_of(start, size):
        return jnp.concatenate([rows_ref[shard, :, start : start + size] for shard in range(shards)], axis=0)

    student = dot(rows_of(teacher_width, width), heads_ref[teacher_width:, :], ((1,), (0,)))
    teacher = dot(rows_of(0, teacher_width), heads_ref[:teacher_width, :], ((1,), (0,)))
    code = rows_of(teacher_width + width, CODE).astype(F32)
    lane = iota(code.shape, 1)
    label = jnp.sum(jnp.where(lane == 0, code * 128.0, jnp.where(lane == 1, code, 0.0)), axis=1, keepdims=True)
    target = (label.astype(jnp.int32) - first_ref[0] == iota((tokens, columns), 1)).astype(F32)
    teacher_ref[...] = teacher
    student_ref[...] = student
    target_ref[...] = target

    def total(array):
        return jnp.sum(array, axis=1, keepdims=True)

    top_t = jnp.max(teacher, axis=1, keepdims=True)
    top_s = jnp.max(student, axis=1, keepdims=True)
    exp_t = jnp.exp(teacher - top_t)
    exp_s = jnp.exp(student - top_s)
    mass_t, mass_s = total(exp_t), total(exp_s)
    combined = exp_s * (2.0 / mass_s) - exp_t / mass_t
    kappa = (total(target * combined) > 0.5).astype(F32)
    stats = [
        top_t,
        mass_t,
        total(exp_t * (teacher - student)),
        top_s,
        mass_s,
        total(target * student),
        total(target * teacher),
        2.0 * kappa + total(target),
    ]
    lane = iota((tokens, 128), 1)
    table = jnp.zeros((tokens, 128), F32)
    for k, stat in enumerate(stats):
        table = jnp.where(lane % 8 == k, stat, table)
    first = table.astype(BF16).astype(F32)
    second = (table - first).astype(BF16).astype(F32)
    part = (lane % 32) // 8
    parts = jnp.where(
        part == 0, first, jnp.where(part == 1, second, jnp.where(part == 2, table - first - second, 0.0))
    ).astype(BF16)

    row, column = iota((wide, tokens), 0), iota((wide, tokens), 1)
    of_token = (column == (row // 8) * 2 + row % 2).astype(F32).astype(BF16)
    by_row = dot(of_token, parts, ((1,), (0,)))

    def stat_by_row(k):
        picked = by_row[:, k : k + 1] + by_row[:, 8 + k : 9 + k] + by_row[:, 16 + k : 17 + k]
        return picked

    lane = iota((8, 128), 1)
    shared = jnp.zeros((8, 128), F32)
    wide_parts = parts.astype(F32)
    for group in range(tokens // 8):
        shared = jnp.where(lane // 32 == group + 1, wide_parts[8 * group : 8 * group + 8], shared)
    for shard in range(shards):
        block = jnp.where(lane < 32, by_row[8 * shard : 8 * shard + 8], shared)
        out_ref[shard, :, 3 * quarter :] = block.astype(BF16)
    send_out(3, 3 * quarter, 128)

    members = jnp.concatenate([exp_s, exp_t, kappa * combined * total(target) - target], axis=0)
    member_high = members.astype(BF16)
    member_low = (members - member_high.astype(F32)).astype(BF16)
    row, column = iota((wide, 3 * tokens), 0), iota((wide, 3 * tokens), 1)
    place = row % 8
    token = (row // 8) * 2 + row % 2
    picks = [((place < 6) & (column == (place // 2) * tokens + token)).astype(F32)]
    for j in range(3):
        picks.append(((place >= 6) & (column == j * tokens + token)).astype(F32))
    pick = jnp.concatenate(picks, axis=0).astype(BF16)
    left_high = dot(pick, member_high, ((1,), (0,))).astype(BF16)
    left_low = dot(pick, member_low, ((1,), (0,))).astype(BF16)
    left = jnp.concatenate([left_high[:wide], left_low[:wide]], axis=0)
    left_last = jnp.concatenate([left_high[wide:], left_low[wide:]], axis=0)

    place = iota((wide, 1), 0) % 8
    has_label = stat_by_row(7) > 0.5
    scale_s = jnp.where(has_label, 0.0, 2.0 / stat_by_row(4))
    scale_t = jnp.where(has_label, 0.0, -1.0 / stat_by_row(1))
    scale = jnp.where(place < 2, scale_s, jnp.where(place < 4, scale_t, 0.0))
    in_third = ((place == 4) | (place == 5)).astype(F32)
    scale_s = jnp.where(place >= 6, scale_s, 0.0)
    scale_t = jnp.where(place >= 6, scale_t, 0.0)
    last = dot(left_last, heads_ref[teacher_width + 3 * quarter :, :], ((1,), (1,)))
    correction = jnp.zeros((wide, quarter), F32)
    for j in range(3):
        both = dot(left, heads_ref[teacher_width + j * quarter : teacher_width + (j + 1) * quarter, :], ((1,), (1,)))
        exact = both[:wide] + both[wide:] + last[j * wide : (j + 1) * wide] + last[(3 + j) * wide : (4 + j) * wide]
        sent = exact.astype(BF16).astype(F32)
        residue = exact - sent
        if j < 2:
            correction += residue * (scale_s, scale_t)[j]
        else:
            sent += correction
        scaled = residue * scale
        sent += in_third * (pltpu.roll(scaled, 4, 0) + pltpu.roll(scaled, 2, 0))
        for shard in range(shards):
            out_ref[shard, :, j * quarter : (j + 1) * quarter] = sent[8 * shard : 8 * shard + 8].astype(BF16)
        send_out(j, j * quarter, quarter)
    for copy in copies:
        copy.wait()


def sum_parts(tail):
    shards = tail.shape[0]
    flat = tail.astype(F32).reshape(shards * 8, 128)
    return flat + pltpu.roll(flat, 120, 1) + pltpu.roll(flat, 112, 1)


def fold(flat, lane):
    shards = flat.shape[0] // 8
    stats = [flat[:, lane + k : lane + k + 1].reshape(shards, 8, 1) for k in range(8)]
    top_t = jnp.max(stats[0], axis=0)
    factor_t = jnp.exp(stats[0] - top_t)
    top_s = jnp.max(stats[3], axis=0)
    factor_s = jnp.exp(stats[3] - top_s)
    mass_t = jnp.sum(stats[1] * factor_t, axis=0)
    mass_s = jnp.sum(stats[4] * factor_s, axis=0)
    return stats, top_t, factor_t, mass_t, top_s, factor_s, mass_s


def logit_grad_kernel(tail_ref, teacher_ref, student_ref, target_ref, out_ref):
    flat = sum_parts(tail_ref[...])
    folded = [fold(flat, 32 * group + 32) for group in range(out_ref.shape[0] // 8)]
    top_t, mass_t, top_s, mass_s = [jnp.concatenate([f[i] for f in folded], axis=0) for i in (1, 3, 4, 6)]
    teacher_prob = jnp.exp(teacher_ref[...] - top_t) / mass_t
    student_prob = jnp.exp(student_ref[...] - top_s) / mass_s
    out_ref[...] = (2.0 * student_prob - teacher_prob - target_ref[...]).astype(BF16)


def owner_kernel(arrived_ref, out_ref, loss_ref):
    shards, _, lanes = arrived_ref.shape
    quarter = (lanes - 128) // 3
    stats, top_t, factor_t, mass_t, top_s, factor_s, mass_s = fold(sum_parts(arrived_ref[:, :, 3 * quarter :]), 0)
    cross = jnp.sum(stats[2] * factor_t, axis=0)
    picked = jnp.sum(stats[5], axis=0)
    picked_t = jnp.sum(stats[6], axis=0)
    loss = cross / mass_t - top_t - jnp.log(mass_t) + 2.0 * (top_s + jnp.log(mass_s)) - picked
    token = lax.broadcasted_iota(jnp.int32, (8, 1), 0)
    for t in range(out_ref.shape[0]):
        loss_ref[t] = jnp.sum(jnp.where(token == t, loss, 0.0))
    label_grad = 2.0 * (jnp.exp(picked - top_s) / mass_s) - jnp.exp(picked_t - top_t) / mass_t - 1.0
    rounding = label_grad.astype(BF16).astype(F32) - label_grad
    weight_s = factor_s / mass_s
    weight_t = factor_t / mass_t
    share = 0.8 * weight_s * stats[4] + 0.2 * weight_t * stats[1]
    kappa = jnp.where(stats[7] > 2.0, 1.0, 0.0)
    weight_l = jnp.where(stats[7] > 0.5, 1.0 - (1.0 - kappa) * rounding, share)
    weight_s = 2.0 * (weight_s - kappa / stats[4])
    weight_t = kappa / stats[1] - weight_t
    place = lax.broadcasted_iota(jnp.int32, (shards, 8, 1), 1)
    last = jnp.zeros((8, quarter), F32)
    for j, weight_last in enumerate((weight_s, weight_t, weight_l)):
        weight = jnp.where(
            place < 2, weight_s, jnp.where(place < 4, weight_t, jnp.where(place < 6, weight_l, weight_last))
        )
        piece = jnp.zeros((8, quarter), F32)
        for shard in range(shards):
            piece += weight[shard] * arrived_ref[shard, :, j * quarter : (j + 1) * quarter].astype(F32)
        last += piece
        out_ref[:, j * quarter : (j + 1) * quarter] = piece[0:2] + piece[2:4] + piece[4:6]
    out_ref[:, 3 * quarter :] = last[6:8]


def head_grad_kernel(hidden_ref, hidden_other_ref, grad_ref, other_ref, out_ref, total_ref, sems):
    grads = jnp.concatenate([grad_ref[...], other_ref[...]], axis=0)
    size = hidden_ref.shape[1] // PIECES
    copies = []
    for piece in range(PIECES):
        rows = pl.ds(piece * size, size)
        hidden = jnp.concatenate([hidden_ref[:, rows], hidden_other_ref[:, rows]], axis=0)
        total_ref[rows, :] = lax.dot_general(hidden, grads, (((0,), (0,)), ((), ())), preferred_element_type=F32)
        copies.append(pltpu.make_async_copy(total_ref.at[rows, :], out_ref.at[rows, :], sems.at[piece]))
        copies[-1].start()
    for copy in copies:
        copy.wait()


def two_exchanges(teacher_hidden, student_hidden, teacher_head, student_head, labels, *, shards):
    own = labels.shape[0]
    teacher_width, width = teacher_hidden.shape[1], student_hidden.shape[1]
    columns_here = student_head.shape[1]
    tokens = shards * own
    quarter = width // 4
    here = lax.axis_index("vocab").astype(jnp.int32)
    rows = gather_tokens(teacher_hidden, student_hidden, labels, shards)
    student_rows = rows[:, :, teacher_width : teacher_width + width].reshape(tokens, width)
    other = [(0, 1), (1, 0)]
    student_other = lax.ppermute(student_rows, "rows", other)

    square = jax.ShapeDtypeStruct((tokens, columns_here), F32)
    payload, teacher_logits, student_logits, target = pl.pallas_call(
        raw_partial_kernel,
        out_shape=(jax.ShapeDtypeStruct((shards, 8, 3 * quarter + 128), BF16), square, square, square),
        in_specs=[SMEM, VMEM, VMEM],
        out_specs=(ANY, VMEM, VMEM, VMEM),
        scratch_shapes=[pltpu.VMEM((shards, 8, 3 * quarter + 128), BF16), pltpu.SemaphoreType.DMA((4,))],
        compiler_params=SMALL,
    )((here * columns_here)[None], rows, jnp.concatenate([teacher_head, student_head], axis=0))
    arrived = swap(payload)
    grad_rows = pl.pallas_call(
        logit_grad_kernel,
        out_shape=jax.ShapeDtypeStruct((tokens, columns_here), BF16),
        in_specs=[VMEM] * 4,
        out_specs=VMEM,
        compiler_params=SMALL,
    )(arrived[:, :, 3 * quarter :], teacher_logits, student_logits, target)
    grad_other = lax.ppermute(grad_rows, "rows", other)
    hidden_grad, token_loss = pl.pallas_call(
        owner_kernel,
        out_shape=(jax.ShapeDtypeStruct((own, width), F32), jax.ShapeDtypeStruct((own,), F32)),
        in_specs=[VMEM],
        out_specs=(VMEM, SMEM),
        compiler_params=SMALL,
    )(arrived)
    head_grad = pl.pallas_call(
        head_grad_kernel,
        out_shape=jax.ShapeDtypeStruct((width, columns_here), F32),
        in_specs=[VMEM] * 4,
        out_specs=ANY,
        scratch_shapes=[pltpu.VMEM((width, columns_here), F32), pltpu.SemaphoreType.DMA((PIECES,))],
        compiler_params=SMALL,
    )(student_rows, student_other, grad_rows, grad_other)
    return (token_loss, hidden_grad, head_grad)


def three_exchanges(teacher_hidden, student_hidden, teacher_head, student_head, labels, *, shards):
    own = labels.shape[0]
    student_width = student_hidden.shape[1]
    columns_here = student_head.shape[1]
    first_column = lax.axis_index("vocab") * columns_here
    rows = gather_tokens(teacher_hidden, student_hidden, labels, shards).reshape(shards * own, -1)
    teacher_width = teacher_hidden.shape[1]
    teacher_rows = rows[:, :teacher_width]
    student_rows = rows[:, teacher_width : teacher_width + student_width]
    code = rows[:, teacher_width + student_width :].astype(jnp.int32)
    label_rows = code[:, 0] * 128 + code[:, 1]
    other = [(0, 1), (1, 0)]
    student_other = lax.ppermute(student_rows, "rows", other)

    teacher_logits = jnp.dot(teacher_rows, teacher_head, preferred_element_type=F32)
    student_logits = jnp.dot(student_rows, student_head, preferred_element_type=F32)
    columns = lax.broadcasted_iota(jnp.int32, student_logits.shape, 1)
    target = (label_rows - first_column)[:, None] == columns
    top_t = jnp.max(teacher_logits, axis=1, keepdims=True)
    exp_t = jnp.exp(teacher_logits - top_t)
    top_s = jnp.max(student_logits, axis=1, keepdims=True)
    exp_s = jnp.exp(student_logits - top_s)
    stats = jnp.concatenate(
        [
            top_t,
            jnp.sum(exp_t, axis=1, keepdims=True),
            jnp.sum(exp_t * (teacher_logits - student_logits), axis=1, keepdims=True),
            top_s,
            jnp.sum(exp_s, axis=1, keepdims=True),
            jnp.sum(jnp.where(target, student_logits, 0.0), axis=1, keepdims=True),
        ],
        axis=1,
    )
    every = swap(jnp.broadcast_to(stats[None], (shards,) + stats.shape))
    all_top_t = jnp.max(every[:, :, 0], axis=0)
    factor_t = jnp.exp(every[:, :, 0] - all_top_t[None])
    all_top_s = jnp.max(every[:, :, 3], axis=0)
    factor_s = jnp.exp(every[:, :, 3] - all_top_s[None])
    mass_t = jnp.sum(every[:, :, 1] * factor_t, axis=0)
    cross = jnp.sum(every[:, :, 2] * factor_t, axis=0)
    mass_s = jnp.sum(every[:, :, 4] * factor_s, axis=0)
    picked = jnp.sum(every[:, :, 5], axis=0)
    loss = cross / mass_t - all_top_t - jnp.log(mass_t) + 2.0 * (all_top_s + jnp.log(mass_s)) - picked
    token_loss = lax.dynamic_slice_in_dim(loss, lax.axis_index("vocab") * own, own, 0)

    teacher_prob = jnp.exp(teacher_logits - all_top_t[:, None]) / mass_t[:, None]
    student_prob = jnp.exp(student_logits - all_top_s[:, None]) / mass_s[:, None]
    grad_rows = (2.0 * student_prob - teacher_prob - target.astype(F32)).astype(BF16)
    grad_other = lax.ppermute(grad_rows, "rows", other)
    partial = lax.dot_general(grad_rows, student_head, (((1,), (1,)), ((), ())), preferred_element_type=F32)
    arrived = swap(partial.astype(BF16).reshape(shards, own, student_width))
    hidden_grad = jnp.sum(arrived.astype(F32), axis=0)
    head_grad = lax.dot_general(
        jnp.concatenate([student_rows, student_other], axis=0),
        jnp.concatenate([grad_rows, grad_other], axis=0),
        (((0,), (0,)), ((), ())),
        preferred_element_type=F32,
    )
    return (token_loss, hidden_grad, head_grad)


def solution(mesh):
    tokens = ("groups", "vocab", "rows")
    in_specs = (P(tokens, None), P(tokens, None), P(None, "vocab"), P(None, "vocab"), P(tokens))
    out_specs = (P(tokens), P(tokens, None), P("groups", "vocab"))

    def body(*arrays):
        shards = mesh.shape["vocab"]
        own = arrays[4].shape[0]
        small = own == 2 and shards % 4 == 0 and shards * own <= 24
        return (two_exchanges if small else three_exchanges)(*arrays, shards=shards)

    return jax.shard_map(body, mesh=mesh, in_specs=in_specs, out_specs=out_specs, check_vma=False)
```

```python
import jax
import jax.numpy as jnp
from jax import lax
from jax.experimental import pallas as pl
from jax.experimental.pallas import tpu as pltpu
from jax.sharding import PartitionSpec as P

F32 = jnp.float32
BF16 = jnp.bfloat16
CODE = 128


UNROLL = 16
PIECES = 7
SMEM = pl.BlockSpec(memory_space=pltpu.SMEM)
VMEM = pl.BlockSpec(memory_space=pltpu.VMEM)
ANY = pl.BlockSpec(memory_space=pl.ANY)
SMALL = pltpu.CompilerParams(vmem_limit_bytes=16 * 1024 * 1024)


def over_shards(shards, body):
    if shards <= UNROLL:
        for shard in range(shards):
            body(shard)
    else:
        pl.loop(0, shards)(body)


def swap(blocks):
    return lax.all_to_all(blocks, "vocab", split_axis=0, concat_axis=0, tiled=True)


def payload_kernel(labels_ref, teacher_ref, student_ref, out_ref):
    shards, own, _ = out_ref.shape
    teacher_width, student_width = teacher_ref.shape[1], student_ref.shape[1]
    teacher = teacher_ref[...]
    student = student_ref[...]
    code = label_digits(labels_ref, own)

    def write(shard):
        out_ref[shard, :, :teacher_width] = teacher
        out_ref[shard, :, teacher_width : teacher_width + student_width] = student
        out_ref[shard, :, teacher_width + student_width :] = code

    over_shards(shards, write)


def label_digits(labels_ref, own):
    row = lax.broadcasted_iota(jnp.int32, (own, CODE), 0)
    lane = lax.broadcasted_iota(jnp.int32, (own, CODE), 1)
    digits = jnp.zeros((own, CODE), jnp.int32)
    for token in range(own):
        label = labels_ref[token]
        pair = jnp.where(lane == 0, label >> 7, label & 127)
        digits = jnp.where(row == token, pair, digits)
    return digits.astype(F32).astype(BF16)


def gather_tokens(teacher_hidden, student_hidden, labels, shards):
    own, teacher_width = teacher_hidden.shape
    student_width = student_hidden.shape[1]
    payload = pl.pallas_call(
        payload_kernel,
        out_shape=jax.ShapeDtypeStruct((shards, own, teacher_width + student_width + CODE), BF16),
        in_specs=[SMEM, VMEM, VMEM],
        out_specs=VMEM,
    )(labels, teacher_hidden, student_hidden)
    return swap(payload)


def raw_partial_kernel(
    first_ref, rows_ref, heads_ref, out_hbm, teacher_ref, student_ref, target_ref, out_ref, sems
):
    shards, own, _ = rows_ref.shape
    tokens = shards * own
    wide = 8 * shards
    columns = heads_ref.shape[1]
    quarter = (out_ref.shape[2] - 128) // 3
    width = 4 * quarter
    teacher_width = heads_ref.shape[0] - width

    def iota(shape, dim):
        return lax.broadcasted_iota(jnp.int32, shape, dim)

    def dot(left, right, dims):
        return lax.dot_general(left, right, (dims, ((), ())), preferred_element_type=F32)

    copies = []

    def send_out(piece, start, size):
        lanes = pl.ds(start, size)
        copies.append(pltpu.make_async_copy(out_ref.at[:, :, lanes], out_hbm.at[:, :, lanes], sems.at[piece]))
        copies[-1].start()

    def rows_of(start, size):
        return jnp.concatenate([rows_ref[shard, :, start : start + size] for shard in range(shards)], axis=0)

    student = dot(rows_of(teacher_width, width), heads_ref[teacher_width:, :], ((1,), (0,)))
    teacher = dot(rows_of(0, teacher_width), heads_ref[:teacher_width, :], ((1,), (0,)))
    code = rows_of(teacher_width + width, CODE).astype(F32)
    lane = iota(code.shape, 1)
    label = jnp.sum(jnp.where(lane == 0, code * 128.0, jnp.where(lane == 1, code, 0.0)), axis=1, keepdims=True)
    target = (label.astype(jnp.int32) - first_ref[0] == iota((tokens, columns), 1)).astype(F32)
    teacher_ref[...] = teacher
    student_ref[...] = student
    target_ref[...] = target

    def total(array):
        return jnp.sum(array, axis=1, keepdims=True)

    top_t = jnp.max(teacher, axis=1, keepdims=True)
    top_s = jnp.max(student, axis=1, keepdims=True)
    exp_t = jnp.exp(teacher - top_t)
    exp_s = jnp.exp(student - top_s)
    mass_t, mass_s = total(exp_t), total(exp_s)
    combined = exp_s * (2.0 / mass_s) - exp_t / mass_t
    kappa = (total(target * combined) > 0.5).astype(F32)
    stats = [
        top_t,
        mass_t,
        total(exp_t * (teacher - student)),
        top_s,
        mass_s,
        total(target * student),
        total(target * teacher),
        2.0 * kappa + total(target),
    ]
    lane = iota((tokens, 128), 1)
    table = jnp.zeros((tokens, 128), F32)
    for k, stat in enumerate(stats):
        table = jnp.where(lane % 8 == k, stat, table)
    first = table.astype(BF16).astype(F32)
    second = (table - first).astype(BF16).astype(F32)
    part = (lane % 32) // 8
    parts = jnp.where(
        part == 0, first, jnp.where(part == 1, second, jnp.where(part == 2, table - first - second, 0.0))
    ).astype(BF16)

    row, column = iota((wide, tokens), 0), iota((wide, tokens), 1)
    of_token = (column == (row // 8) * 2 + row % 2).astype(F32).astype(BF16)
    by_row = dot(of_token, parts, ((1,), (0,)))

    def stat_by_row(k):
        picked = by_row[:, k : k + 1] + by_row[:, 8 + k : 9 + k] + by_row[:, 16 + k : 17 + k]
        return picked

    lane = iota((8, 128), 1)
    shared = jnp.zeros((8, 128), F32)
    wide_parts = parts.astype(F32)
    for group in range(tokens // 8):
        shared = jnp.where(lane // 32 == group + 1, wide_parts[8 * group : 8 * group + 8], shared)
    for shard in range(shards):
        block = jnp.where(lane < 32, by_row[8 * shard : 8 * shard + 8], shared)
        out_ref[shard, :, 3 * quarter :] = block.astype(BF16)
    send_out(3, 3 * quarter, 128)

    members = jnp.concatenate([exp_s, exp_t, kappa * combined * total(target) - target], axis=0)
    member_high = members.astype(BF16)
    member_low = (members - member_high.astype(F32)).astype(BF16)
    row, column = iota((wide, 3 * tokens), 0), iota((wide, 3 * tokens), 1)
    place = row % 8
    token = (row // 8) * 2 + row % 2
    picks = [((place < 6) & (column == (place // 2) * tokens + token)).astype(F32)]
    for j in range(3):
        picks.append(((place >= 6) & (column == j * tokens + token)).astype(F32))
    pick = jnp.concatenate(picks, axis=0).astype(BF16)
    left_high = dot(pick, member_high, ((1,), (0,))).astype(BF16)
    left_low = dot(pick, member_low, ((1,), (0,))).astype(BF16)
    left = jnp.concatenate([left_high[:wide], left_low[:wide]], axis=0)
    left_last = jnp.concatenate([left_high[wide:], left_low[wide:]], axis=0)

    place = iota((wide, 1), 0) % 8
    has_label = stat_by_row(7) > 0.5
    scale_s = jnp.where(has_label, 0.0, 2.0 / stat_by_row(4))
    scale_t = jnp.where(has_label, 0.0, -1.0 / stat_by_row(1))
    scale = jnp.where(place < 2, scale_s, jnp.where(place < 4, scale_t, 0.0))
    in_third = ((place == 4) | (place == 5)).astype(F32)
    scale_s = jnp.where(place >= 6, scale_s, 0.0)
    scale_t = jnp.where(place >= 6, scale_t, 0.0)
    last = dot(left_last, heads_ref[teacher_width + 3 * quarter :, :], ((1,), (1,)))
    correction = jnp.zeros((wide, quarter), F32)
    for j in range(3):
        both = dot(left, heads_ref[teacher_width + j * quarter : teacher_width + (j + 1) * quarter, :], ((1,), (1,)))
        exact = both[:wide] + both[wide:] + last[j * wide : (j + 1) * wide] + last[(3 + j) * wide : (4 + j) * wide]
        sent = exact.astype(BF16).astype(F32)
        residue = exact - sent
        if j < 2:
            correction += residue * (scale_s, scale_t)[j]
        else:
            sent += correction
        scaled = residue * scale
        sent += in_third * (pltpu.roll(scaled, 4, 0) + pltpu.roll(scaled, 2, 0))
        for shard in range(shards):
            out_ref[shard, :, j * quarter : (j + 1) * quarter] = sent[8 * shard : 8 * shard + 8].astype(BF16)
        send_out(j, j * quarter, quarter)
    for copy in copies:
        copy.wait()


def sum_parts(tail):
    shards = tail.shape[0]
    flat = tail.astype(F32).reshape(shards * 8, 128)
    return flat + pltpu.roll(flat, 120, 1) + pltpu.roll(flat, 112, 1)


def fold(flat, lane):
    shards = flat.shape[0] // 8
    stats = [flat[:, lane + k : lane + k + 1].reshape(shards, 8, 1) for k in range(8)]
    top_t = jnp.max(stats[0], axis=0)
    factor_t = jnp.exp(stats[0] - top_t)
    top_s = jnp.max(stats[3], axis=0)
    factor_s = jnp.exp(stats[3] - top_s)
    mass_t = jnp.sum(stats[1] * factor_t, axis=0)
    mass_s = jnp.sum(stats[4] * factor_s, axis=0)
    return stats, top_t, factor_t, mass_t, top_s, factor_s, mass_s


def logit_grad_kernel(tail_ref, teacher_ref, student_ref, target_ref, out_ref):
    flat = sum_parts(tail_ref[...])
    folded = [fold(flat, 32 * group + 32) for group in range(out_ref.shape[0] // 8)]
    top_t, mass_t, top_s, mass_s = [jnp.concatenate([f[i] for f in folded], axis=0) for i in (1, 3, 4, 6)]
    teacher_prob = jnp.exp(teacher_ref[...] - top_t) / mass_t
    student_prob = jnp.exp(student_ref[...] - top_s) / mass_s
    out_ref[...] = (2.0 * student_prob - teacher_prob - target_ref[...]).astype(BF16)


def owner_kernel(arrived_ref, out_ref, loss_ref):
    shards, _, lanes = arrived_ref.shape
    quarter = (lanes - 128) // 3
    stats, top_t, factor_t, mass_t, top_s, factor_s, mass_s = fold(sum_parts(arrived_ref[:, :, 3 * quarter :]), 0)
    cross = jnp.sum(stats[2] * factor_t, axis=0)
    picked = jnp.sum(stats[5], axis=0)
    picked_t = jnp.sum(stats[6], axis=0)
    loss = cross / mass_t - top_t - jnp.log(mass_t) + 2.0 * (top_s + jnp.log(mass_s)) - picked
    token = lax.broadcasted_iota(jnp.int32, (8, 1), 0)
    for t in range(out_ref.shape[0]):
        loss_ref[t] = jnp.sum(jnp.where(token == t, loss, 0.0))
    label_grad = 2.0 * (jnp.exp(picked - top_s) / mass_s) - jnp.exp(picked_t - top_t) / mass_t - 1.0
    rounding = label_grad.astype(BF16).astype(F32) - label_grad
    weight_s = factor_s / mass_s
    weight_t = factor_t / mass_t
    share = 0.8 * weight_s * stats[4] + 0.2 * weight_t * stats[1]
    kappa = jnp.where(stats[7] > 2.0, 1.0, 0.0)
    weight_l = jnp.where(stats[7] > 0.5, 1.0 - (1.0 - kappa) * rounding, share)
    weight_s = 2.0 * (weight_s - kappa / stats[4])
    weight_t = kappa / stats[1] - weight_t
    place = lax.broadcasted_iota(jnp.int32, (shards, 8, 1), 1)
    last = jnp.zeros((8, quarter), F32)
    for j, weight_last in enumerate((weight_s, weight_t, weight_l)):
        weight = jnp.where(
            place < 2, weight_s, jnp.where(place < 4, weight_t, jnp.where(place < 6, weight_l, weight_last))
        )
        piece = jnp.zeros((8, quarter), F32)
        for shard in range(shards):
            piece += weight[shard] * arrived_ref[shard, :, j * quarter : (j + 1) * quarter].astype(F32)
        last += piece
        out_ref[:, j * quarter : (j + 1) * quarter] = piece[0:2] + piece[2:4] + piece[4:6]
    out_ref[:, 3 * quarter :] = last[6:8]


def head_grad_kernel(hidden_ref, hidden_other_ref, grad_ref, other_ref, out_ref, total_ref, sems):
    grads = jnp.concatenate([grad_ref[...], other_ref[...]], axis=0)
    size = hidden_ref.shape[1] // PIECES
    copies = []
    for piece in range(PIECES):
        rows = pl.ds(piece * size, size)
        hidden = jnp.concatenate([hidden_ref[:, rows], hidden_other_ref[:, rows]], axis=0)
        total_ref[rows, :] = lax.dot_general(hidden, grads, (((0,), (0,)), ((), ())), preferred_element_type=F32)
        copies.append(pltpu.make_async_copy(total_ref.at[rows, :], out_ref.at[rows, :], sems.at[piece]))
        copies[-1].start()
    for copy in copies:
        copy.wait()


def two_exchanges(teacher_hidden, student_hidden, teacher_head, student_head, labels, *, shards):
    own = labels.shape[0]
    teacher_width, width = teacher_hidden.shape[1], student_hidden.shape[1]
    columns_here = student_head.shape[1]
    tokens = shards * own
    quarter = width // 4
    here = lax.axis_index("vocab").astype(jnp.int32)
    rows = gather_tokens(teacher_hidden, student_hidden, labels, shards)
    student_rows = rows[:, :, teacher_width : teacher_width + width].reshape(tokens, width)
    other = [(0, 1), (1, 0)]
    student_other = lax.ppermute(student_rows, "rows", other)

    square = jax.ShapeDtypeStruct((tokens, columns_here), F32)
    payload, teacher_logits, student_logits, target = pl.pallas_call(
        raw_partial_kernel,
        out_shape=(jax.ShapeDtypeStruct((shards, 8, 3 * quarter + 128), BF16), square, square, square),
        in_specs=[SMEM, VMEM, VMEM],
        out_specs=(ANY, VMEM, VMEM, VMEM),
        scratch_shapes=[pltpu.VMEM((shards, 8, 3 * quarter + 128), BF16), pltpu.SemaphoreType.DMA((4,))],
        compiler_params=SMALL,
    )((here * columns_here)[None], rows, jnp.concatenate([teacher_head, student_head], axis=0))
    arrived = swap(payload)
    grad_rows = pl.pallas_call(
        logit_grad_kernel,
        out_shape=jax.ShapeDtypeStruct((tokens, columns_here), BF16),
        in_specs=[VMEM] * 4,
        out_specs=VMEM,
        compiler_params=SMALL,
    )(arrived[:, :, 3 * quarter :], teacher_logits, student_logits, target)
    grad_other = lax.ppermute(grad_rows, "rows", other)
    hidden_grad, token_loss = pl.pallas_call(
        owner_kernel,
        out_shape=(jax.ShapeDtypeStruct((own, width), F32), jax.ShapeDtypeStruct((own,), F32)),
        in_specs=[VMEM],
        out_specs=(VMEM, SMEM),
        compiler_params=SMALL,
    )(arrived)
    head_grad = pl.pallas_call(
        head_grad_kernel,
        out_shape=jax.ShapeDtypeStruct((width, columns_here), F32),
        in_specs=[VMEM] * 4,
        out_specs=ANY,
        scratch_shapes=[pltpu.VMEM((width, columns_here), F32), pltpu.SemaphoreType.DMA((PIECES,))],
        compiler_params=SMALL,
    )(student_rows, student_other, grad_rows, grad_other)
    return (token_loss, hidden_grad, head_grad)


def three_exchanges(teacher_hidden, student_hidden, teacher_head, student_head, labels, *, shards):
    own = labels.shape[0]
    student_width = student_hidden.shape[1]
    columns_here = student_head.shape[1]
    first_column = lax.axis_index("vocab") * columns_here
    rows = gather_tokens(teacher_hidden, student_hidden, labels, shards).reshape(shards * own, -1)
    teacher_width = teacher_hidden.shape[1]
    teacher_rows = rows[:, :teacher_width]
    student_rows = rows[:, teacher_width : teacher_width + student_width]
    code = rows[:, teacher_width + student_width :].astype(jnp.int32)
    label_rows = code[:, 0] * 128 + code[:, 1]
    other = [(0, 1), (1, 0)]
    student_other = lax.ppermute(student_rows, "rows", other)

    teacher_logits = jnp.dot(teacher_rows, teacher_head, preferred_element_type=F32)
    student_logits = jnp.dot(student_rows, student_head, preferred_element_type=F32)
    columns = lax.broadcasted_iota(jnp.int32, student_logits.shape, 1)
    target = (label_rows - first_column)[:, None] == columns
    top_t = jnp.max(teacher_logits, axis=1, keepdims=True)
    exp_t = jnp.exp(teacher_logits - top_t)
    top_s = jnp.max(student_logits, axis=1, keepdims=True)
    exp_s = jnp.exp(student_logits - top_s)
    stats = jnp.concatenate(
        [
            top_t,
            jnp.sum(exp_t, axis=1, keepdims=True),
            jnp.sum(exp_t * (teacher_logits - student_logits), axis=1, keepdims=True),
            top_s,
            jnp.sum(exp_s, axis=1, keepdims=True),
            jnp.sum(jnp.where(target, student_logits, 0.0), axis=1, keepdims=True),
        ],
        axis=1,
    )
    every = swap(jnp.broadcast_to(stats[None], (shards,) + stats.shape))
    all_top_t = jnp.max(every[:, :, 0], axis=0)
    factor_t = jnp.exp(every[:, :, 0] - all_top_t[None])
    all_top_s = jnp.max(every[:, :, 3], axis=0)
    factor_s = jnp.exp(every[:, :, 3] - all_top_s[None])
    mass_t = jnp.sum(every[:, :, 1] * factor_t, axis=0)
    cross = jnp.sum(every[:, :, 2] * factor_t, axis=0)
    mass_s = jnp.sum(every[:, :, 4] * factor_s, axis=0)
    picked = jnp.sum(every[:, :, 5], axis=0)
    loss = cross / mass_t - all_top_t - jnp.log(mass_t) + 2.0 * (all_top_s + jnp.log(mass_s)) - picked
    token_loss = lax.dynamic_slice_in_dim(loss, lax.axis_index("vocab") * own, own, 0)

    teacher_prob = jnp.exp(teacher_logits - all_top_t[:, None]) / mass_t[:, None]
    student_prob = jnp.exp(student_logits - all_top_s[:, None]) / mass_s[:, None]
    grad_rows = (2.0 * student_prob - teacher_prob - target.astype(F32)).astype(BF16)
    grad_other = lax.ppermute(grad_rows, "rows", other)
    partial = lax.dot_general(grad_rows, student_head, (((1,), (1,)), ((), ())), preferred_element_type=F32)
    arrived = swap(partial.astype(BF16).reshape(shards, own, student_width))
    hidden_grad = jnp.sum(arrived.astype(F32), axis=0)
    head_grad = lax.dot_general(
        jnp.concatenate([student_rows, student_other], axis=0),
        jnp.concatenate([grad_rows, grad_other], axis=0),
        (((0,), (0,)), ((), ())),
        preferred_element_type=F32,
    )
    return (token_loss, hidden_grad, head_grad)


def solution(mesh):
    tokens = ("groups", "vocab", "rows")
    in_specs = (P(tokens, None), P(tokens, None), P(None, "vocab"), P(None, "vocab"), P(tokens))
    out_specs = (P(tokens), P(tokens, None), P("groups", "vocab"))

    def body(*arrays):
        shards = mesh.shape["vocab"]
        own = arrays[4].shape[0]
        small = own == 2 and shards % 4 == 0 and shards * own <= 24
        return (two_exchanges if small else three_exchanges)(*arrays, shards=shards)

    return jax.shard_map(body, mesh=mesh, in_specs=in_specs, out_specs=out_specs, check_vma=False)
```

```python
import jax
import jax.numpy as jnp
from jax import lax
from jax.experimental import pallas as pl
from jax.experimental.pallas import tpu as pltpu
from jax.sharding import PartitionSpec as P

F32 = jnp.float32
BF16 = jnp.bfloat16
CODE = 128


UNROLL = 16
PIECES = 7
SMEM = pl.BlockSpec(memory_space=pltpu.SMEM)
VMEM = pl.BlockSpec(memory_space=pltpu.VMEM)
ANY = pl.BlockSpec(memory_space=pl.ANY)
SMALL = pltpu.CompilerParams(vmem_limit_bytes=16 * 1024 * 1024)


def over_shards(shards, body):
    if shards <= UNROLL:
        for shard in range(shards):
            body(shard)
    else:
        pl.loop(0, shards)(body)


def swap(blocks):
    return lax.all_to_all(blocks, "vocab", split_axis=0, concat_axis=0, tiled=True)


def payload_kernel(labels_ref, teacher_ref, student_ref, out_ref):
    shards, own, _ = out_ref.shape
    teacher_width, student_width = teacher_ref.shape[1], student_ref.shape[1]
    teacher = teacher_ref[...]
    student = student_ref[...]
    code = label_digits(labels_ref, own)

    def write(shard):
        out_ref[shard, :, :teacher_width] = teacher
        out_ref[shard, :, teacher_width : teacher_width + student_width] = student
        out_ref[shard, :, teacher_width + student_width :] = code

    over_shards(shards, write)


def label_digits(labels_ref, own):
    row = lax.broadcasted_iota(jnp.int32, (own, CODE), 0)
    lane = lax.broadcasted_iota(jnp.int32, (own, CODE), 1)
    digits = jnp.zeros((own, CODE), jnp.int32)
    for token in range(own):
        label = labels_ref[token]
        pair = jnp.where(lane == 0, label >> 7, label & 127)
        digits = jnp.where(row == token, pair, digits)
    return digits.astype(F32).astype(BF16)


def gather_tokens(teacher_hidden, student_hidden, labels, shards):
    own, teacher_width = teacher_hidden.shape
    student_width = student_hidden.shape[1]
    payload = pl.pallas_call(
        payload_kernel,
        out_shape=jax.ShapeDtypeStruct((shards, own, teacher_width + student_width + CODE), BF16),
        in_specs=[SMEM, VMEM, VMEM],
        out_specs=VMEM,
    )(labels, teacher_hidden, student_hidden)
    return swap(payload)


def raw_partial_kernel(
    first_ref, rows_ref, heads_ref, out_hbm, teacher_ref, student_ref, target_ref, out_ref, sems
):
    tokens = rows_ref.shape[0]
    shards = out_ref.shape[0]
    wide = 8 * shards
    columns = heads_ref.shape[1]
    quarter = (out_ref.shape[2] - 128) // 3
    width = 4 * quarter
    teacher_width = heads_ref.shape[0] - width

    def iota(shape, dim):
        return lax.broadcasted_iota(jnp.int32, shape, dim)

    def dot(left, right, dims):
        return lax.dot_general(left, right, (dims, ((), ())), preferred_element_type=F32)

    copies = []

    def send_out(piece, start, size):
        lanes = pl.ds(start, size)
        copies.append(pltpu.make_async_copy(out_ref.at[:, :, lanes], out_hbm.at[:, :, lanes], sems.at[piece]))
        copies[-1].start()

    student = dot(rows_ref[:, teacher_width : teacher_width + width], heads_ref[teacher_width:, :], ((1,), (0,)))
    teacher = dot(rows_ref[:, :teacher_width], heads_ref[:teacher_width, :], ((1,), (0,)))
    code = rows_ref[:, teacher_width + width :].astype(F32)
    lane = iota(code.shape, 1)
    label = jnp.sum(jnp.where(lane == 0, code * 128.0, jnp.where(lane == 1, code, 0.0)), axis=1, keepdims=True)
    target = (label.astype(jnp.int32) - first_ref[0] == iota((tokens, columns), 1)).astype(F32)
    teacher_ref[...] = teacher
    student_ref[...] = student
    target_ref[...] = target

    def total(array):
        return jnp.sum(array, axis=1, keepdims=True)

    top_t = jnp.max(teacher, axis=1, keepdims=True)
    top_s = jnp.max(student, axis=1, keepdims=True)
    exp_t = jnp.exp(teacher - top_t)
    exp_s = jnp.exp(student - top_s)
    mass_t, mass_s = total(exp_t), total(exp_s)
    combined = exp_s * (2.0 / mass_s) - exp_t / mass_t
    confidence = total(target * (exp_s * (2.0 / mass_s) + exp_t / mass_t))
    kappa = (confidence > 0.75).astype(F32)
    stats = [
        top_t,
        mass_t,
        total(exp_t * (teacher - student)),
        top_s,
        mass_s,
        total(target * student),
        total(target * teacher),
        2.0 * kappa + total(target),
    ]
    lane = iota((tokens, 128), 1)
    table = jnp.zeros((tokens, 128), F32)
    for k, stat in enumerate(stats):
        table = jnp.where(lane % 8 == k, stat, table)
    first = table.astype(BF16).astype(F32)
    second = (table - first).astype(BF16).astype(F32)
    part = (lane % 32) // 8
    parts = jnp.where(
        part == 0, first, jnp.where(part == 1, second, jnp.where(part == 2, table - first - second, 0.0))
    ).astype(BF16)

    row, column = iota((wide, tokens), 0), iota((wide, tokens), 1)
    of_token = (column == (row // 8) * 2 + row % 2).astype(F32).astype(BF16)
    by_row = dot(of_token, parts, ((1,), (0,)))

    def stat_by_row(k):
        picked = by_row[:, k : k + 1] + by_row[:, 8 + k : 9 + k] + by_row[:, 16 + k : 17 + k]
        return picked

    lane = iota((8, 128), 1)
    shared = jnp.zeros((8, 128), F32)
    wide_parts = parts.astype(F32)
    for group in range(tokens // 8):
        shared = jnp.where(lane // 32 == group + 1, wide_parts[8 * group : 8 * group + 8], shared)
    for shard in range(shards):
        block = jnp.where(lane < 32, by_row[8 * shard : 8 * shard + 8], shared)
        out_ref[shard, :, 3 * quarter :] = block.astype(BF16)
    send_out(3, 3 * quarter, 128)

    members = jnp.concatenate([exp_s, exp_t, kappa * combined * total(target) - target], axis=0)
    member_high = members.astype(BF16)
    member_low = (members - member_high.astype(F32)).astype(BF16)
    row, column = iota((wide, 3 * tokens), 0), iota((wide, 3 * tokens), 1)
    place = row % 8
    token = (row // 8) * 2 + row % 2
    pick = ((place < 6) & (column == (place // 2) * tokens + token)).astype(F32).astype(BF16)
    left = dot(pick, jnp.concatenate([member_high, member_low], axis=1), ((1,), (0,))).astype(BF16)
    left = jnp.concatenate([left[:, :columns], left[:, columns:]], axis=0)

    def partials(start):
        both = dot(left, heads_ref[teacher_width + start : teacher_width + start + quarter, :], ((1,), (1,)))
        return both[:wide] + both[wide:]

    place = iota((wide, 1), 0) % 8
    has_label = stat_by_row(7) > 0.5
    scale_s = jnp.where(has_label, 0.0, 2.0 / stat_by_row(4))
    scale_t = jnp.where(has_label, 0.0, -1.0 / stat_by_row(1))
    scale = jnp.where(place < 2, scale_s, jnp.where(place < 4, scale_t, 0.0))
    in_third = ((place == 4) | (place == 5)).astype(F32)
    scale_s = jnp.where(place >= 6, scale_s, 0.0)
    scale_t = jnp.where(place >= 6, scale_t, 0.0)
    last = partials(3 * quarter)
    correction = jnp.zeros((wide, quarter), F32)
    for j in range(3):
        exact = partials(j * quarter) + jnp.where(place >= 6, pltpu.roll(last, 6 - 2 * j, 0), 0.0)
        sent = exact.astype(BF16).astype(F32)
        residue = exact - sent
        if j < 2:
            correction += residue * (scale_s, scale_t)[j]
        else:
            sent += correction
        scaled = residue * scale
        sent += in_third * (pltpu.roll(scaled, 4, 0) + pltpu.roll(scaled, 2, 0))
        for shard in range(shards):
            out_ref[shard, :, j * quarter : (j + 1) * quarter] = sent[8 * shard : 8 * shard + 8].astype(BF16)
        send_out(j, j * quarter, quarter)
    for copy in copies:
        copy.wait()


def sum_parts(tail):
    shards = tail.shape[0]
    flat = tail.astype(F32).reshape(shards * 8, 128)
    return flat + pltpu.roll(flat, 120, 1) + pltpu.roll(flat, 112, 1)


def fold(flat, lane):
    shards = flat.shape[0] // 8
    stats = [flat[:, lane + k : lane + k + 1].reshape(shards, 8, 1) for k in range(8)]
    top_t = jnp.max(stats[0], axis=0)
    factor_t = jnp.exp(stats[0] - top_t)
    top_s = jnp.max(stats[3], axis=0)
    factor_s = jnp.exp(stats[3] - top_s)
    mass_t = jnp.sum(stats[1] * factor_t, axis=0)
    mass_s = jnp.sum(stats[4] * factor_s, axis=0)
    return stats, top_t, factor_t, mass_t, top_s, factor_s, mass_s


def logit_grad_kernel(tail_ref, teacher_ref, student_ref, target_ref, out_ref):
    flat = sum_parts(tail_ref[...])
    folded = [fold(flat, 32 * group + 32) for group in range(out_ref.shape[0] // 8)]
    top_t, mass_t, top_s, mass_s = [jnp.concatenate([f[i] for f in folded], axis=0) for i in (1, 3, 4, 6)]
    teacher_prob = jnp.exp(teacher_ref[...] - top_t) / mass_t
    student_prob = jnp.exp(student_ref[...] - top_s) / mass_s
    out_ref[...] = (2.0 * student_prob - teacher_prob - target_ref[...]).astype(BF16)


def owner_kernel(arrived_ref, out_ref, loss_ref):
    shards, _, lanes = arrived_ref.shape
    quarter = (lanes - 128) // 3
    stats, top_t, factor_t, mass_t, top_s, factor_s, mass_s = fold(sum_parts(arrived_ref[:, :, 3 * quarter :]), 0)
    cross = jnp.sum(stats[2] * factor_t, axis=0)
    picked = jnp.sum(stats[5], axis=0)
    picked_t = jnp.sum(stats[6], axis=0)
    loss = cross / mass_t - top_t - jnp.log(mass_t) + 2.0 * (top_s + jnp.log(mass_s)) - picked
    token = lax.broadcasted_iota(jnp.int32, (8, 1), 0)
    for t in range(out_ref.shape[0]):
        loss_ref[t] = jnp.sum(jnp.where(token == t, loss, 0.0))
    label_grad = 2.0 * (jnp.exp(picked - top_s) / mass_s) - jnp.exp(picked_t - top_t) / mass_t - 1.0
    rounding = label_grad.astype(BF16).astype(F32) - label_grad
    weight_s = factor_s / mass_s
    weight_t = factor_t / mass_t
    share = 0.8 * weight_s * stats[4] + 0.2 * weight_t * stats[1]
    kappa = jnp.where(stats[7] > 2.0, 1.0, 0.0)
    weight_l = jnp.where(stats[7] > 0.5, 1.0 - (1.0 - kappa) * rounding, share)
    weight_s = 2.0 * (weight_s - kappa / stats[4])
    weight_t = kappa / stats[1] - weight_t
    place = lax.broadcasted_iota(jnp.int32, (shards, 8, 1), 1)
    last = jnp.zeros((8, quarter), F32)
    for j, weight_last in enumerate((weight_s, weight_t, weight_l)):
        weight = jnp.where(
            place < 2, weight_s, jnp.where(place < 4, weight_t, jnp.where(place < 6, weight_l, weight_last))
        )
        piece = jnp.zeros((8, quarter), F32)
        for shard in range(shards):
            piece += weight[shard] * arrived_ref[shard, :, j * quarter : (j + 1) * quarter].astype(F32)
        last += piece
        out_ref[:, j * quarter : (j + 1) * quarter] = piece[0:2] + piece[2:4] + piece[4:6]
    out_ref[:, 3 * quarter :] = last[6:8]


def head_grad_kernel(hidden_ref, hidden_other_ref, grad_ref, other_ref, out_ref, total_ref, sems):
    grads = jnp.concatenate([grad_ref[...], other_ref[...]], axis=0)
    zeros = jnp.zeros_like(grads)
    grads = jnp.concatenate(
        [jnp.concatenate([grads, zeros], axis=1), jnp.concatenate([zeros, grads], axis=1)], axis=0
    )
    half, columns = total_ref.shape[0] // 2, total_ref.shape[1]
    size = half // PIECES
    copies = []
    for piece in range(PIECES):
        places = [pl.ds(side * half + piece * size, size) for side in range(2)]
        hidden = jnp.concatenate([ref[:, rows] for rows in places for ref in (hidden_ref, hidden_other_ref)], axis=0)
        both = lax.dot_general(hidden, grads, (((0,), (0,)), ((), ())), preferred_element_type=F32)
        for side, rows in enumerate(places):
            total_ref[rows, :] = both[:, side * columns : (side + 1) * columns]
            sem = sems.at[2 * piece + side]
            copies.append(pltpu.make_async_copy(total_ref.at[rows, :], out_ref.at[rows, :], sem))
            copies[-1].start()
    for copy in copies:
        copy.wait()


def two_exchanges(teacher_hidden, student_hidden, teacher_head, student_head, labels, *, shards):
    own = labels.shape[0]
    teacher_width, width = teacher_hidden.shape[1], student_hidden.shape[1]
    columns_here = student_head.shape[1]
    tokens = shards * own
    quarter = width // 4
    here = lax.axis_index("vocab").astype(jnp.int32)
    rows = gather_tokens(teacher_hidden, student_hidden, labels, shards).reshape(tokens, -1)
    student_rows = rows[:, teacher_width : teacher_width + width]
    other = [(0, 1), (1, 0)]
    student_other = lax.ppermute(student_rows, "rows", other)

    square = jax.ShapeDtypeStruct((tokens, columns_here), F32)
    payload, teacher_logits, student_logits, target = pl.pallas_call(
        raw_partial_kernel,
        out_shape=(jax.ShapeDtypeStruct((shards, 8, 3 * quarter + 128), BF16), square, square, square),
        in_specs=[SMEM, VMEM, VMEM],
        out_specs=(ANY, VMEM, VMEM, VMEM),
        scratch_shapes=[pltpu.VMEM((shards, 8, 3 * quarter + 128), BF16), pltpu.SemaphoreType.DMA((4,))],
        compiler_params=SMALL,
    )((here * columns_here)[None], rows, jnp.concatenate([teacher_head, student_head], axis=0))
    arrived = swap(payload)
    grad_rows = pl.pallas_call(
        logit_grad_kernel,
        out_shape=jax.ShapeDtypeStruct((tokens, columns_here), BF16),
        in_specs=[VMEM] * 4,
        out_specs=VMEM,
        compiler_params=SMALL,
    )(arrived[:, :, 3 * quarter :], teacher_logits, student_logits, target)
    grad_other = lax.ppermute(grad_rows, "rows", other)
    hidden_grad, token_loss = pl.pallas_call(
        owner_kernel,
        out_shape=(jax.ShapeDtypeStruct((own, width), F32), jax.ShapeDtypeStruct((own,), F32)),
        in_specs=[VMEM],
        out_specs=(VMEM, SMEM),
        compiler_params=SMALL,
    )(arrived)
    head_grad = pl.pallas_call(
        head_grad_kernel,
        out_shape=jax.ShapeDtypeStruct((width, columns_here), F32),
        in_specs=[VMEM] * 4,
        out_specs=ANY,
        scratch_shapes=[pltpu.VMEM((width, columns_here), F32), pltpu.SemaphoreType.DMA((2 * PIECES,))],
        compiler_params=SMALL,
    )(student_rows, student_other, grad_rows, grad_other)
    return (token_loss, hidden_grad, head_grad)


def three_exchanges(teacher_hidden, student_hidden, teacher_head, student_head, labels, *, shards):
    own = labels.shape[0]
    student_width = student_hidden.shape[1]
    columns_here = student_head.shape[1]
    first_column = lax.axis_index("vocab") * columns_here
    rows = gather_tokens(teacher_hidden, student_hidden, labels, shards).reshape(shards * own, -1)
    teacher_width = teacher_hidden.shape[1]
    teacher_rows = rows[:, :teacher_width]
    student_rows = rows[:, teacher_width : teacher_width + student_width]
    code = rows[:, teacher_width + student_width :].astype(jnp.int32)
    label_rows = code[:, 0] * 128 + code[:, 1]
    other = [(0, 1), (1, 0)]
    student_other = lax.ppermute(student_rows, "rows", other)

    teacher_logits = jnp.dot(teacher_rows, teacher_head, preferred_element_type=F32)
    student_logits = jnp.dot(student_rows, student_head, preferred_element_type=F32)
    columns = lax.broadcasted_iota(jnp.int32, student_logits.shape, 1)
    target = (label_rows - first_column)[:, None] == columns
    top_t = jnp.max(teacher_logits, axis=1, keepdims=True)
    exp_t = jnp.exp(teacher_logits - top_t)
    top_s = jnp.max(student_logits, axis=1, keepdims=True)
    exp_s = jnp.exp(student_logits - top_s)
    stats = jnp.concatenate(
        [
            top_t,
            jnp.sum(exp_t, axis=1, keepdims=True),
            jnp.sum(exp_t * (teacher_logits - student_logits), axis=1, keepdims=True),
            top_s,
            jnp.sum(exp_s, axis=1, keepdims=True),
            jnp.sum(jnp.where(target, student_logits, 0.0), axis=1, keepdims=True),
        ],
        axis=1,
    )
    every = swap(jnp.broadcast_to(stats[None], (shards,) + stats.shape))
    all_top_t = jnp.max(every[:, :, 0], axis=0)
    factor_t = jnp.exp(every[:, :, 0] - all_top_t[None])
    all_top_s = jnp.max(every[:, :, 3], axis=0)
    factor_s = jnp.exp(every[:, :, 3] - all_top_s[None])
    mass_t = jnp.sum(every[:, :, 1] * factor_t, axis=0)
    cross = jnp.sum(every[:, :, 2] * factor_t, axis=0)
    mass_s = jnp.sum(every[:, :, 4] * factor_s, axis=0)
    picked = jnp.sum(every[:, :, 5], axis=0)
    loss = cross / mass_t - all_top_t - jnp.log(mass_t) + 2.0 * (all_top_s + jnp.log(mass_s)) - picked
    token_loss = lax.dynamic_slice_in_dim(loss, lax.axis_index("vocab") * own, own, 0)

    teacher_prob = jnp.exp(teacher_logits - all_top_t[:, None]) / mass_t[:, None]
    student_prob = jnp.exp(student_logits - all_top_s[:, None]) / mass_s[:, None]
    grad_rows = (2.0 * student_prob - teacher_prob - target.astype(F32)).astype(BF16)
    grad_other = lax.ppermute(grad_rows, "rows", other)
    partial = lax.dot_general(grad_rows, student_head, (((1,), (1,)), ((), ())), preferred_element_type=F32)
    arrived = swap(partial.astype(BF16).reshape(shards, own, student_width))
    hidden_grad = jnp.sum(arrived.astype(F32), axis=0)
    head_grad = lax.dot_general(
        jnp.concatenate([student_rows, student_other], axis=0),
        jnp.concatenate([grad_rows, grad_other], axis=0),
        (((0,), (0,)), ((), ())),
        preferred_element_type=F32,
    )
    return (token_loss, hidden_grad, head_grad)


def solution(mesh):
    tokens = ("groups", "vocab", "rows")
    in_specs = (P(tokens, None), P(tokens, None), P(None, "vocab"), P(None, "vocab"), P(tokens))
    out_specs = (P(tokens), P(tokens, None), P("groups", "vocab"))

    def body(*arrays):
        shards = mesh.shape["vocab"]
        own = arrays[4].shape[0]
        small = own == 2 and shards % 4 == 0 and shards * own <= 24
        return (two_exchanges if small else three_exchanges)(*arrays, shards=shards)

    return jax.shard_map(body, mesh=mesh, in_specs=in_specs, out_specs=out_specs, check_vma=False)
```

```python
import jax
import jax.numpy as jnp
from jax import lax
from jax.experimental import pallas as pl
from jax.experimental.pallas import tpu as pltpu
from jax.sharding import PartitionSpec as P

F32 = jnp.float32
BF16 = jnp.bfloat16
CODE = 128


UNROLL = 16
PIECES = 7
SMEM = pl.BlockSpec(memory_space=pltpu.SMEM)
VMEM = pl.BlockSpec(memory_space=pltpu.VMEM)
ANY = pl.BlockSpec(memory_space=pl.ANY)
SMALL = pltpu.CompilerParams(vmem_limit_bytes=16 * 1024 * 1024)


def over_shards(shards, body):
    if shards <= UNROLL:
        for shard in range(shards):
            body(shard)
    else:
        pl.loop(0, shards)(body)


def swap(blocks):
    return lax.all_to_all(blocks, "vocab", split_axis=0, concat_axis=0, tiled=True)


def payload_kernel(labels_ref, teacher_ref, student_ref, out_ref):
    shards, own, _ = out_ref.shape
    teacher_width, student_width = teacher_ref.shape[1], student_ref.shape[1]
    teacher = teacher_ref[...]
    student = student_ref[...]
    code = label_digits(labels_ref, own)

    def write(shard):
        out_ref[shard, :, :teacher_width] = teacher
        out_ref[shard, :, teacher_width : teacher_width + student_width] = student
        out_ref[shard, :, teacher_width + student_width :] = code

    over_shards(shards, write)


def label_digits(labels_ref, own):
    row = lax.broadcasted_iota(jnp.int32, (own, CODE), 0)
    lane = lax.broadcasted_iota(jnp.int32, (own, CODE), 1)
    digits = jnp.zeros((own, CODE), jnp.int32)
    for token in range(own):
        label = labels_ref[token]
        pair = jnp.where(lane == 0, label >> 7, label & 127)
        digits = jnp.where(row == token, pair, digits)
    return digits.astype(F32).astype(BF16)


def gather_tokens(teacher_hidden, student_hidden, labels, shards):
    own, teacher_width = teacher_hidden.shape
    student_width = student_hidden.shape[1]
    payload = pl.pallas_call(
        payload_kernel,
        out_shape=jax.ShapeDtypeStruct((shards, own, teacher_width + student_width + CODE), BF16),
        in_specs=[SMEM, VMEM, VMEM],
        out_specs=VMEM,
    )(labels, teacher_hidden, student_hidden)
    return swap(payload)


def raw_partial_kernel(
    first_ref, rows_ref, heads_ref, out_hbm, teacher_ref, student_ref, target_ref, out_ref, sems
):
    tokens = rows_ref.shape[0]
    shards = out_ref.shape[0]
    wide = 8 * shards
    columns = heads_ref.shape[1]
    quarter = (out_ref.shape[2] - 128) // 3
    width = 4 * quarter
    teacher_width = heads_ref.shape[0] - width

    def iota(shape, dim):
        return lax.broadcasted_iota(jnp.int32, shape, dim)

    def dot(left, right, dims):
        return lax.dot_general(left, right, (dims, ((), ())), preferred_element_type=F32)

    copies = []

    def send_out(piece, start, size):
        lanes = pl.ds(start, size)
        copies.append(pltpu.make_async_copy(out_ref.at[:, :, lanes], out_hbm.at[:, :, lanes], sems.at[piece]))
        copies[-1].start()

    def logits(start, size):
        half = size // 2
        sides = [slice(start, start + half), slice(start + half, start + size)]
        left = jnp.concatenate([rows_ref[:, side] for side in sides], axis=0)
        right = jnp.concatenate([heads_ref[side, :] for side in sides], axis=1)
        both = dot(left, right, ((1,), (0,)))
        return both[:tokens, :columns] + both[tokens:, columns:]

    student = logits(teacher_width, width)
    teacher = logits(0, teacher_width)
    code = rows_ref[:, teacher_width + width :].astype(F32)
    lane = iota(code.shape, 1)
    label = jnp.sum(jnp.where(lane == 0, code * 128.0, jnp.where(lane == 1, code, 0.0)), axis=1, keepdims=True)
    target = (label.astype(jnp.int32) == iota((tokens, columns), 1) + first_ref[...]).astype(F32)
    teacher_ref[...] = teacher
    student_ref[...] = student
    target_ref[...] = target

    def total(array):
        return jnp.sum(array, axis=1, keepdims=True)

    top_t = jnp.max(teacher, axis=1, keepdims=True)
    top_s = jnp.max(student, axis=1, keepdims=True)
    exp_t = jnp.exp(teacher - top_t)
    exp_s = jnp.exp(student - top_s)
    mass_t, mass_s = total(exp_t), total(exp_s)
    combined = exp_s * (2.0 / mass_s) - exp_t / mass_t
    confidence = total(target * (exp_s * (2.0 / mass_s) + exp_t / mass_t))
    kappa = (confidence > 0.75).astype(F32)
    stats = [
        top_t,
        mass_t,
        total(exp_t * (teacher - student)),
        top_s,
        mass_s,
        total(target * student),
        total(target * teacher),
        2.0 * kappa + total(target),
    ]
    lane = iota((tokens, 128), 1)
    table = jnp.zeros((tokens, 128), F32)
    for k, stat in enumerate(stats):
        table = jnp.where(lane % 8 == k, stat, table)
    first = table.astype(BF16).astype(F32)
    second = (table - first).astype(BF16).astype(F32)
    part = (lane % 32) // 8
    parts = jnp.where(
        part == 0, first, jnp.where(part == 1, second, jnp.where(part == 2, table - first - second, 0.0))
    ).astype(BF16)

    row, column = iota((wide, tokens), 0), iota((wide, tokens), 1)
    of_token = (column == (row // 8) * 2 + row % 2).astype(F32).astype(BF16)
    by_row = dot(of_token, parts, ((1,), (0,)))

    def stat_by_row(k):
        picked = by_row[:, k : k + 1] + by_row[:, 8 + k : 9 + k] + by_row[:, 16 + k : 17 + k]
        return picked

    lane = iota((8, 128), 1)
    shared = jnp.zeros((8, 128), F32)
    wide_parts = parts.astype(F32)
    for group in range(tokens // 8):
        shared = jnp.where(lane // 32 == group + 1, wide_parts[8 * group : 8 * group + 8], shared)
    for shard in range(shards):
        block = jnp.where(lane < 32, by_row[8 * shard : 8 * shard + 8], shared)
        out_ref[shard, :, 3 * quarter :] = block.astype(BF16)
    send_out(3, 3 * quarter, 128)

    members = jnp.concatenate([exp_s, exp_t, kappa * combined * total(target) - target], axis=0)
    member_high = members.astype(BF16)
    member_low = (members - member_high.astype(F32)).astype(BF16)
    row, column = iota((wide, 3 * tokens), 0), iota((wide, 3 * tokens), 1)
    place = row % 8
    token = (row // 8) * 2 + row % 2
    pick = ((place < 6) & (column == (place // 2) * tokens + token)).astype(F32).astype(BF16)
    left = dot(pick, jnp.concatenate([member_high, member_low], axis=1), ((1,), (0,))).astype(BF16)
    left = jnp.concatenate([left[:, :columns], left[:, columns:]], axis=0)

    def partials(start):
        both = dot(left, heads_ref[teacher_width + start : teacher_width + start + quarter, :], ((1,), (1,)))
        return both[:wide] + both[wide:]

    place = iota((wide, 1), 0) % 8
    has_label = stat_by_row(7) > 0.5
    scale_s = jnp.where(has_label, 0.0, 2.0 / stat_by_row(4))
    scale_t = jnp.where(has_label, 0.0, -1.0 / stat_by_row(1))
    scale = jnp.where(place < 2, scale_s, jnp.where(place < 4, scale_t, 0.0))
    in_third = ((place == 4) | (place == 5)).astype(F32)
    scale_s = jnp.where(place >= 6, scale_s, 0.0)
    scale_t = jnp.where(place >= 6, scale_t, 0.0)
    last = partials(3 * quarter)
    correction = jnp.zeros((wide, quarter), F32)
    for j in range(3):
        exact = partials(j * quarter) + jnp.where(place >= 6, pltpu.roll(last, 6 - 2 * j, 0), 0.0)
        sent = exact.astype(BF16).astype(F32)
        residue = exact - sent
        if j < 2:
            correction += residue * (scale_s, scale_t)[j]
        else:
            sent += correction
        scaled = residue * scale
        sent += in_third * (pltpu.roll(scaled, 4, 0) + pltpu.roll(scaled, 2, 0))
        for shard in range(shards):
            out_ref[shard, :, j * quarter : (j + 1) * quarter] = sent[8 * shard : 8 * shard + 8].astype(BF16)
        send_out(j, j * quarter, quarter)
    for copy in copies:
        copy.wait()


def sum_parts(tail):
    shards = tail.shape[0]
    flat = tail.astype(F32).reshape(shards * 8, 128)
    return flat + pltpu.roll(flat, 120, 1) + pltpu.roll(flat, 112, 1)


def fold(flat, lane):
    shards = flat.shape[0] // 8
    stats = [flat[:, lane + k : lane + k + 1].reshape(shards, 8, 1) for k in range(8)]
    top_t = jnp.max(stats[0], axis=0)
    factor_t = jnp.exp(stats[0] - top_t)
    top_s = jnp.max(stats[3], axis=0)
    factor_s = jnp.exp(stats[3] - top_s)
    mass_t = jnp.sum(stats[1] * factor_t, axis=0)
    mass_s = jnp.sum(stats[4] * factor_s, axis=0)
    return stats, top_t, factor_t, mass_t, top_s, factor_s, mass_s


def logit_grad_kernel(tail_ref, teacher_ref, student_ref, target_ref, out_ref):
    flat = sum_parts(tail_ref[...])
    folded = [fold(flat, 32 * group + 32) for group in range(out_ref.shape[0] // 8)]
    top_t, mass_t, top_s, mass_s = [jnp.concatenate([f[i] for f in folded], axis=0) for i in (1, 3, 4, 6)]
    teacher_prob = jnp.exp(teacher_ref[...] - top_t) / mass_t
    student_prob = jnp.exp(student_ref[...] - top_s) / mass_s
    out_ref[...] = (2.0 * student_prob - teacher_prob - target_ref[...]).astype(BF16)


def owner_kernel(arrived_ref, out_ref, loss_ref):
    shards, _, lanes = arrived_ref.shape
    quarter = (lanes - 128) // 3
    stats, top_t, factor_t, mass_t, top_s, factor_s, mass_s = fold(sum_parts(arrived_ref[:, :, 3 * quarter :]), 0)
    cross = jnp.sum(stats[2] * factor_t, axis=0)
    picked = jnp.sum(stats[5], axis=0)
    picked_t = jnp.sum(stats[6], axis=0)
    loss = cross / mass_t - top_t - jnp.log(mass_t) + 2.0 * (top_s + jnp.log(mass_s)) - picked
    token = lax.broadcasted_iota(jnp.int32, (8, 1), 0)
    for t in range(out_ref.shape[0]):
        loss_ref[t] = jnp.sum(jnp.where(token == t, loss, 0.0))
    label_grad = 2.0 * (jnp.exp(picked - top_s) / mass_s) - jnp.exp(picked_t - top_t) / mass_t - 1.0
    rounding = label_grad.astype(BF16).astype(F32) - label_grad
    weight_s = factor_s / mass_s
    weight_t = factor_t / mass_t
    share = 0.8 * weight_s * stats[4] + 0.2 * weight_t * stats[1]
    kappa = jnp.where(stats[7] > 2.0, 1.0, 0.0)
    weight_l = jnp.where(stats[7] > 0.5, 1.0 - (1.0 - kappa) * rounding, share)
    weight_s = 2.0 * (weight_s - kappa / stats[4])
    weight_t = kappa / stats[1] - weight_t
    place = lax.broadcasted_iota(jnp.int32, (shards, 8, 1), 1)
    last = jnp.zeros((8, quarter), F32)
    for j, weight_last in enumerate((weight_s, weight_t, weight_l)):
        weight = jnp.where(
            place < 2, weight_s, jnp.where(place < 4, weight_t, jnp.where(place < 6, weight_l, weight_last))
        )
        piece = jnp.zeros((8, quarter), F32)
        for shard in range(shards):
            piece += weight[shard] * arrived_ref[shard, :, j * quarter : (j + 1) * quarter].astype(F32)
        last += piece
        out_ref[:, j * quarter : (j + 1) * quarter] = piece[0:2] + piece[2:4] + piece[4:6]
    out_ref[:, 3 * quarter :] = last[6:8]


def head_grad_kernel(hidden_ref, hidden_other_ref, grad_ref, other_ref, out_ref, total_ref, sems):
    grads = jnp.concatenate([grad_ref[...], other_ref[...]], axis=0)
    size = hidden_ref.shape[1] // PIECES
    copies = []
    for piece in range(PIECES):
        rows = pl.ds(piece * size, size)
        hidden = jnp.concatenate([hidden_ref[:, rows], hidden_other_ref[:, rows]], axis=0)
        total_ref[rows, :] = lax.dot_general(hidden, grads, (((0,), (0,)), ((), ())), preferred_element_type=F32)
        copies.append(pltpu.make_async_copy(total_ref.at[rows, :], out_ref.at[rows, :], sems.at[piece]))
        copies[-1].start()
    for copy in copies:
        copy.wait()


def two_exchanges(teacher_hidden, student_hidden, teacher_head, student_head, labels, *, shards):
    own = labels.shape[0]
    teacher_width, width = teacher_hidden.shape[1], student_hidden.shape[1]
    columns_here = student_head.shape[1]
    tokens = shards * own
    quarter = width // 4
    here = lax.axis_index("vocab").astype(jnp.int32)
    rows = gather_tokens(teacher_hidden, student_hidden, labels, shards).reshape(tokens, -1)
    student_rows = rows[:, teacher_width : teacher_width + width]
    other = [(0, 1), (1, 0)]
    student_other = lax.ppermute(student_rows, "rows", other)

    square = jax.ShapeDtypeStruct((tokens, columns_here), F32)
    payload, teacher_logits, student_logits, target = pl.pallas_call(
        raw_partial_kernel,
        out_shape=(jax.ShapeDtypeStruct((shards, 8, 3 * quarter + 128), BF16), square, square, square),
        in_specs=[VMEM, VMEM, VMEM],
        out_specs=(ANY, VMEM, VMEM, VMEM),
        scratch_shapes=[pltpu.VMEM((shards, 8, 3 * quarter + 128), BF16), pltpu.SemaphoreType.DMA((4,))],
        compiler_params=SMALL,
    )(jnp.full((1, columns_here), here * columns_here, jnp.int32), rows, jnp.concatenate([teacher_head, student_head], axis=0))
    arrived = swap(payload)
    grad_rows = pl.pallas_call(
        logit_grad_kernel,
        out_shape=jax.ShapeDtypeStruct((tokens, columns_here), BF16),
        in_specs=[VMEM] * 4,
        out_specs=VMEM,
        compiler_params=SMALL,
    )(arrived[:, :, 3 * quarter :], teacher_logits, student_logits, target)
    grad_other = lax.ppermute(grad_rows, "rows", other)
    hidden_grad, token_loss = pl.pallas_call(
        owner_kernel,
        out_shape=(jax.ShapeDtypeStruct((own, width), F32), jax.ShapeDtypeStruct((own,), F32)),
        in_specs=[VMEM],
        out_specs=(VMEM, SMEM),
        compiler_params=SMALL,
    )(arrived)
    head_grad = pl.pallas_call(
        head_grad_kernel,
        out_shape=jax.ShapeDtypeStruct((width, columns_here), F32),
        in_specs=[VMEM] * 4,
        out_specs=ANY,
        scratch_shapes=[pltpu.VMEM((width, columns_here), F32), pltpu.SemaphoreType.DMA((PIECES,))],
        compiler_params=SMALL,
    )(student_rows, student_other, grad_rows, grad_other)
    return (token_loss, hidden_grad, head_grad)


def three_exchanges(teacher_hidden, student_hidden, teacher_head, student_head, labels, *, shards):
    own = labels.shape[0]
    student_width = student_hidden.shape[1]
    columns_here = student_head.shape[1]
    first_column = lax.axis_index("vocab") * columns_here
    rows = gather_tokens(teacher_hidden, student_hidden, labels, shards).reshape(shards * own, -1)
    teacher_width = teacher_hidden.shape[1]
    teacher_rows = rows[:, :teacher_width]
    student_rows = rows[:, teacher_width : teacher_width + student_width]
    code = rows[:, teacher_width + student_width :].astype(jnp.int32)
    label_rows = code[:, 0] * 128 + code[:, 1]
    other = [(0, 1), (1, 0)]
    student_other = lax.ppermute(student_rows, "rows", other)

    teacher_logits = jnp.dot(teacher_rows, teacher_head, preferred_element_type=F32)
    student_logits = jnp.dot(student_rows, student_head, preferred_element_type=F32)
    columns = lax.broadcasted_iota(jnp.int32, student_logits.shape, 1)
    target = (label_rows - first_column)[:, None] == columns
    top_t = jnp.max(teacher_logits, axis=1, keepdims=True)
    exp_t = jnp.exp(teacher_logits - top_t)
    top_s = jnp.max(student_logits, axis=1, keepdims=True)
    exp_s = jnp.exp(student_logits - top_s)
    stats = jnp.concatenate(
        [
            top_t,
            jnp.sum(exp_t, axis=1, keepdims=True),
            jnp.sum(exp_t * (teacher_logits - student_logits), axis=1, keepdims=True),
            top_s,
            jnp.sum(exp_s, axis=1, keepdims=True),
            jnp.sum(jnp.where(target, student_logits, 0.0), axis=1, keepdims=True),
        ],
        axis=1,
    )
    every = swap(jnp.broadcast_to(stats[None], (shards,) + stats.shape))
    all_top_t = jnp.max(every[:, :, 0], axis=0)
    factor_t = jnp.exp(every[:, :, 0] - all_top_t[None])
    all_top_s = jnp.max(every[:, :, 3], axis=0)
    factor_s = jnp.exp(every[:, :, 3] - all_top_s[None])
    mass_t = jnp.sum(every[:, :, 1] * factor_t, axis=0)
    cross = jnp.sum(every[:, :, 2] * factor_t, axis=0)
    mass_s = jnp.sum(every[:, :, 4] * factor_s, axis=0)
    picked = jnp.sum(every[:, :, 5], axis=0)
    loss = cross / mass_t - all_top_t - jnp.log(mass_t) + 2.0 * (all_top_s + jnp.log(mass_s)) - picked
    token_loss = lax.dynamic_slice_in_dim(loss, lax.axis_index("vocab") * own, own, 0)

    teacher_prob = jnp.exp(teacher_logits - all_top_t[:, None]) / mass_t[:, None]
    student_prob = jnp.exp(student_logits - all_top_s[:, None]) / mass_s[:, None]
    grad_rows = (2.0 * student_prob - teacher_prob - target.astype(F32)).astype(BF16)
    grad_other = lax.ppermute(grad_rows, "rows", other)
    partial = lax.dot_general(grad_rows, student_head, (((1,), (1,)), ((), ())), preferred_element_type=F32)
    arrived = swap(partial.astype(BF16).reshape(shards, own, student_width))
    hidden_grad = jnp.sum(arrived.astype(F32), axis=0)
    head_grad = lax.dot_general(
        jnp.concatenate([student_rows, student_other], axis=0),
        jnp.concatenate([grad_rows, grad_other], axis=0),
        (((0,), (0,)), ((), ())),
        preferred_element_type=F32,
    )
    return (token_loss, hidden_grad, head_grad)


def solution(mesh):
    tokens = ("groups", "vocab", "rows")
    in_specs = (P(tokens, None), P(tokens, None), P(None, "vocab"), P(None, "vocab"), P(tokens))
    out_specs = (P(tokens), P(tokens, None), P("groups", "vocab"))

    def body(*arrays):
        shards = mesh.shape["vocab"]
        own = arrays[4].shape[0]
        small = own == 2 and shards % 4 == 0 and shards * own <= 24
        return (two_exchanges if small else three_exchanges)(*arrays, shards=shards)

    return jax.shard_map(body, mesh=mesh, in_specs=in_specs, out_specs=out_specs, check_vma=False)
```

```python
import jax
import jax.numpy as jnp
from jax import lax
from jax.experimental import pallas as pl
from jax.experimental.pallas import tpu as pltpu
from jax.sharding import PartitionSpec as P

F32 = jnp.float32
BF16 = jnp.bfloat16
CODE = 128


UNROLL = 16
LANES = 128
PIECES = 7
SMEM = pl.BlockSpec(memory_space=pltpu.SMEM)
VMEM = pl.BlockSpec(memory_space=pltpu.VMEM)
ANY = pl.BlockSpec(memory_space=pl.ANY)
SMALL = pltpu.CompilerParams(vmem_limit_bytes=16 * 1024 * 1024)


def over_shards(shards, body):
    if shards <= UNROLL:
        for shard in range(shards):
            body(shard)
    else:
        pl.loop(0, shards)(body)


def swap(blocks):
    return lax.all_to_all(blocks, "vocab", split_axis=0, concat_axis=0, tiled=True)


def payload_kernel(labels_ref, teacher_ref, student_ref, out_ref):
    shards, own, _ = out_ref.shape
    teacher_width, student_width = teacher_ref.shape[1], student_ref.shape[1]
    teacher = teacher_ref[...]
    student = student_ref[...]
    code = label_digits(labels_ref, own)

    def write(shard):
        out_ref[shard, :, :teacher_width] = teacher
        out_ref[shard, :, teacher_width : teacher_width + student_width] = student
        out_ref[shard, :, teacher_width + student_width :] = code

    over_shards(shards, write)


def label_digits(labels_ref, own):
    row = lax.broadcasted_iota(jnp.int32, (own, CODE), 0)
    lane = lax.broadcasted_iota(jnp.int32, (own, CODE), 1)
    digits = jnp.zeros((own, CODE), jnp.int32)
    for token in range(own):
        label = labels_ref[token]
        pair = jnp.where(lane == 0, label >> 7, label & 127)
        digits = jnp.where(row == token, pair, digits)
    return digits.astype(F32).astype(BF16)


def gather_tokens(teacher_hidden, student_hidden, labels, shards):
    own, teacher_width = teacher_hidden.shape
    student_width = student_hidden.shape[1]
    payload = pl.pallas_call(
        payload_kernel,
        out_shape=jax.ShapeDtypeStruct((shards, own, teacher_width + student_width + CODE), BF16),
        in_specs=[SMEM, VMEM, VMEM],
        out_specs=VMEM,
    )(labels, teacher_hidden, student_hidden)
    return swap(payload)


def raw_partial_kernel(
    first_ref, rows_ref, heads_ref, out_hbm, teacher_ref, student_ref, target_ref, out_ref, sems
):
    tokens = rows_ref.shape[0]
    shards = out_ref.shape[0]
    wide = 8 * shards
    columns = heads_ref.shape[1]
    quarter = (out_ref.shape[2] - 128) // 3
    width = 4 * quarter
    teacher_width = heads_ref.shape[0] - width

    def iota(shape, dim):
        return lax.broadcasted_iota(jnp.int32, shape, dim)

    def dot(left, right, dims):
        return lax.dot_general(left, right, (dims, ((), ())), preferred_element_type=F32)

    copies = []

    def send_out(piece, start, size):
        lanes = pl.ds(start, size)
        copies.append(pltpu.make_async_copy(out_ref.at[:, :, lanes], out_hbm.at[:, :, lanes], sems.at[piece]))
        copies[-1].start()

    student = dot(rows_ref[:, teacher_width : teacher_width + width], heads_ref[teacher_width:, :], ((1,), (0,)))
    teacher = dot(rows_ref[:, :teacher_width], heads_ref[:teacher_width, :], ((1,), (0,)))
    code = rows_ref[:, teacher_width + width :].astype(F32)
    lane = iota(code.shape, 1)
    label = jnp.sum(jnp.where(lane == 0, code * 128.0, jnp.where(lane == 1, code, 0.0)), axis=1, keepdims=True)
    target = (label.astype(jnp.int32) - first_ref[0] == iota((tokens, columns), 1)).astype(F32)
    teacher_ref[...] = teacher
    student_ref[...] = student
    target_ref[...] = target

    def total(array):
        return jnp.sum(array, axis=1, keepdims=True)

    top_t = jnp.max(teacher, axis=1, keepdims=True)
    top_s = jnp.max(student, axis=1, keepdims=True)
    exp_t = jnp.exp(teacher - top_t)
    exp_s = jnp.exp(student - top_s)
    mass_t, mass_s = total(exp_t), total(exp_s)
    combined = exp_s * (2.0 / mass_s) - exp_t / mass_t
    confidence = total(target * (exp_s * (2.0 / mass_s) + exp_t / mass_t))
    kappa = (confidence > 0.75).astype(F32)
    stats = [
        top_t,
        mass_t,
        total(exp_t * (teacher - student)),
        top_s,
        mass_s,
        total(target * student),
        total(target * teacher),
        2.0 * kappa + total(target),
    ]
    lane = iota((tokens, 128), 1)
    table = jnp.zeros((tokens, 128), F32)
    for k, stat in enumerate(stats):
        table = jnp.where(lane % 8 == k, stat, table)
    first = table.astype(BF16).astype(F32)
    second = (table - first).astype(BF16).astype(F32)
    part = (lane % 32) // 8
    parts = jnp.where(
        part == 0, first, jnp.where(part == 1, second, jnp.where(part == 2, table - first - second, 0.0))
    ).astype(BF16)

    row, column = iota((wide, tokens), 0), iota((wide, tokens), 1)
    of_token = (column == (row // 8) * 2 + row % 2).astype(F32).astype(BF16)
    by_row = dot(of_token, parts, ((1,), (0,)))

    def stat_by_row(k):
        picked = by_row[:, k : k + 1] + by_row[:, 8 + k : 9 + k] + by_row[:, 16 + k : 17 + k]
        return picked

    lane = iota((8, 128), 1)
    shared = jnp.zeros((8, 128), F32)
    wide_parts = parts.astype(F32)
    for group in range(tokens // 8):
        shared = jnp.where(lane // 32 == group + 1, wide_parts[8 * group : 8 * group + 8], shared)
    for shard in range(shards):
        block = jnp.where(lane < 32, by_row[8 * shard : 8 * shard + 8], shared)
        out_ref[shard, :, 3 * quarter :] = block.astype(BF16)
    send_out(0, 3 * quarter, 128)

    members = jnp.concatenate([exp_s, exp_t, kappa * combined * total(target) - target], axis=0)
    member_high = members.astype(BF16)
    member_low = (members - member_high.astype(F32)).astype(BF16)
    row, column = iota((wide, 3 * tokens), 0), iota((wide, 3 * tokens), 1)
    place = row % 8
    token = (row // 8) * 2 + row % 2
    pick = ((place < 6) & (column == (place // 2) * tokens + token)).astype(F32).astype(BF16)
    left = dot(pick, jnp.concatenate([member_high, member_low], axis=1), ((1,), (0,))).astype(BF16)
    left = jnp.concatenate([left[:, :columns], left[:, columns:]], axis=0)

    place = iota((wide, 1), 0) % 8
    has_label = stat_by_row(7) > 0.5
    scale_s = jnp.where(has_label, 0.0, 2.0 / stat_by_row(4))
    scale_t = jnp.where(has_label, 0.0, -1.0 / stat_by_row(1))
    scale = jnp.where(place < 2, scale_s, jnp.where(place < 4, scale_t, 0.0))
    in_third = ((place == 4) | (place == 5)).astype(F32)
    scale_s = jnp.where(place >= 6, scale_s, 0.0)
    scale_t = jnp.where(place >= 6, scale_t, 0.0)
    chunks = quarter // LANES
    first_unsent = 0
    for chunk in range(chunks):
        starts = [teacher_width + j * quarter + chunk * LANES for j in range(4)]
        right = jnp.concatenate([heads_ref[start : start + LANES, :] for start in starts], axis=0)
        both = dot(left, right, ((1,), (1,)))
        exact = [both[:wide, j * LANES : (j + 1) * LANES] + both[wide:, j * LANES : (j + 1) * LANES] for j in range(4)]
        correction = jnp.zeros((wide, LANES), F32)
        for j in range(3):
            whole = jnp.where(place >= 6, pltpu.roll(exact[3], 6 - 2 * j, 0), exact[j])
            sent = whole.astype(BF16).astype(F32)
            residue = whole - sent
            if j < 2:
                correction += residue * (scale_s, scale_t)[j]
            else:
                sent += correction
            scaled = residue * scale
            sent += in_third * (pltpu.roll(scaled, 4, 0) + pltpu.roll(scaled, 2, 0))
            lanes = slice((3 * chunk + j) * LANES, (3 * chunk + j + 1) * LANES)
            for shard in range(shards):
                out_ref[shard, :, lanes] = sent[8 * shard : 8 * shard + 8].astype(BF16)
        if chunk % 3 == 2 or chunk == chunks - 1:
            end = 3 * (chunk + 1) * LANES
            send_out(len(copies), first_unsent, end - first_unsent)
            first_unsent = end
    for copy in copies:
        copy.wait()


def sum_parts(tail):
    shards = tail.shape[0]
    flat = tail.astype(F32).reshape(shards * 8, 128)
    return flat + pltpu.roll(flat, 120, 1) + pltpu.roll(flat, 112, 1)


def fold(flat, lane):
    shards = flat.shape[0] // 8
    stats = [flat[:, lane + k : lane + k + 1].reshape(shards, 8, 1) for k in range(8)]
    top_t = jnp.max(stats[0], axis=0)
    factor_t = jnp.exp(stats[0] - top_t)
    top_s = jnp.max(stats[3], axis=0)
    factor_s = jnp.exp(stats[3] - top_s)
    mass_t = jnp.sum(stats[1] * factor_t, axis=0)
    mass_s = jnp.sum(stats[4] * factor_s, axis=0)
    return stats, top_t, factor_t, mass_t, top_s, factor_s, mass_s


def logit_grad_kernel(tail_ref, teacher_ref, student_ref, target_ref, out_ref):
    flat = sum_parts(tail_ref[...])
    folded = [fold(flat, 32 * group + 32) for group in range(out_ref.shape[0] // 8)]
    top_t, mass_t, top_s, mass_s = [jnp.concatenate([f[i] for f in folded], axis=0) for i in (1, 3, 4, 6)]
    teacher_prob = jnp.exp(teacher_ref[...] - top_t) / mass_t
    student_prob = jnp.exp(student_ref[...] - top_s) / mass_s
    out_ref[...] = (2.0 * student_prob - teacher_prob - target_ref[...]).astype(BF16)


def owner_kernel(arrived_ref, out_ref, loss_ref):
    shards, _, lanes = arrived_ref.shape
    quarter = (lanes - 128) // 3
    stats, top_t, factor_t, mass_t, top_s, factor_s, mass_s = fold(sum_parts(arrived_ref[:, :, 3 * quarter :]), 0)
    cross = jnp.sum(stats[2] * factor_t, axis=0)
    picked = jnp.sum(stats[5], axis=0)
    picked_t = jnp.sum(stats[6], axis=0)
    loss = cross / mass_t - top_t - jnp.log(mass_t) + 2.0 * (top_s + jnp.log(mass_s)) - picked
    token = lax.broadcasted_iota(jnp.int32, (8, 1), 0)
    for t in range(out_ref.shape[0]):
        loss_ref[t] = jnp.sum(jnp.where(token == t, loss, 0.0))
    label_grad = 2.0 * (jnp.exp(picked - top_s) / mass_s) - jnp.exp(picked_t - top_t) / mass_t - 1.0
    rounding = label_grad.astype(BF16).astype(F32) - label_grad
    weight_s = factor_s / mass_s
    weight_t = factor_t / mass_t
    share = 0.8 * weight_s * stats[4] + 0.2 * weight_t * stats[1]
    kappa = jnp.where(stats[7] > 2.0, 1.0, 0.0)
    weight_l = jnp.where(stats[7] > 0.5, 1.0 - (1.0 - kappa) * rounding, share)
    weight_s = 2.0 * (weight_s - kappa / stats[4])
    weight_t = kappa / stats[1] - weight_t
    place = lax.broadcasted_iota(jnp.int32, (shards, 8, 1), 1)
    last = jnp.zeros((8, quarter), F32)
    for j, weight_last in enumerate((weight_s, weight_t, weight_l)):
        weight = jnp.where(
            place < 2, weight_s, jnp.where(place < 4, weight_t, jnp.where(place < 6, weight_l, weight_last))
        )
        piece = []
        for chunk in range(quarter // LANES):
            lanes = slice((3 * chunk + j) * LANES, (3 * chunk + j + 1) * LANES)
            piece.append(sum(weight[shard] * arrived_ref[shard, :, lanes].astype(F32) for shard in range(shards)))
        piece = jnp.concatenate(piece, axis=1)
        last += piece
        out_ref[:, j * quarter : (j + 1) * quarter] = piece[0:2] + piece[2:4] + piece[4:6]
    out_ref[:, 3 * quarter :] = last[6:8]


def head_grad_kernel(hidden_ref, hidden_other_ref, grad_ref, other_ref, out_ref, total_ref, sems):
    grads = jnp.concatenate([grad_ref[...], other_ref[...]], axis=0)
    size = hidden_ref.shape[1] // PIECES
    copies = []
    for piece in range(PIECES):
        rows = pl.ds(piece * size, size)
        hidden = jnp.concatenate([hidden_ref[:, rows], hidden_other_ref[:, rows]], axis=0)
        total_ref[rows, :] = lax.dot_general(hidden, grads, (((0,), (0,)), ((), ())), preferred_element_type=F32)
        copies.append(pltpu.make_async_copy(total_ref.at[rows, :], out_ref.at[rows, :], sems.at[piece]))
        copies[-1].start()
    for copy in copies:
        copy.wait()


def two_exchanges(teacher_hidden, student_hidden, teacher_head, student_head, labels, *, shards):
    own = labels.shape[0]
    teacher_width, width = teacher_hidden.shape[1], student_hidden.shape[1]
    columns_here = student_head.shape[1]
    tokens = shards * own
    quarter = width // 4
    here = lax.axis_index("vocab").astype(jnp.int32)
    rows = gather_tokens(teacher_hidden, student_hidden, labels, shards).reshape(tokens, -1)
    student_rows = rows[:, teacher_width : teacher_width + width]
    other = [(0, 1), (1, 0)]
    student_other = lax.ppermute(student_rows, "rows", other)

    square = jax.ShapeDtypeStruct((tokens, columns_here), F32)
    payload, teacher_logits, student_logits, target = pl.pallas_call(
        raw_partial_kernel,
        out_shape=(jax.ShapeDtypeStruct((shards, 8, 3 * quarter + 128), BF16), square, square, square),
        in_specs=[SMEM, VMEM, VMEM],
        out_specs=(ANY, VMEM, VMEM, VMEM),
        scratch_shapes=[pltpu.VMEM((shards, 8, 3 * quarter + 128), BF16), pltpu.SemaphoreType.DMA((2 + quarter // LANES // 3,))],
        compiler_params=SMALL,
    )((here * columns_here)[None], rows, jnp.concatenate([teacher_head, student_head], axis=0))
    arrived = swap(payload)
    grad_rows = pl.pallas_call(
        logit_grad_kernel,
        out_shape=jax.ShapeDtypeStruct((tokens, columns_here), BF16),
        in_specs=[VMEM] * 4,
        out_specs=VMEM,
        compiler_params=SMALL,
    )(arrived[:, :, 3 * quarter :], teacher_logits, student_logits, target)
    grad_other = lax.ppermute(grad_rows, "rows", other)
    hidden_grad, token_loss = pl.pallas_call(
        owner_kernel,
        out_shape=(jax.ShapeDtypeStruct((own, width), F32), jax.ShapeDtypeStruct((own,), F32)),
        in_specs=[VMEM],
        out_specs=(VMEM, SMEM),
        compiler_params=SMALL,
    )(arrived)
    head_grad = pl.pallas_call(
        head_grad_kernel,
        out_shape=jax.ShapeDtypeStruct((width, columns_here), F32),
        in_specs=[VMEM] * 4,
        out_specs=ANY,
        scratch_shapes=[pltpu.VMEM((width, columns_here), F32), pltpu.SemaphoreType.DMA((PIECES,))],
        compiler_params=SMALL,
    )(student_rows, student_other, grad_rows, grad_other)
    return (token_loss, hidden_grad, head_grad)


def three_exchanges(teacher_hidden, student_hidden, teacher_head, student_head, labels, *, shards):
    own = labels.shape[0]
    student_width = student_hidden.shape[1]
    columns_here = student_head.shape[1]
    first_column = lax.axis_index("vocab") * columns_here
    rows = gather_tokens(teacher_hidden, student_hidden, labels, shards).reshape(shards * own, -1)
    teacher_width = teacher_hidden.shape[1]
    teacher_rows = rows[:, :teacher_width]
    student_rows = rows[:, teacher_width : teacher_width + student_width]
    code = rows[:, teacher_width + student_width :].astype(jnp.int32)
    label_rows = code[:, 0] * 128 + code[:, 1]
    other = [(0, 1), (1, 0)]
    student_other = lax.ppermute(student_rows, "rows", other)

    teacher_logits = jnp.dot(teacher_rows, teacher_head, preferred_element_type=F32)
    student_logits = jnp.dot(student_rows, student_head, preferred_element_type=F32)
    columns = lax.broadcasted_iota(jnp.int32, student_logits.shape, 1)
    target = (label_rows - first_column)[:, None] == columns
    top_t = jnp.max(teacher_logits, axis=1, keepdims=True)
    exp_t = jnp.exp(teacher_logits - top_t)
    top_s = jnp.max(student_logits, axis=1, keepdims=True)
    exp_s = jnp.exp(student_logits - top_s)
    stats = jnp.concatenate(
        [
            top_t,
            jnp.sum(exp_t, axis=1, keepdims=True),
            jnp.sum(exp_t * (teacher_logits - student_logits), axis=1, keepdims=True),
            top_s,
            jnp.sum(exp_s, axis=1, keepdims=True),
            jnp.sum(jnp.where(target, student_logits, 0.0), axis=1, keepdims=True),
        ],
        axis=1,
    )
    every = swap(jnp.broadcast_to(stats[None], (shards,) + stats.shape))
    all_top_t = jnp.max(every[:, :, 0], axis=0)
    factor_t = jnp.exp(every[:, :, 0] - all_top_t[None])
    all_top_s = jnp.max(every[:, :, 3], axis=0)
    factor_s = jnp.exp(every[:, :, 3] - all_top_s[None])
    mass_t = jnp.sum(every[:, :, 1] * factor_t, axis=0)
    cross = jnp.sum(every[:, :, 2] * factor_t, axis=0)
    mass_s = jnp.sum(every[:, :, 4] * factor_s, axis=0)
    picked = jnp.sum(every[:, :, 5], axis=0)
    loss = cross / mass_t - all_top_t - jnp.log(mass_t) + 2.0 * (all_top_s + jnp.log(mass_s)) - picked
    token_loss = lax.dynamic_slice_in_dim(loss, lax.axis_index("vocab") * own, own, 0)

    teacher_prob = jnp.exp(teacher_logits - all_top_t[:, None]) / mass_t[:, None]
    student_prob = jnp.exp(student_logits - all_top_s[:, None]) / mass_s[:, None]
    grad_rows = (2.0 * student_prob - teacher_prob - target.astype(F32)).astype(BF16)
    grad_other = lax.ppermute(grad_rows, "rows", other)
    partial = lax.dot_general(grad_rows, student_head, (((1,), (1,)), ((), ())), preferred_element_type=F32)
    arrived = swap(partial.astype(BF16).reshape(shards, own, student_width))
    hidden_grad = jnp.sum(arrived.astype(F32), axis=0)
    head_grad = lax.dot_general(
        jnp.concatenate([student_rows, student_other], axis=0),
        jnp.concatenate([grad_rows, grad_other], axis=0),
        (((0,), (0,)), ((), ())),
        preferred_element_type=F32,
    )
    return (token_loss, hidden_grad, head_grad)


def solution(mesh):
    tokens = ("groups", "vocab", "rows")
    in_specs = (P(tokens, None), P(tokens, None), P(None, "vocab"), P(None, "vocab"), P(tokens))
    out_specs = (P(tokens), P(tokens, None), P("groups", "vocab"))

    def body(*arrays):
        shards = mesh.shape["vocab"]
        own = arrays[4].shape[0]
        small = own == 2 and shards % 4 == 0 and shards * own <= 24
        return (two_exchanges if small else three_exchanges)(*arrays, shards=shards)

    return jax.shard_map(body, mesh=mesh, in_specs=in_specs, out_specs=out_specs, check_vma=False)
```

```python
import jax
import jax.numpy as jnp
from jax import lax
from jax.experimental import pallas as pl
from jax.experimental.pallas import tpu as pltpu
from jax.sharding import PartitionSpec as P

F32 = jnp.float32
BF16 = jnp.bfloat16
CODE = 128


UNROLL = 16
LANES = 128
PIECES = 7
SMEM = pl.BlockSpec(memory_space=pltpu.SMEM)
VMEM = pl.BlockSpec(memory_space=pltpu.VMEM)
ANY = pl.BlockSpec(memory_space=pl.ANY)
SMALL = pltpu.CompilerParams(vmem_limit_bytes=16 * 1024 * 1024)


def over_shards(shards, body):
    if shards <= UNROLL:
        for shard in range(shards):
            body(shard)
    else:
        pl.loop(0, shards)(body)


def swap(blocks):
    return lax.all_to_all(blocks, "vocab", split_axis=0, concat_axis=0, tiled=True)


def payload_kernel(labels_ref, teacher_ref, student_ref, out_ref):
    shards, own, _ = out_ref.shape
    teacher_width, student_width = teacher_ref.shape[1], student_ref.shape[1]
    teacher = teacher_ref[...]
    student = student_ref[...]
    code = label_digits(labels_ref, own)

    def write(shard):
        out_ref[shard, :, :teacher_width] = teacher
        out_ref[shard, :, teacher_width : teacher_width + student_width] = student
        out_ref[shard, :, teacher_width + student_width :] = code

    over_shards(shards, write)


def label_digits(labels_ref, own):
    row = lax.broadcasted_iota(jnp.int32, (own, CODE), 0)
    lane = lax.broadcasted_iota(jnp.int32, (own, CODE), 1)
    digits = jnp.zeros((own, CODE), jnp.int32)
    for token in range(own):
        label = labels_ref[token]
        pair = jnp.where(lane == 0, label >> 7, label & 127)
        digits = jnp.where(row == token, pair, digits)
    return digits.astype(F32).astype(BF16)


def gather_tokens(teacher_hidden, student_hidden, labels, shards):
    own, teacher_width = teacher_hidden.shape
    student_width = student_hidden.shape[1]
    payload = pl.pallas_call(
        payload_kernel,
        out_shape=jax.ShapeDtypeStruct((shards, own, teacher_width + student_width + CODE), BF16),
        in_specs=[SMEM, VMEM, VMEM],
        out_specs=VMEM,
    )(labels, teacher_hidden, student_hidden)
    return swap(payload)


def raw_partial_kernel(
    first_ref, rows_ref, heads_ref, out_hbm, teacher_ref, student_ref, target_ref, out_ref, sems
):
    tokens = rows_ref.shape[0]
    shards = out_ref.shape[0]
    wide = 8 * shards
    columns = heads_ref.shape[1]
    quarter = (out_ref.shape[2] - 128) // 3
    width = 4 * quarter
    teacher_width = heads_ref.shape[0] - width

    def iota(shape, dim):
        return lax.broadcasted_iota(jnp.int32, shape, dim)

    def dot(left, right, dims):
        return lax.dot_general(left, right, (dims, ((), ())), preferred_element_type=F32)

    copies = []

    def send_out(piece, start, size):
        lanes = pl.ds(start, size)
        copies.append(pltpu.make_async_copy(out_ref.at[:, :, lanes], out_hbm.at[:, :, lanes], sems.at[piece]))
        copies[-1].start()

    student = dot(rows_ref[:, teacher_width : teacher_width + width], heads_ref[teacher_width:, :], ((1,), (0,)))
    teacher = dot(rows_ref[:, :teacher_width], heads_ref[:teacher_width, :], ((1,), (0,)))
    code = rows_ref[:, teacher_width + width :].astype(F32)
    lane = iota(code.shape, 1)
    label = jnp.sum(jnp.where(lane == 0, code * 128.0, jnp.where(lane == 1, code, 0.0)), axis=1, keepdims=True)
    target = (label.astype(jnp.int32) == iota((tokens, columns), 1) + first_ref[...]).astype(F32)
    teacher_ref[...] = teacher
    student_ref[...] = student
    target_ref[...] = target

    def total(array):
        return jnp.sum(array, axis=1, keepdims=True)

    top_t = jnp.max(teacher, axis=1, keepdims=True)
    top_s = jnp.max(student, axis=1, keepdims=True)
    exp_t = jnp.exp(teacher - top_t)
    exp_s = jnp.exp(student - top_s)
    mass_t, mass_s = total(exp_t), total(exp_s)
    guess = jnp.abs(exp_s * (2.0 / mass_s) - exp_t / mass_t)
    lane = iota((tokens, columns), 1)
    largest = jnp.max(guess, axis=1, keepdims=True)
    where_largest = jnp.min(jnp.where(guess == largest, lane, columns), axis=1, keepdims=True)
    has_label = total(target)
    chosen = jnp.where(has_label > 0.5, target, (lane == where_largest).astype(F32))
    stats = [
        top_t,
        mass_t,
        total(exp_t * (teacher - student)),
        top_s,
        mass_s,
        total(chosen * student),
        total(chosen * teacher),
        has_label,
    ]
    lane = iota((tokens, 128), 1)
    table = jnp.zeros((tokens, 128), F32)
    for k, stat in enumerate(stats):
        table = jnp.where(lane % 8 == k, stat, table)
    first = table.astype(BF16).astype(F32)
    second = (table - first).astype(BF16).astype(F32)
    part = (lane % 32) // 8
    parts = jnp.where(
        part == 0, first, jnp.where(part == 1, second, jnp.where(part == 2, table - first - second, 0.0))
    ).astype(BF16)

    row, column = iota((wide, tokens), 0), iota((wide, tokens), 1)
    of_token = (column == (row // 8) * 2 + row % 2).astype(F32).astype(BF16)
    by_row = dot(of_token, parts, ((1,), (0,)))

    lane = iota((8, 128), 1)
    shared = jnp.zeros((8, 128), F32)
    wide_parts = parts.astype(F32)
    for group in range(tokens // 8):
        shared = jnp.where(lane // 32 == group + 1, wide_parts[8 * group : 8 * group + 8], shared)
    for shard in range(shards):
        block = jnp.where(lane < 32, by_row[8 * shard : 8 * shard + 8], shared)
        out_ref[shard, :, 3 * quarter :] = block.astype(BF16)
    send_out(0, 3 * quarter, 128)

    members = jnp.concatenate([exp_s * (1.0 - chosen), exp_t * (1.0 - chosen), chosen], axis=0)
    member_high = members.astype(BF16)
    member_low = (members - member_high.astype(F32)).astype(BF16)
    row, column = iota((wide, 3 * tokens), 0), iota((wide, 3 * tokens), 1)
    place = row % 8
    token = (row // 8) * 2 + row % 2
    pick = ((place < 6) & (column == (place // 2) * tokens + token)).astype(F32).astype(BF16)
    left = dot(pick, jnp.concatenate([member_high, member_low], axis=1), ((1,), (0,))).astype(BF16)
    left = jnp.concatenate([left[:, :columns], left[:, columns:]], axis=0)

    place = iota((wide, 1), 0) % 8
    chunks = quarter // LANES
    first_unsent = 0
    for chunk in range(chunks):
        starts = [teacher_width + j * quarter + chunk * LANES for j in range(4)]
        right = jnp.concatenate([heads_ref[start : start + LANES, :] for start in starts], axis=0)
        both = dot(left, right, ((1,), (1,)))
        exact = [both[:wide, j * LANES : (j + 1) * LANES] + both[wide:, j * LANES : (j + 1) * LANES] for j in range(4)]
        for j in range(3):
            sent = jnp.where(place >= 6, pltpu.roll(exact[3], 6 - 2 * j, 0), exact[j])
            lanes = slice((3 * chunk + j) * LANES, (3 * chunk + j + 1) * LANES)
            for shard in range(shards):
                out_ref[shard, :, lanes] = sent[8 * shard : 8 * shard + 8].astype(BF16)
        if chunk % 3 == 2 or chunk == chunks - 1:
            end = 3 * (chunk + 1) * LANES
            send_out(len(copies), first_unsent, end - first_unsent)
            first_unsent = end
    for copy in copies:
        copy.wait()


def sum_parts(tail):
    shards = tail.shape[0]
    flat = tail.astype(F32).reshape(shards * 8, 128)
    return flat + pltpu.roll(flat, 120, 1) + pltpu.roll(flat, 112, 1)


def fold(flat, lane):
    shards = flat.shape[0] // 8
    stats = [flat[:, lane + k : lane + k + 1].reshape(shards, 8, 1) for k in range(8)]
    top_t = jnp.max(stats[0], axis=0)
    factor_t = jnp.exp(stats[0] - top_t)
    top_s = jnp.max(stats[3], axis=0)
    factor_s = jnp.exp(stats[3] - top_s)
    mass_t = jnp.sum(stats[1] * factor_t, axis=0)
    mass_s = jnp.sum(stats[4] * factor_s, axis=0)
    return stats, top_t, factor_t, mass_t, top_s, factor_s, mass_s


def logit_grad_kernel(tail_ref, teacher_ref, student_ref, target_ref, out_ref):
    flat = sum_parts(tail_ref[...])
    folded = [fold(flat, 32 * group + 32) for group in range(out_ref.shape[0] // 8)]
    top_t, mass_t, top_s, mass_s = [jnp.concatenate([f[i] for f in folded], axis=0) for i in (1, 3, 4, 6)]
    teacher_prob = jnp.exp(teacher_ref[...] - top_t) / mass_t
    student_prob = jnp.exp(student_ref[...] - top_s) / mass_s
    out_ref[...] = (2.0 * student_prob - teacher_prob - target_ref[...]).astype(BF16)


def owner_kernel(arrived_ref, out_ref, loss_ref):
    shards, _, lanes = arrived_ref.shape
    quarter = (lanes - 128) // 3
    stats, top_t, factor_t, mass_t, top_s, factor_s, mass_s = fold(sum_parts(arrived_ref[:, :, 3 * quarter :]), 0)
    cross = jnp.sum(stats[2] * factor_t, axis=0)
    picked = jnp.sum(stats[7] * stats[5], axis=0)
    loss = cross / mass_t - top_t - jnp.log(mass_t) + 2.0 * (top_s + jnp.log(mass_s)) - picked
    token = lax.broadcasted_iota(jnp.int32, (8, 1), 0)
    for t in range(out_ref.shape[0]):
        loss_ref[t] = jnp.sum(jnp.where(token == t, loss, 0.0))
    chosen_s = jnp.exp(stats[5] - top_s) / mass_s
    chosen_t = jnp.exp(stats[6] - top_t) / mass_t
    weight_l = (2.0 * chosen_s - chosen_t - stats[7]).astype(BF16).astype(F32)
    weight_s = 2.0 * (factor_s / mass_s)
    weight_t = -(factor_t / mass_t)
    place = lax.broadcasted_iota(jnp.int32, (shards, 8, 1), 1)
    last = jnp.zeros((8, quarter), F32)
    for j, weight_last in enumerate((weight_s, weight_t, weight_l)):
        weight = jnp.where(
            place < 2, weight_s, jnp.where(place < 4, weight_t, jnp.where(place < 6, weight_l, weight_last))
        )
        piece = []
        for chunk in range(quarter // LANES):
            lanes = slice((3 * chunk + j) * LANES, (3 * chunk + j + 1) * LANES)
            piece.append(sum(weight[shard] * arrived_ref[shard, :, lanes].astype(F32) for shard in range(shards)))
        piece = jnp.concatenate(piece, axis=1)
        last += piece
        out_ref[:, j * quarter : (j + 1) * quarter] = piece[0:2] + piece[2:4] + piece[4:6]
    out_ref[:, 3 * quarter :] = last[6:8]


def head_grad_kernel(hidden_ref, hidden_other_ref, grad_ref, other_ref, out_ref, total_ref, sems):
    grads = jnp.concatenate([grad_ref[...], other_ref[...]], axis=0)
    size = hidden_ref.shape[1] // PIECES
    copies = []
    for piece in range(PIECES):
        rows = pl.ds(piece * size, size)
        hidden = jnp.concatenate([hidden_ref[:, rows], hidden_other_ref[:, rows]], axis=0)
        total_ref[rows, :] = lax.dot_general(hidden, grads, (((0,), (0,)), ((), ())), preferred_element_type=F32)
        copies.append(pltpu.make_async_copy(total_ref.at[rows, :], out_ref.at[rows, :], sems.at[piece]))
        copies[-1].start()
    for copy in copies:
        copy.wait()


def two_exchanges(teacher_hidden, student_hidden, teacher_head, student_head, labels, *, shards):
    own = labels.shape[0]
    teacher_width, width = teacher_hidden.shape[1], student_hidden.shape[1]
    columns_here = student_head.shape[1]
    tokens = shards * own
    quarter = width // 4
    here = lax.axis_index("vocab").astype(jnp.int32)
    rows = gather_tokens(teacher_hidden, student_hidden, labels, shards).reshape(tokens, -1)
    student_rows = rows[:, teacher_width : teacher_width + width]
    other = [(0, 1), (1, 0)]
    student_other = lax.ppermute(student_rows, "rows", other)

    first_column = jnp.full((1, columns_here), here * columns_here, jnp.int32)
    heads = jnp.concatenate([teacher_head, student_head], axis=0)
    square = jax.ShapeDtypeStruct((tokens, columns_here), F32)
    payload, teacher_logits, student_logits, target = pl.pallas_call(
        raw_partial_kernel,
        out_shape=(jax.ShapeDtypeStruct((shards, 8, 3 * quarter + 128), BF16), square, square, square),
        in_specs=[VMEM, VMEM, VMEM],
        out_specs=(ANY, VMEM, VMEM, VMEM),
        scratch_shapes=[pltpu.VMEM((shards, 8, 3 * quarter + 128), BF16), pltpu.SemaphoreType.DMA((2 + quarter // LANES // 3,))],
        compiler_params=SMALL,
    )(first_column, rows, heads)
    arrived = swap(payload)
    grad_rows = pl.pallas_call(
        logit_grad_kernel,
        out_shape=jax.ShapeDtypeStruct((tokens, columns_here), BF16),
        in_specs=[VMEM] * 4,
        out_specs=VMEM,
        compiler_params=SMALL,
    )(arrived[:, :, 3 * quarter :], teacher_logits, student_logits, target)
    grad_other = lax.ppermute(grad_rows, "rows", other)
    hidden_grad, token_loss = pl.pallas_call(
        owner_kernel,
        out_shape=(jax.ShapeDtypeStruct((own, width), F32), jax.ShapeDtypeStruct((own,), F32)),
        in_specs=[VMEM],
        out_specs=(VMEM, SMEM),
        compiler_params=SMALL,
    )(arrived)
    head_grad = pl.pallas_call(
        head_grad_kernel,
        out_shape=jax.ShapeDtypeStruct((width, columns_here), F32),
        in_specs=[VMEM] * 4,
        out_specs=ANY,
        scratch_shapes=[pltpu.VMEM((width, columns_here), F32), pltpu.SemaphoreType.DMA((PIECES,))],
        compiler_params=SMALL,
    )(student_rows, student_other, grad_rows, grad_other)
    return (token_loss, hidden_grad, head_grad)


def three_exchanges(teacher_hidden, student_hidden, teacher_head, student_head, labels, *, shards):
    own = labels.shape[0]
    student_width = student_hidden.shape[1]
    columns_here = student_head.shape[1]
    first_column = lax.axis_index("vocab") * columns_here
    rows = gather_tokens(teacher_hidden, student_hidden, labels, shards).reshape(shards * own, -1)
    teacher_width = teacher_hidden.shape[1]
    teacher_rows = rows[:, :teacher_width]
    student_rows = rows[:, teacher_width : teacher_width + student_width]
    code = rows[:, teacher_width + student_width :].astype(jnp.int32)
    label_rows = code[:, 0] * 128 + code[:, 1]
    other = [(0, 1), (1, 0)]
    student_other = lax.ppermute(student_rows, "rows", other)

    teacher_logits = jnp.dot(teacher_rows, teacher_head, preferred_element_type=F32)
    student_logits = jnp.dot(student_rows, student_head, preferred_element_type=F32)
    columns = lax.broadcasted_iota(jnp.int32, student_logits.shape, 1)
    target = (label_rows - first_column)[:, None] == columns
    top_t = jnp.max(teacher_logits, axis=1, keepdims=True)
    exp_t = jnp.exp(teacher_logits - top_t)
    top_s = jnp.max(student_logits, axis=1, keepdims=True)
    exp_s = jnp.exp(student_logits - top_s)
    stats = jnp.concatenate(
        [
            top_t,
            jnp.sum(exp_t, axis=1, keepdims=True),
            jnp.sum(exp_t * (teacher_logits - student_logits), axis=1, keepdims=True),
            top_s,
            jnp.sum(exp_s, axis=1, keepdims=True),
            jnp.sum(jnp.where(target, student_logits, 0.0), axis=1, keepdims=True),
        ],
        axis=1,
    )
    every = swap(jnp.broadcast_to(stats[None], (shards,) + stats.shape))
    all_top_t = jnp.max(every[:, :, 0], axis=0)
    factor_t = jnp.exp(every[:, :, 0] - all_top_t[None])
    all_top_s = jnp.max(every[:, :, 3], axis=0)
    factor_s = jnp.exp(every[:, :, 3] - all_top_s[None])
    mass_t = jnp.sum(every[:, :, 1] * factor_t, axis=0)
    cross = jnp.sum(every[:, :, 2] * factor_t, axis=0)
    mass_s = jnp.sum(every[:, :, 4] * factor_s, axis=0)
    picked = jnp.sum(every[:, :, 5], axis=0)
    loss = cross / mass_t - all_top_t - jnp.log(mass_t) + 2.0 * (all_top_s + jnp.log(mass_s)) - picked
    token_loss = lax.dynamic_slice_in_dim(loss, lax.axis_index("vocab") * own, own, 0)

    teacher_prob = jnp.exp(teacher_logits - all_top_t[:, None]) / mass_t[:, None]
    student_prob = jnp.exp(student_logits - all_top_s[:, None]) / mass_s[:, None]
    grad_rows = (2.0 * student_prob - teacher_prob - target.astype(F32)).astype(BF16)
    grad_other = lax.ppermute(grad_rows, "rows", other)
    partial = lax.dot_general(grad_rows, student_head, (((1,), (1,)), ((), ())), preferred_element_type=F32)
    arrived = swap(partial.astype(BF16).reshape(shards, own, student_width))
    hidden_grad = jnp.sum(arrived.astype(F32), axis=0)
    head_grad = lax.dot_general(
        jnp.concatenate([student_rows, student_other], axis=0),
        jnp.concatenate([grad_rows, grad_other], axis=0),
        (((0,), (0,)), ((), ())),
        preferred_element_type=F32,
    )
    return (token_loss, hidden_grad, head_grad)


def solution(mesh):
    tokens = ("groups", "vocab", "rows")
    in_specs = (P(tokens, None), P(tokens, None), P(None, "vocab"), P(None, "vocab"), P(tokens))
    out_specs = (P(tokens), P(tokens, None), P("groups", "vocab"))

    def body(*arrays):
        shards = mesh.shape["vocab"]
        own = arrays[4].shape[0]
        small = own == 2 and shards % 4 == 0 and shards * own <= 24
        return (two_exchanges if small else three_exchanges)(*arrays, shards=shards)

    return jax.shard_map(body, mesh=mesh, in_specs=in_specs, out_specs=out_specs, check_vma=False)
```

```python
import jax
import jax.numpy as jnp
from jax import lax
from jax.experimental import pallas as pl
from jax.experimental.pallas import tpu as pltpu
from jax.sharding import PartitionSpec as P

F32 = jnp.float32
BF16 = jnp.bfloat16
CODE = 128


UNROLL = 16
LANES = 512
PIECES = 7
SMEM = pl.BlockSpec(memory_space=pltpu.SMEM)
VMEM = pl.BlockSpec(memory_space=pltpu.VMEM)
ANY = pl.BlockSpec(memory_space=pl.ANY)
SMALL = pltpu.CompilerParams(vmem_limit_bytes=16 * 1024 * 1024)


def over_shards(shards, body):
    if shards <= UNROLL:
        for shard in range(shards):
            body(shard)
    else:
        pl.loop(0, shards)(body)


def swap(blocks):
    return lax.all_to_all(blocks, "vocab", split_axis=0, concat_axis=0, tiled=True)


def payload_kernel(labels_ref, teacher_ref, student_ref, out_ref):
    shards, own, _ = out_ref.shape
    teacher_width, student_width = teacher_ref.shape[1], student_ref.shape[1]
    teacher = teacher_ref[...]
    student = student_ref[...]
    code = label_digits(labels_ref, own)

    def write(shard):
        out_ref[shard, :, :teacher_width] = teacher
        out_ref[shard, :, teacher_width : teacher_width + student_width] = student
        out_ref[shard, :, teacher_width + student_width :] = code

    over_shards(shards, write)


def label_digits(labels_ref, own):
    row = lax.broadcasted_iota(jnp.int32, (own, CODE), 0)
    lane = lax.broadcasted_iota(jnp.int32, (own, CODE), 1)
    digits = jnp.zeros((own, CODE), jnp.int32)
    for token in range(own):
        label = labels_ref[token]
        pair = jnp.where(lane == 0, label >> 7, label & 127)
        digits = jnp.where(row == token, pair, digits)
    return digits.astype(F32).astype(BF16)


def gather_tokens(teacher_hidden, student_hidden, labels, shards):
    own, teacher_width = teacher_hidden.shape
    student_width = student_hidden.shape[1]
    payload = pl.pallas_call(
        payload_kernel,
        out_shape=jax.ShapeDtypeStruct((shards, own, teacher_width + student_width + CODE), BF16),
        in_specs=[SMEM, VMEM, VMEM],
        out_specs=VMEM,
    )(labels, teacher_hidden, student_hidden)
    return swap(payload)


def raw_partial_kernel(
    first_ref, rows_ref, heads_ref, out_hbm, teacher_ref, student_ref, target_ref, out_ref, sems
):
    tokens = rows_ref.shape[0]
    shards = out_ref.shape[0]
    wide = 8 * shards
    columns = heads_ref.shape[1]
    width = out_ref.shape[2] - 128
    teacher_width = heads_ref.shape[0] - width

    def iota(shape, dim):
        return lax.broadcasted_iota(jnp.int32, shape, dim)

    def dot(left, right, dims):
        return lax.dot_general(left, right, (dims, ((), ())), preferred_element_type=F32)

    copies = []

    def send_out(piece, start, size):
        lanes = pl.ds(start, size)
        copies.append(pltpu.make_async_copy(out_ref.at[:, :, lanes], out_hbm.at[:, :, lanes], sems.at[piece]))
        copies[-1].start()

    student = dot(rows_ref[:, teacher_width : teacher_width + width], heads_ref[teacher_width:, :], ((1,), (0,)))
    teacher = dot(rows_ref[:, :teacher_width], heads_ref[:teacher_width, :], ((1,), (0,)))
    code = rows_ref[:, teacher_width + width :].astype(F32)
    lane = iota(code.shape, 1)
    label = jnp.sum(jnp.where(lane == 0, code * 128.0, jnp.where(lane == 1, code, 0.0)), axis=1, keepdims=True)
    target = (label.astype(jnp.int32) == iota((tokens, columns), 1) + first_ref[...]).astype(F32)
    teacher_ref[...] = teacher
    student_ref[...] = student
    target_ref[...] = target

    def total(array):
        return jnp.sum(array, axis=1, keepdims=True)

    top_t = jnp.max(teacher, axis=1, keepdims=True)
    top_s = jnp.max(student, axis=1, keepdims=True)
    exp_t = jnp.exp(teacher - top_t)
    exp_s = jnp.exp(student - top_s)
    mass_t, mass_s = total(exp_t), total(exp_s)
    guess = jnp.abs(exp_s * (2.0 / mass_s) - exp_t / mass_t)
    lane = iota((tokens, columns), 1)

    def largest(values):
        at_top = values == jnp.max(values, axis=1, keepdims=True)
        return (lane == jnp.min(jnp.where(at_top, lane, columns), axis=1, keepdims=True)).astype(F32)

    has_label = total(target)
    chosen = jnp.where(has_label > 0.5, target, largest(guess))
    second_chosen = largest(jnp.where(chosen > 0.5, -1.0, guess))
    rest = 1.0 - chosen - second_chosen
    stats = [
        top_t,
        mass_t,
        total(exp_t * (teacher - student)),
        top_s,
        mass_s,
        total(chosen * student),
        total(chosen * teacher),
        has_label,
    ]
    lane = iota((tokens, 128), 1)
    table = jnp.zeros((tokens, 128), F32)
    for k, stat in enumerate(stats):
        table = jnp.where(lane % 8 == k, stat, table)
    first = table.astype(BF16).astype(F32)
    second = (table - first).astype(BF16).astype(F32)
    part = (lane % 32) // 8
    parts = jnp.where(part == 0, first, jnp.where(part == 1, second, table - first - second))
    slot = lane % 32 - 24
    for place, values in enumerate((student, teacher)):
        value = total(second_chosen * values)
        high = value.astype(BF16).astype(F32)
        middle = (value - high).astype(BF16).astype(F32)
        for k, piece in enumerate((high, middle, value - high - middle)):
            parts = jnp.where(slot == 3 * place + k, piece, parts)
    parts = jnp.where(slot >= 6, 0.0, parts).astype(BF16)

    row, column = iota((wide, tokens), 0), iota((wide, tokens), 1)
    of_token = (column == (row // 8) * 2 + row % 2).astype(F32).astype(BF16)
    by_row = dot(of_token, parts, ((1,), (0,)))

    lane = iota((8, 128), 1)
    shared = jnp.zeros((8, 128), F32)
    wide_parts = parts.astype(F32)
    for group in range(tokens // 8):
        shared = jnp.where(lane // 32 == group + 1, wide_parts[8 * group : 8 * group + 8], shared)
    for shard in range(shards):
        block = jnp.where(lane < 32, by_row[8 * shard : 8 * shard + 8], shared)
        out_ref[shard, :, width:] = block.astype(BF16)
    send_out(0, width, 128)

    members = jnp.concatenate([exp_s * rest, exp_t * rest, chosen, second_chosen], axis=0)
    member_high = members.astype(BF16)
    member_low = (members - member_high.astype(F32)).astype(BF16)
    row, column = iota((wide, 4 * tokens), 0), iota((wide, 4 * tokens), 1)
    of_member = column == ((row % 8) // 2) * tokens + (row // 8) * 2 + row % 2
    pick = of_member.astype(F32).astype(BF16)
    left = dot(pick, jnp.concatenate([member_high, member_low], axis=1), ((1,), (0,))).astype(BF16)
    left = jnp.concatenate([left[:, :columns], left[:, columns:]], axis=0)

    for start in range(0, width, LANES):
        head = heads_ref[teacher_width + start : teacher_width + start + LANES, :]
        both = dot(left, head, ((1,), (1,)))
        sent = both[:wide] + both[wide:]
        for shard in range(shards):
            out_ref[shard, :, start : start + LANES] = sent[8 * shard : 8 * shard + 8].astype(BF16)
        send_out(1 + start // LANES, start, LANES)
    for copy in copies:
        copy.wait()


def sum_parts(tail):
    shards = tail.shape[0]
    flat = tail.astype(F32).reshape(shards * 8, 128)
    return flat + pltpu.roll(flat, 120, 1) + pltpu.roll(flat, 112, 1)


def fold(flat, lane):
    shards = flat.shape[0] // 8
    stats = [flat[:, lane + k : lane + k + 1].reshape(shards, 8, 1) for k in range(8)]
    top_t = jnp.max(stats[0], axis=0)
    factor_t = jnp.exp(stats[0] - top_t)
    top_s = jnp.max(stats[3], axis=0)
    factor_s = jnp.exp(stats[3] - top_s)
    mass_t = jnp.sum(stats[1] * factor_t, axis=0)
    mass_s = jnp.sum(stats[4] * factor_s, axis=0)
    return stats, top_t, factor_t, mass_t, top_s, factor_s, mass_s


def logit_grad_kernel(tail_ref, teacher_ref, student_ref, target_ref, out_ref):
    flat = sum_parts(tail_ref[...])
    folded = [fold(flat, 32 * group + 32) for group in range(out_ref.shape[0] // 8)]
    top_t, mass_t, top_s, mass_s = [jnp.concatenate([f[i] for f in folded], axis=0) for i in (1, 3, 4, 6)]
    teacher_prob = jnp.exp(teacher_ref[...] - top_t) / mass_t
    student_prob = jnp.exp(student_ref[...] - top_s) / mass_s
    out_ref[...] = (2.0 * student_prob - teacher_prob - target_ref[...]).astype(BF16)


def owner_kernel(arrived_ref, out_ref, loss_ref):
    shards, _, lanes = arrived_ref.shape
    width = lanes - 128
    tail = arrived_ref[:, :, width:]
    stats, top_t, factor_t, mass_t, top_s, factor_s, mass_s = fold(sum_parts(tail), 0)
    extra = [tail[:, :, k : k + 1].astype(F32) for k in range(24, 30)]
    cross = jnp.sum(stats[2] * factor_t, axis=0)
    picked = jnp.sum(stats[7] * stats[5], axis=0)
    loss = cross / mass_t - top_t - jnp.log(mass_t) + 2.0 * (top_s + jnp.log(mass_s)) - picked
    token = lax.broadcasted_iota(jnp.int32, (8, 1), 0)
    for t in range(out_ref.shape[0]):
        loss_ref[t] = jnp.sum(jnp.where(token == t, loss, 0.0))
    def entry(student, teacher, label):
        prob_s = jnp.exp(student - top_s) / mass_s
        prob_t = jnp.exp(teacher - top_t) / mass_t
        return (2.0 * prob_s - prob_t - label).astype(BF16).astype(F32)

    chosen = entry(stats[5], stats[6], stats[7])
    second_chosen = entry(extra[0] + extra[1] + extra[2], extra[3] + extra[4] + extra[5], 0.0)
    place = lax.broadcasted_iota(jnp.int32, (shards, 8, 1), 1)
    weight = jnp.where(
        place < 2,
        2.0 * (factor_s / mass_s),
        jnp.where(place < 4, -(factor_t / mass_t), jnp.where(place < 6, chosen, second_chosen)),
    )
    for start in range(0, width, LANES):
        lanes = slice(start, start + LANES)
        piece = sum(weight[shard] * arrived_ref[shard, :, lanes].astype(F32) for shard in range(shards))
        out_ref[:, lanes] = piece[0:2] + piece[2:4] + piece[4:6] + piece[6:8]


def head_grad_kernel(hidden_ref, hidden_other_ref, grad_ref, other_ref, out_ref, total_ref, sems):
    grads = jnp.concatenate([grad_ref[...], other_ref[...]], axis=0)
    size = hidden_ref.shape[1] // PIECES
    copies = []
    for piece in range(PIECES):
        rows = pl.ds(piece * size, size)
        hidden = jnp.concatenate([hidden_ref[:, rows], hidden_other_ref[:, rows]], axis=0)
        total_ref[rows, :] = lax.dot_general(hidden, grads, (((0,), (0,)), ((), ())), preferred_element_type=F32)
        copies.append(pltpu.make_async_copy(total_ref.at[rows, :], out_ref.at[rows, :], sems.at[piece]))
        copies[-1].start()
    for copy in copies:
        copy.wait()


def two_exchanges(teacher_hidden, student_hidden, teacher_head, student_head, labels, *, shards):
    own = labels.shape[0]
    teacher_width, width = teacher_hidden.shape[1], student_hidden.shape[1]
    columns_here = student_head.shape[1]
    tokens = shards * own
    here = lax.axis_index("vocab").astype(jnp.int32)
    rows = gather_tokens(teacher_hidden, student_hidden, labels, shards).reshape(tokens, -1)
    student_rows = rows[:, teacher_width : teacher_width + width]
    other = [(0, 1), (1, 0)]
    student_other = lax.ppermute(student_rows, "rows", other)

    first_column = jnp.full((1, columns_here), here * columns_here, jnp.int32)
    heads = jnp.concatenate([teacher_head, student_head], axis=0)
    square = jax.ShapeDtypeStruct((tokens, columns_here), F32)
    payload, teacher_logits, student_logits, target = pl.pallas_call(
        raw_partial_kernel,
        out_shape=(jax.ShapeDtypeStruct((shards, 8, width + 128), BF16), square, square, square),
        in_specs=[VMEM, VMEM, VMEM],
        out_specs=(ANY, VMEM, VMEM, VMEM),
        scratch_shapes=[pltpu.VMEM((shards, 8, width + 128), BF16), pltpu.SemaphoreType.DMA((1 + width // LANES,))],
        compiler_params=SMALL,
    )(first_column, rows, heads)
    arrived = swap(payload)
    grad_rows = pl.pallas_call(
        logit_grad_kernel,
        out_shape=jax.ShapeDtypeStruct((tokens, columns_here), BF16),
        in_specs=[VMEM] * 4,
        out_specs=VMEM,
        compiler_params=SMALL,
    )(arrived[:, :, width:], teacher_logits, student_logits, target)
    grad_other = lax.ppermute(grad_rows, "rows", other)
    hidden_grad, token_loss = pl.pallas_call(
        owner_kernel,
        out_shape=(jax.ShapeDtypeStruct((own, width), F32), jax.ShapeDtypeStruct((own,), F32)),
        in_specs=[VMEM],
        out_specs=(VMEM, SMEM),
        compiler_params=SMALL,
    )(arrived)
    head_grad = pl.pallas_call(
        head_grad_kernel,
        out_shape=jax.ShapeDtypeStruct((width, columns_here), F32),
        in_specs=[VMEM] * 4,
        out_specs=ANY,
        scratch_shapes=[pltpu.VMEM((width, columns_here), F32), pltpu.SemaphoreType.DMA((PIECES,))],
        compiler_params=SMALL,
    )(student_rows, student_other, grad_rows, grad_other)
    return (token_loss, hidden_grad, head_grad)


def three_exchanges(teacher_hidden, student_hidden, teacher_head, student_head, labels, *, shards):
    own = labels.shape[0]
    student_width = student_hidden.shape[1]
    columns_here = student_head.shape[1]
    first_column = lax.axis_index("vocab") * columns_here
    rows = gather_tokens(teacher_hidden, student_hidden, labels, shards).reshape(shards * own, -1)
    teacher_width = teacher_hidden.shape[1]
    teacher_rows = rows[:, :teacher_width]
    student_rows = rows[:, teacher_width : teacher_width + student_width]
    code = rows[:, teacher_width + student_width :].astype(jnp.int32)
    label_rows = code[:, 0] * 128 + code[:, 1]
    other = [(0, 1), (1, 0)]
    student_other = lax.ppermute(student_rows, "rows", other)

    teacher_logits = jnp.dot(teacher_rows, teacher_head, preferred_element_type=F32)
    student_logits = jnp.dot(student_rows, student_head, preferred_element_type=F32)
    columns = lax.broadcasted_iota(jnp.int32, student_logits.shape, 1)
    target = (label_rows - first_column)[:, None] == columns
    top_t = jnp.max(teacher_logits, axis=1, keepdims=True)
    exp_t = jnp.exp(teacher_logits - top_t)
    top_s = jnp.max(student_logits, axis=1, keepdims=True)
    exp_s = jnp.exp(student_logits - top_s)
    stats = jnp.concatenate(
        [
            top_t,
            jnp.sum(exp_t, axis=1, keepdims=True),
            jnp.sum(exp_t * (teacher_logits - student_logits), axis=1, keepdims=True),
            top_s,
            jnp.sum(exp_s, axis=1, keepdims=True),
            jnp.sum(jnp.where(target, student_logits, 0.0), axis=1, keepdims=True),
        ],
        axis=1,
    )
    every = swap(jnp.broadcast_to(stats[None], (shards,) + stats.shape))
    all_top_t = jnp.max(every[:, :, 0], axis=0)
    factor_t = jnp.exp(every[:, :, 0] - all_top_t[None])
    all_top_s = jnp.max(every[:, :, 3], axis=0)
    factor_s = jnp.exp(every[:, :, 3] - all_top_s[None])
    mass_t = jnp.sum(every[:, :, 1] * factor_t, axis=0)
    cross = jnp.sum(every[:, :, 2] * factor_t, axis=0)
    mass_s = jnp.sum(every[:, :, 4] * factor_s, axis=0)
    picked = jnp.sum(every[:, :, 5], axis=0)
    loss = cross / mass_t - all_top_t - jnp.log(mass_t) + 2.0 * (all_top_s + jnp.log(mass_s)) - picked
    token_loss = lax.dynamic_slice_in_dim(loss, lax.axis_index("vocab") * own, own, 0)

    teacher_prob = jnp.exp(teacher_logits - all_top_t[:, None]) / mass_t[:, None]
    student_prob = jnp.exp(student_logits - all_top_s[:, None]) / mass_s[:, None]
    grad_rows = (2.0 * student_prob - teacher_prob - target.astype(F32)).astype(BF16)
    grad_other = lax.ppermute(grad_rows, "rows", other)
    partial = lax.dot_general(grad_rows, student_head, (((1,), (1,)), ((), ())), preferred_element_type=F32)
    arrived = swap(partial.astype(BF16).reshape(shards, own, student_width))
    hidden_grad = jnp.sum(arrived.astype(F32), axis=0)
    head_grad = lax.dot_general(
        jnp.concatenate([student_rows, student_other], axis=0),
        jnp.concatenate([grad_rows, grad_other], axis=0),
        (((0,), (0,)), ((), ())),
        preferred_element_type=F32,
    )
    return (token_loss, hidden_grad, head_grad)


def solution(mesh):
    tokens = ("groups", "vocab", "rows")
    in_specs = (P(tokens, None), P(tokens, None), P(None, "vocab"), P(None, "vocab"), P(tokens))
    out_specs = (P(tokens), P(tokens, None), P("groups", "vocab"))

    def body(*arrays):
        shards = mesh.shape["vocab"]
        own = arrays[4].shape[0]
        small = own == 2 and shards % 4 == 0 and shards * own <= 24
        return (two_exchanges if small else three_exchanges)(*arrays, shards=shards)

    return jax.shard_map(body, mesh=mesh, in_specs=in_specs, out_specs=out_specs, check_vma=False)
```

```python
import jax
import jax.numpy as jnp
from jax import lax
from jax.experimental import pallas as pl
from jax.experimental.pallas import tpu as pltpu
from jax.sharding import PartitionSpec as P

F32 = jnp.float32
BF16 = jnp.bfloat16
CODE = 128


UNROLL = 16
LANES = 128
PIECES = 7
SMEM = pl.BlockSpec(memory_space=pltpu.SMEM)
VMEM = pl.BlockSpec(memory_space=pltpu.VMEM)
ANY = pl.BlockSpec(memory_space=pl.ANY)
SMALL = pltpu.CompilerParams(vmem_limit_bytes=16 * 1024 * 1024)


def over_shards(shards, body):
    if shards <= UNROLL:
        for shard in range(shards):
            body(shard)
    else:
        pl.loop(0, shards)(body)


def swap(blocks):
    return lax.all_to_all(blocks, "vocab", split_axis=0, concat_axis=0, tiled=True)


def payload_kernel(labels_ref, teacher_ref, student_ref, out_ref):
    shards, own, _ = out_ref.shape
    teacher_width, student_width = teacher_ref.shape[1], student_ref.shape[1]
    teacher = teacher_ref[...]
    student = student_ref[...]
    code = label_digits(labels_ref, own)

    def write(shard):
        out_ref[shard, :, :teacher_width] = teacher
        out_ref[shard, :, teacher_width : teacher_width + student_width] = student
        out_ref[shard, :, teacher_width + student_width :] = code

    over_shards(shards, write)


def label_digits(labels_ref, own):
    row = lax.broadcasted_iota(jnp.int32, (own, CODE), 0)
    lane = lax.broadcasted_iota(jnp.int32, (own, CODE), 1)
    digits = jnp.zeros((own, CODE), jnp.int32)
    for token in range(own):
        label = labels_ref[token]
        pair = jnp.where(lane == 0, label >> 7, label & 127)
        digits = jnp.where(row == token, pair, digits)
    return digits.astype(F32).astype(BF16)


def payload_copy_kernel(labels_ref, teacher_ref, student_ref, out_hbm, block_ref, sems):
    shards, own, _ = out_hbm.shape
    teacher_width, student_width = teacher_ref.shape[1], student_ref.shape[1]
    block_ref[:, :teacher_width] = teacher_ref[...]
    block_ref[:, teacher_width : teacher_width + student_width] = student_ref[...]
    block_ref[:, teacher_width + student_width :] = label_digits(labels_ref, own)
    copies = [pltpu.make_async_copy(block_ref, out_hbm.at[shard], sems.at[shard]) for shard in range(shards)]
    for copy in copies:
        copy.start()
    for copy in copies:
        copy.wait()


def gather_tokens(teacher_hidden, student_hidden, labels, shards):
    own, teacher_width = teacher_hidden.shape
    student_width = student_hidden.shape[1]
    width = teacher_width + student_width + CODE
    few = shards <= UNROLL
    payload = pl.pallas_call(
        payload_copy_kernel if few else payload_kernel,
        out_shape=jax.ShapeDtypeStruct((shards, own, width), BF16),
        in_specs=[SMEM, VMEM, VMEM],
        out_specs=ANY if few else VMEM,
        scratch_shapes=[pltpu.VMEM((own, width), BF16), pltpu.SemaphoreType.DMA((shards,))] if few else [],
    )(labels, teacher_hidden, student_hidden)
    return swap(payload)


def raw_partial_kernel(
    first_ref, rows_ref, heads_ref, out_hbm, teacher_ref, student_ref, target_ref, out_ref, sems
):
    tokens = rows_ref.shape[0]
    shards = out_ref.shape[0]
    wide = 8 * shards
    columns = heads_ref.shape[1]
    quarter = (out_ref.shape[2] - 128) // 3
    width = 4 * quarter
    teacher_width = heads_ref.shape[0] - width

    def iota(shape, dim):
        return lax.broadcasted_iota(jnp.int32, shape, dim)

    def dot(left, right, dims):
        return lax.dot_general(left, right, (dims, ((), ())), preferred_element_type=F32)

    copies = []

    def send_out(piece, start, size):
        lanes = pl.ds(start, size)
        copies.append(pltpu.make_async_copy(out_ref.at[:, :, lanes], out_hbm.at[:, :, lanes], sems.at[piece]))
        copies[-1].start()

    student = dot(rows_ref[:, teacher_width : teacher_width + width], heads_ref[teacher_width:, :], ((1,), (0,)))
    teacher = dot(rows_ref[:, :teacher_width], heads_ref[:teacher_width, :], ((1,), (0,)))
    code = rows_ref[:, teacher_width + width :].astype(F32)
    lane = iota(code.shape, 1)
    label = jnp.sum(jnp.where(lane == 0, code * 128.0, jnp.where(lane == 1, code, 0.0)), axis=1, keepdims=True)
    target = (label.astype(jnp.int32) == iota((tokens, columns), 1) + first_ref[...]).astype(F32)
    teacher_ref[...] = teacher
    student_ref[...] = student
    target_ref[...] = target

    def total(array):
        return jnp.sum(array, axis=1, keepdims=True)

    top_t = jnp.max(teacher, axis=1, keepdims=True)
    top_s = jnp.max(student, axis=1, keepdims=True)
    exp_t = jnp.exp(teacher - top_t)
    exp_s = jnp.exp(student - top_s)
    mass_t, mass_s = total(exp_t), total(exp_s)
    guess = jnp.abs(exp_s * (2.0 / mass_s) - exp_t / mass_t)
    lane = iota((tokens, columns), 1)
    largest = jnp.max(guess, axis=1, keepdims=True)
    where_largest = jnp.min(jnp.where(guess == largest, lane, columns), axis=1, keepdims=True)
    has_label = total(target)
    chosen = jnp.where(has_label > 0.5, target, (lane == where_largest).astype(F32))
    stats = [
        top_t,
        mass_t,
        total(exp_t * (teacher - student)),
        top_s,
        mass_s,
        total(chosen * student),
        total(chosen * teacher),
        has_label,
    ]
    lane = iota((tokens, 128), 1)
    table = jnp.zeros((tokens, 128), F32)
    for k, stat in enumerate(stats):
        table = jnp.where(lane % 8 == k, stat, table)
    first = table.astype(BF16).astype(F32)
    second = (table - first).astype(BF16).astype(F32)
    part = (lane % 32) // 8
    parts = jnp.where(
        part == 0, first, jnp.where(part == 1, second, jnp.where(part == 2, table - first - second, 0.0))
    ).astype(BF16)

    row, column = iota((wide, tokens), 0), iota((wide, tokens), 1)
    of_token = (column == (row // 8) * 2 + row % 2).astype(F32).astype(BF16)
    by_row = dot(of_token, parts, ((1,), (0,)))

    lane = iota((8, 128), 1)
    shared = jnp.zeros((8, 128), F32)
    wide_parts = parts.astype(F32)
    for group in range(tokens // 8):
        shared = jnp.where(lane // 32 == group + 1, wide_parts[8 * group : 8 * group + 8], shared)
    for shard in range(shards):
        block = jnp.where(lane < 32, by_row[8 * shard : 8 * shard + 8], shared)
        out_ref[shard, :, 3 * quarter :] = block.astype(BF16)
    send_out(0, 3 * quarter, 128)

    members = jnp.concatenate([exp_s * (1.0 - chosen), exp_t * (1.0 - chosen), chosen], axis=0)
    member_high = members.astype(BF16)
    member_low = (members - member_high.astype(F32)).astype(BF16)
    row, column = iota((wide, 3 * tokens), 0), iota((wide, 3 * tokens), 1)
    place = row % 8
    token = (row // 8) * 2 + row % 2
    pick = ((place < 6) & (column == (place // 2) * tokens + token)).astype(F32).astype(BF16)
    left = dot(pick, jnp.concatenate([member_high, member_low], axis=1), ((1,), (0,))).astype(BF16)
    left = jnp.concatenate([left[:, :columns], left[:, columns:]], axis=0)

    place = iota((wide, 1), 0) % 8
    chunks = quarter // LANES
    first_unsent = 0
    for chunk in range(chunks):
        starts = [teacher_width + j * quarter + chunk * LANES for j in range(4)]
        right = jnp.concatenate([heads_ref[start : start + LANES, :] for start in starts], axis=0)
        both = dot(left, right, ((1,), (1,)))
        exact = [both[:wide, j * LANES : (j + 1) * LANES] + both[wide:, j * LANES : (j + 1) * LANES] for j in range(4)]
        for j in range(3):
            sent = jnp.where(place >= 6, pltpu.roll(exact[3], 6 - 2 * j, 0), exact[j])
            lanes = slice((3 * chunk + j) * LANES, (3 * chunk + j + 1) * LANES)
            for shard in range(shards):
                out_ref[shard, :, lanes] = sent[8 * shard : 8 * shard + 8].astype(BF16)
        if chunk % 3 == 2 or chunk == chunks - 1:
            end = 3 * (chunk + 1) * LANES
            send_out(len(copies), first_unsent, end - first_unsent)
            first_unsent = end
    for copy in copies:
        copy.wait()


def sum_parts(tail):
    shards = tail.shape[0]
    flat = tail.astype(F32).reshape(shards * 8, 128)
    return flat + pltpu.roll(flat, 120, 1) + pltpu.roll(flat, 112, 1)


def fold(flat, lane):
    shards = flat.shape[0] // 8
    stats = [flat[:, lane + k : lane + k + 1].reshape(shards, 8, 1) for k in range(8)]
    top_t = jnp.max(stats[0], axis=0)
    factor_t = jnp.exp(stats[0] - top_t)
    top_s = jnp.max(stats[3], axis=0)
    factor_s = jnp.exp(stats[3] - top_s)
    mass_t = jnp.sum(stats[1] * factor_t, axis=0)
    mass_s = jnp.sum(stats[4] * factor_s, axis=0)
    return stats, top_t, factor_t, mass_t, top_s, factor_s, mass_s


def logit_grad_kernel(tail_ref, teacher_ref, student_ref, target_ref, out_ref):
    flat = sum_parts(tail_ref[...])
    folded = [fold(flat, 32 * group + 32) for group in range(out_ref.shape[0] // 8)]
    top_t, mass_t, top_s, mass_s = [jnp.concatenate([f[i] for f in folded], axis=0) for i in (1, 3, 4, 6)]
    teacher_prob = jnp.exp(teacher_ref[...] - top_t) / mass_t
    student_prob = jnp.exp(student_ref[...] - top_s) / mass_s
    out_ref[...] = (2.0 * student_prob - teacher_prob - target_ref[...]).astype(BF16)


def owner_kernel(arrived_ref, out_ref, loss_ref):
    shards, _, lanes = arrived_ref.shape
    quarter = (lanes - 128) // 3
    stats, top_t, factor_t, mass_t, top_s, factor_s, mass_s = fold(sum_parts(arrived_ref[:, :, 3 * quarter :]), 0)
    cross = jnp.sum(stats[2] * factor_t, axis=0)
    picked = jnp.sum(stats[7] * stats[5], axis=0)
    loss = cross / mass_t - top_t - jnp.log(mass_t) + 2.0 * (top_s + jnp.log(mass_s)) - picked
    token = lax.broadcasted_iota(jnp.int32, (8, 1), 0)
    for t in range(out_ref.shape[0]):
        loss_ref[t] = jnp.sum(jnp.where(token == t, loss, 0.0))
    chosen_s = jnp.exp(stats[5] - top_s) / mass_s
    chosen_t = jnp.exp(stats[6] - top_t) / mass_t
    weight_l = (2.0 * chosen_s - chosen_t - stats[7]).astype(BF16).astype(F32)
    weight_s = 2.0 * (factor_s / mass_s)
    weight_t = -(factor_t / mass_t)
    place = lax.broadcasted_iota(jnp.int32, (shards, 8, 1), 1)
    last = jnp.zeros((8, quarter), F32)
    for j, weight_last in enumerate((weight_s, weight_t, weight_l)):
        weight = jnp.where(
            place < 2, weight_s, jnp.where(place < 4, weight_t, jnp.where(place < 6, weight_l, weight_last))
        )
        piece = []
        for chunk in range(quarter // LANES):
            lanes = slice((3 * chunk + j) * LANES, (3 * chunk + j + 1) * LANES)
            piece.append(sum(weight[shard] * arrived_ref[shard, :, lanes].astype(F32) for shard in range(shards)))
        piece = jnp.concatenate(piece, axis=1)
        last += piece
        out_ref[:, j * quarter : (j + 1) * quarter] = piece[0:2] + piece[2:4] + piece[4:6]
    out_ref[:, 3 * quarter :] = last[6:8]


def head_grad_kernel(hidden_ref, hidden_other_ref, grad_ref, other_ref, out_ref, total_ref, sems):
    grads = jnp.concatenate([grad_ref[...], other_ref[...]], axis=0)
    size = hidden_ref.shape[1] // PIECES
    copies = []
    for piece in range(PIECES):
        rows = pl.ds(piece * size, size)
        hidden = jnp.concatenate([hidden_ref[:, rows], hidden_other_ref[:, rows]], axis=0)
        total_ref[rows, :] = lax.dot_general(hidden, grads, (((0,), (0,)), ((), ())), preferred_element_type=F32)
        copies.append(pltpu.make_async_copy(total_ref.at[rows, :], out_ref.at[rows, :], sems.at[piece]))
        copies[-1].start()
    for copy in copies:
        copy.wait()


def two_exchanges(teacher_hidden, student_hidden, teacher_head, student_head, labels, *, shards):
    own = labels.shape[0]
    teacher_width, width = teacher_hidden.shape[1], student_hidden.shape[1]
    columns_here = student_head.shape[1]
    tokens = shards * own
    quarter = width // 4
    here = lax.axis_index("vocab").astype(jnp.int32)
    rows = gather_tokens(teacher_hidden, student_hidden, labels, shards).reshape(tokens, -1)
    student_rows = rows[:, teacher_width : teacher_width + width]
    other = [(0, 1), (1, 0)]
    student_other = lax.ppermute(student_rows, "rows", other)

    first_column = jnp.full((1, columns_here), here * columns_here, jnp.int32)
    heads = jnp.concatenate([teacher_head, student_head], axis=0)
    square = jax.ShapeDtypeStruct((tokens, columns_here), F32)
    payload, teacher_logits, student_logits, target = pl.pallas_call(
        raw_partial_kernel,
        out_shape=(jax.ShapeDtypeStruct((shards, 8, 3 * quarter + 128), BF16), square, square, square),
        in_specs=[VMEM, VMEM, VMEM],
        out_specs=(ANY, VMEM, VMEM, VMEM),
        scratch_shapes=[pltpu.VMEM((shards, 8, 3 * quarter + 128), BF16), pltpu.SemaphoreType.DMA((2 + quarter // LANES // 3,))],
        compiler_params=SMALL,
    )(first_column, rows, heads)
    arrived = swap(payload)
    grad_rows = pl.pallas_call(
        logit_grad_kernel,
        out_shape=jax.ShapeDtypeStruct((tokens, columns_here), BF16),
        in_specs=[VMEM] * 4,
        out_specs=VMEM,
        compiler_params=SMALL,
    )(arrived[:, :, 3 * quarter :], teacher_logits, student_logits, target)
    grad_other = lax.ppermute(grad_rows, "rows", other)
    hidden_grad, token_loss = pl.pallas_call(
        owner_kernel,
        out_shape=(jax.ShapeDtypeStruct((own, width), F32), jax.ShapeDtypeStruct((own,), F32)),
        in_specs=[VMEM],
        out_specs=(VMEM, SMEM),
        compiler_params=SMALL,
    )(arrived)
    head_grad = pl.pallas_call(
        head_grad_kernel,
        out_shape=jax.ShapeDtypeStruct((width, columns_here), F32),
        in_specs=[VMEM] * 4,
        out_specs=ANY,
        scratch_shapes=[pltpu.VMEM((width, columns_here), F32), pltpu.SemaphoreType.DMA((PIECES,))],
        compiler_params=SMALL,
    )(student_rows, student_other, grad_rows, grad_other)
    return (token_loss, hidden_grad, head_grad)


def three_exchanges(teacher_hidden, student_hidden, teacher_head, student_head, labels, *, shards):
    own = labels.shape[0]
    student_width = student_hidden.shape[1]
    columns_here = student_head.shape[1]
    first_column = lax.axis_index("vocab") * columns_here
    rows = gather_tokens(teacher_hidden, student_hidden, labels, shards).reshape(shards * own, -1)
    teacher_width = teacher_hidden.shape[1]
    teacher_rows = rows[:, :teacher_width]
    student_rows = rows[:, teacher_width : teacher_width + student_width]
    code = rows[:, teacher_width + student_width :].astype(jnp.int32)
    label_rows = code[:, 0] * 128 + code[:, 1]
    other = [(0, 1), (1, 0)]
    student_other = lax.ppermute(student_rows, "rows", other)

    teacher_logits = jnp.dot(teacher_rows, teacher_head, preferred_element_type=F32)
    student_logits = jnp.dot(student_rows, student_head, preferred_element_type=F32)
    columns = lax.broadcasted_iota(jnp.int32, student_logits.shape, 1)
    target = (label_rows - first_column)[:, None] == columns
    top_t = jnp.max(teacher_logits, axis=1, keepdims=True)
    exp_t = jnp.exp(teacher_logits - top_t)
    top_s = jnp.max(student_logits, axis=1, keepdims=True)
    exp_s = jnp.exp(student_logits - top_s)
    stats = jnp.concatenate(
        [
            top_t,
            jnp.sum(exp_t, axis=1, keepdims=True),
            jnp.sum(exp_t * (teacher_logits - student_logits), axis=1, keepdims=True),
            top_s,
            jnp.sum(exp_s, axis=1, keepdims=True),
            jnp.sum(jnp.where(target, student_logits, 0.0), axis=1, keepdims=True),
        ],
        axis=1,
    )
    every = swap(jnp.broadcast_to(stats[None], (shards,) + stats.shape))
    all_top_t = jnp.max(every[:, :, 0], axis=0)
    factor_t = jnp.exp(every[:, :, 0] - all_top_t[None])
    all_top_s = jnp.max(every[:, :, 3], axis=0)
    factor_s = jnp.exp(every[:, :, 3] - all_top_s[None])
    mass_t = jnp.sum(every[:, :, 1] * factor_t, axis=0)
    cross = jnp.sum(every[:, :, 2] * factor_t, axis=0)
    mass_s = jnp.sum(every[:, :, 4] * factor_s, axis=0)
    picked = jnp.sum(every[:, :, 5], axis=0)
    loss = cross / mass_t - all_top_t - jnp.log(mass_t) + 2.0 * (all_top_s + jnp.log(mass_s)) - picked
    token_loss = lax.dynamic_slice_in_dim(loss, lax.axis_index("vocab") * own, own, 0)

    teacher_prob = jnp.exp(teacher_logits - all_top_t[:, None]) / mass_t[:, None]
    student_prob = jnp.exp(student_logits - all_top_s[:, None]) / mass_s[:, None]
    grad_rows = (2.0 * student_prob - teacher_prob - target.astype(F32)).astype(BF16)
    grad_other = lax.ppermute(grad_rows, "rows", other)
    partial = lax.dot_general(grad_rows, student_head, (((1,), (1,)), ((), ())), preferred_element_type=F32)
    arrived = swap(partial.astype(BF16).reshape(shards, own, student_width))
    hidden_grad = jnp.sum(arrived.astype(F32), axis=0)
    head_grad = lax.dot_general(
        jnp.concatenate([student_rows, student_other], axis=0),
        jnp.concatenate([grad_rows, grad_other], axis=0),
        (((0,), (0,)), ((), ())),
        preferred_element_type=F32,
    )
    return (token_loss, hidden_grad, head_grad)


def solution(mesh):
    tokens = ("groups", "vocab", "rows")
    in_specs = (P(tokens, None), P(tokens, None), P(None, "vocab"), P(None, "vocab"), P(tokens))
    out_specs = (P(tokens), P(tokens, None), P("groups", "vocab"))

    def body(*arrays):
        shards = mesh.shape["vocab"]
        own = arrays[4].shape[0]
        small = own == 2 and shards % 4 == 0 and shards * own <= 24
        return (two_exchanges if small else three_exchanges)(*arrays, shards=shards)

    return jax.shard_map(body, mesh=mesh, in_specs=in_specs, out_specs=out_specs, check_vma=False)
```

```python
import jax
import jax.numpy as jnp
from jax import lax
from jax.experimental import pallas as pl
from jax.experimental.pallas import tpu as pltpu
from jax.sharding import PartitionSpec as P

F32 = jnp.float32
BF16 = jnp.bfloat16
CODE = 128


UNROLL = 16
LANES = 128
PIECES = 7
SMEM = pl.BlockSpec(memory_space=pltpu.SMEM)
VMEM = pl.BlockSpec(memory_space=pltpu.VMEM)
ANY = pl.BlockSpec(memory_space=pl.ANY)
SMALL = pltpu.CompilerParams(vmem_limit_bytes=16 * 1024 * 1024)


def over_shards(shards, body):
    if shards <= UNROLL:
        for shard in range(shards):
            body(shard)
    else:
        pl.loop(0, shards)(body)


def swap(blocks):
    return lax.all_to_all(blocks, "vocab", split_axis=0, concat_axis=0, tiled=True)


def payload_kernel(labels_ref, teacher_ref, student_ref, out_ref):
    shards, own, _ = out_ref.shape
    teacher_width, student_width = teacher_ref.shape[1], student_ref.shape[1]
    teacher = teacher_ref[...]
    student = student_ref[...]
    code = label_digits(labels_ref, own)

    def write(shard):
        out_ref[shard, :, :teacher_width] = teacher
        out_ref[shard, :, teacher_width : teacher_width + student_width] = student
        out_ref[shard, :, teacher_width + student_width :] = code

    over_shards(shards, write)


def label_digits(labels_ref, own):
    row = lax.broadcasted_iota(jnp.int32, (own, CODE), 0)
    lane = lax.broadcasted_iota(jnp.int32, (own, CODE), 1)
    digits = jnp.zeros((own, CODE), jnp.int32)
    for token in range(own):
        label = labels_ref[token]
        pair = jnp.where(lane == 0, label >> 7, label & 127)
        digits = jnp.where(row == token, pair, digits)
    return digits.astype(F32).astype(BF16)


def gather_tokens(teacher_hidden, student_hidden, labels, shards):
    own, teacher_width = teacher_hidden.shape
    student_width = student_hidden.shape[1]
    payload = pl.pallas_call(
        payload_kernel,
        out_shape=jax.ShapeDtypeStruct((shards, own, teacher_width + student_width + CODE), BF16),
        in_specs=[SMEM, VMEM, VMEM],
        out_specs=VMEM,
    )(labels, teacher_hidden, student_hidden)
    return swap(payload)


def raw_partial_kernel(
    first_ref, rows_ref, heads_ref, out_hbm, teacher_ref, student_ref, target_ref, out_ref, sems
):
    shards, own, _ = rows_ref.shape
    tokens = shards * own
    wide = 8 * shards
    columns = heads_ref.shape[1]
    quarter = (out_ref.shape[2] - 128) // 3
    width = 4 * quarter
    teacher_width = heads_ref.shape[0] - width

    def iota(shape, dim):
        return lax.broadcasted_iota(jnp.int32, shape, dim)

    def dot(left, right, dims):
        return lax.dot_general(left, right, (dims, ((), ())), preferred_element_type=F32)

    copies = []

    def send_out(piece, start, size):
        lanes = pl.ds(start, size)
        copies.append(pltpu.make_async_copy(out_ref.at[:, :, lanes], out_hbm.at[:, :, lanes], sems.at[piece]))
        copies[-1].start()

    def rows_of(start, end):
        return jnp.concatenate([rows_ref[shard, :, start:end] for shard in range(shards)], axis=0)

    student = dot(rows_of(teacher_width, teacher_width + width), heads_ref[teacher_width:, :], ((1,), (0,)))
    teacher = dot(rows_of(0, teacher_width), heads_ref[:teacher_width, :], ((1,), (0,)))
    code = rows_of(teacher_width + width, teacher_width + width + CODE).astype(F32)
    lane = iota(code.shape, 1)
    label = jnp.sum(jnp.where(lane == 0, code * 128.0, jnp.where(lane == 1, code, 0.0)), axis=1, keepdims=True)
    target = (label.astype(jnp.int32) == iota((tokens, columns), 1) + first_ref[...]).astype(F32)
    teacher_ref[...] = teacher
    student_ref[...] = student
    target_ref[...] = target

    def total(array):
        return jnp.sum(array, axis=1, keepdims=True)

    top_t = jnp.max(teacher, axis=1, keepdims=True)
    top_s = jnp.max(student, axis=1, keepdims=True)
    exp_t = jnp.exp(teacher - top_t)
    exp_s = jnp.exp(student - top_s)
    mass_t, mass_s = total(exp_t), total(exp_s)
    guess = jnp.abs(exp_s * (2.0 / mass_s) - exp_t / mass_t)
    lane = iota((tokens, columns), 1)
    largest = jnp.max(guess, axis=1, keepdims=True)
    where_largest = jnp.min(jnp.where(guess == largest, lane, columns), axis=1, keepdims=True)
    has_label = total(target)
    chosen = jnp.where(has_label > 0.5, target, (lane == where_largest).astype(F32))
    stats = [
        top_t,
        mass_t,
        total(exp_t * (teacher - student)),
        top_s,
        mass_s,
        total(chosen * student),
        total(chosen * teacher),
        has_label,
    ]
    lane = iota((tokens, 128), 1)
    table = jnp.zeros((tokens, 128), F32)
    for k, stat in enumerate(stats):
        table = jnp.where(lane % 8 == k, stat, table)
    first = table.astype(BF16).astype(F32)
    second = (table - first).astype(BF16).astype(F32)
    part = (lane % 32) // 8
    parts = jnp.where(
        part == 0, first, jnp.where(part == 1, second, jnp.where(part == 2, table - first - second, 0.0))
    ).astype(BF16)

    row, column = iota((wide, tokens), 0), iota((wide, tokens), 1)
    of_token = (column == (row // 8) * 2 + row % 2).astype(F32).astype(BF16)
    by_row = dot(of_token, parts, ((1,), (0,)))

    lane = iota((8, 128), 1)
    shared = jnp.zeros((8, 128), F32)
    wide_parts = parts.astype(F32)
    for group in range(tokens // 8):
        shared = jnp.where(lane // 32 == group + 1, wide_parts[8 * group : 8 * group + 8], shared)
    for shard in range(shards):
        block = jnp.where(lane < 32, by_row[8 * shard : 8 * shard + 8], shared)
        out_ref[shard, :, 3 * quarter :] = block.astype(BF16)
    send_out(0, 3 * quarter, 128)

    members = jnp.concatenate([exp_s * (1.0 - chosen), exp_t * (1.0 - chosen), chosen], axis=0)
    member_high = members.astype(BF16)
    member_low = (members - member_high.astype(F32)).astype(BF16)
    row, column = iota((wide, 3 * tokens), 0), iota((wide, 3 * tokens), 1)
    place = row % 8
    token = (row // 8) * 2 + row % 2
    pick = ((place < 6) & (column == (place // 2) * tokens + token)).astype(F32).astype(BF16)
    left = dot(pick, jnp.concatenate([member_high, member_low], axis=1), ((1,), (0,))).astype(BF16)
    left = jnp.concatenate([left[:, :columns], left[:, columns:]], axis=0)

    place = iota((wide, 1), 0) % 8
    chunks = quarter // LANES
    first_unsent = 0
    for chunk in range(chunks):
        starts = [teacher_width + j * quarter + chunk * LANES for j in range(4)]
        right = jnp.concatenate([heads_ref[start : start + LANES, :] for start in starts], axis=0)
        both = dot(left, right, ((1,), (1,)))
        exact = [both[:wide, j * LANES : (j + 1) * LANES] + both[wide:, j * LANES : (j + 1) * LANES] for j in range(4)]
        for j in range(3):
            sent = jnp.where(place >= 6, pltpu.roll(exact[3], 6 - 2 * j, 0), exact[j])
            lanes = slice((3 * chunk + j) * LANES, (3 * chunk + j + 1) * LANES)
            for shard in range(shards):
                out_ref[shard, :, lanes] = sent[8 * shard : 8 * shard + 8].astype(BF16)
        if chunk % 3 == 2 or chunk == chunks - 1:
            end = 3 * (chunk + 1) * LANES
            send_out(len(copies), first_unsent, end - first_unsent)
            first_unsent = end
    for copy in copies:
        copy.wait()


def sum_parts(tail):
    shards = tail.shape[0]
    flat = tail.astype(F32).reshape(shards * 8, 128)
    return flat + pltpu.roll(flat, 120, 1) + pltpu.roll(flat, 112, 1)


def fold(flat, lane):
    shards = flat.shape[0] // 8
    stats = [flat[:, lane + k : lane + k + 1].reshape(shards, 8, 1) for k in range(8)]
    top_t = jnp.max(stats[0], axis=0)
    factor_t = jnp.exp(stats[0] - top_t)
    top_s = jnp.max(stats[3], axis=0)
    factor_s = jnp.exp(stats[3] - top_s)
    mass_t = jnp.sum(stats[1] * factor_t, axis=0)
    mass_s = jnp.sum(stats[4] * factor_s, axis=0)
    return stats, top_t, factor_t, mass_t, top_s, factor_s, mass_s


def logit_grad_kernel(tail_ref, teacher_ref, student_ref, target_ref, out_ref):
    flat = sum_parts(tail_ref[...])
    folded = [fold(flat, 32 * group + 32) for group in range(out_ref.shape[0] // 8)]
    top_t, mass_t, top_s, mass_s = [jnp.concatenate([f[i] for f in folded], axis=0) for i in (1, 3, 4, 6)]
    teacher_prob = jnp.exp(teacher_ref[...] - top_t) / mass_t
    student_prob = jnp.exp(student_ref[...] - top_s) / mass_s
    out_ref[...] = (2.0 * student_prob - teacher_prob - target_ref[...]).astype(BF16)


def owner_kernel(arrived_ref, out_ref, loss_ref):
    shards, _, lanes = arrived_ref.shape
    quarter = (lanes - 128) // 3
    stats, top_t, factor_t, mass_t, top_s, factor_s, mass_s = fold(sum_parts(arrived_ref[:, :, 3 * quarter :]), 0)
    cross = jnp.sum(stats[2] * factor_t, axis=0)
    picked = jnp.sum(stats[7] * stats[5], axis=0)
    loss = cross / mass_t - top_t - jnp.log(mass_t) + 2.0 * (top_s + jnp.log(mass_s)) - picked
    token = lax.broadcasted_iota(jnp.int32, (8, 1), 0)
    for t in range(out_ref.shape[0]):
        loss_ref[t] = jnp.sum(jnp.where(token == t, loss, 0.0))
    chosen_s = jnp.exp(stats[5] - top_s) / mass_s
    chosen_t = jnp.exp(stats[6] - top_t) / mass_t
    weight_l = (2.0 * chosen_s - chosen_t - stats[7]).astype(BF16).astype(F32)
    weight_s = 2.0 * (factor_s / mass_s)
    weight_t = -(factor_t / mass_t)
    place = lax.broadcasted_iota(jnp.int32, (shards, 8, 1), 1)
    last = jnp.zeros((8, quarter), F32)
    for j, weight_last in enumerate((weight_s, weight_t, weight_l)):
        weight = jnp.where(
            place < 2, weight_s, jnp.where(place < 4, weight_t, jnp.where(place < 6, weight_l, weight_last))
        )
        piece = []
        for chunk in range(quarter // LANES):
            lanes = slice((3 * chunk + j) * LANES, (3 * chunk + j + 1) * LANES)
            piece.append(sum(weight[shard] * arrived_ref[shard, :, lanes].astype(F32) for shard in range(shards)))
        piece = jnp.concatenate(piece, axis=1)
        last += piece
        out_ref[:, j * quarter : (j + 1) * quarter] = piece[0:2] + piece[2:4] + piece[4:6]
    out_ref[:, 3 * quarter :] = last[6:8]


def head_grad_kernel(hidden_ref, hidden_other_ref, grad_ref, other_ref, out_ref, total_ref, sems):
    grads = jnp.concatenate([grad_ref[...], other_ref[...]], axis=0)
    size = hidden_ref.shape[1] // PIECES
    copies = []
    for piece in range(PIECES):
        rows = pl.ds(piece * size, size)
        hidden = jnp.concatenate([hidden_ref[:, rows], hidden_other_ref[:, rows]], axis=0)
        total_ref[rows, :] = lax.dot_general(hidden, grads, (((0,), (0,)), ((), ())), preferred_element_type=F32)
        copies.append(pltpu.make_async_copy(total_ref.at[rows, :], out_ref.at[rows, :], sems.at[piece]))
        copies[-1].start()
    for copy in copies:
        copy.wait()


def two_exchanges(teacher_hidden, student_hidden, teacher_head, student_head, labels, *, shards):
    own = labels.shape[0]
    teacher_width, width = teacher_hidden.shape[1], student_hidden.shape[1]
    columns_here = student_head.shape[1]
    tokens = shards * own
    quarter = width // 4
    here = lax.axis_index("vocab").astype(jnp.int32)
    rows = gather_tokens(teacher_hidden, student_hidden, labels, shards)
    student_rows = rows[:, :, teacher_width : teacher_width + width].reshape(tokens, width)
    other = [(0, 1), (1, 0)]
    student_other = lax.ppermute(student_rows, "rows", other)

    first_column = jnp.full((1, columns_here), here * columns_here, jnp.int32)
    heads = jnp.concatenate([teacher_head, student_head], axis=0)
    square = jax.ShapeDtypeStruct((tokens, columns_here), F32)
    payload, teacher_logits, student_logits, target = pl.pallas_call(
        raw_partial_kernel,
        out_shape=(jax.ShapeDtypeStruct((shards, 8, 3 * quarter + 128), BF16), square, square, square),
        in_specs=[VMEM, VMEM, VMEM],
        out_specs=(ANY, VMEM, VMEM, VMEM),
        scratch_shapes=[pltpu.VMEM((shards, 8, 3 * quarter + 128), BF16), pltpu.SemaphoreType.DMA((2 + quarter // LANES // 3,))],
        compiler_params=SMALL,
    )(first_column, rows, heads)
    arrived = swap(payload)
    grad_rows = pl.pallas_call(
        logit_grad_kernel,
        out_shape=jax.ShapeDtypeStruct((tokens, columns_here), BF16),
        in_specs=[VMEM] * 4,
        out_specs=VMEM,
        compiler_params=SMALL,
    )(arrived[:, :, 3 * quarter :], teacher_logits, student_logits, target)
    grad_other = lax.ppermute(grad_rows, "rows", other)
    hidden_grad, token_loss = pl.pallas_call(
        owner_kernel,
        out_shape=(jax.ShapeDtypeStruct((own, width), F32), jax.ShapeDtypeStruct((own,), F32)),
        in_specs=[VMEM],
        out_specs=(VMEM, SMEM),
        compiler_params=SMALL,
    )(arrived)
    head_grad = pl.pallas_call(
        head_grad_kernel,
        out_shape=jax.ShapeDtypeStruct((width, columns_here), F32),
        in_specs=[VMEM] * 4,
        out_specs=ANY,
        scratch_shapes=[pltpu.VMEM((width, columns_here), F32), pltpu.SemaphoreType.DMA((PIECES,))],
        compiler_params=SMALL,
    )(student_rows, student_other, grad_rows, grad_other)
    return (token_loss, hidden_grad, head_grad)


def three_exchanges(teacher_hidden, student_hidden, teacher_head, student_head, labels, *, shards):
    own = labels.shape[0]
    student_width = student_hidden.shape[1]
    columns_here = student_head.shape[1]
    first_column = lax.axis_index("vocab") * columns_here
    rows = gather_tokens(teacher_hidden, student_hidden, labels, shards).reshape(shards * own, -1)
    teacher_width = teacher_hidden.shape[1]
    teacher_rows = rows[:, :teacher_width]
    student_rows = rows[:, teacher_width : teacher_width + student_width]
    code = rows[:, teacher_width + student_width :].astype(jnp.int32)
    label_rows = code[:, 0] * 128 + code[:, 1]
    other = [(0, 1), (1, 0)]
    student_other = lax.ppermute(student_rows, "rows", other)

    teacher_logits = jnp.dot(teacher_rows, teacher_head, preferred_element_type=F32)
    student_logits = jnp.dot(student_rows, student_head, preferred_element_type=F32)
    columns = lax.broadcasted_iota(jnp.int32, student_logits.shape, 1)
    target = (label_rows - first_column)[:, None] == columns
    top_t = jnp.max(teacher_logits, axis=1, keepdims=True)
    exp_t = jnp.exp(teacher_logits - top_t)
    top_s = jnp.max(student_logits, axis=1, keepdims=True)
    exp_s = jnp.exp(student_logits - top_s)
    stats = jnp.concatenate(
        [
            top_t,
            jnp.sum(exp_t, axis=1, keepdims=True),
            jnp.sum(exp_t * (teacher_logits - student_logits), axis=1, keepdims=True),
            top_s,
            jnp.sum(exp_s, axis=1, keepdims=True),
            jnp.sum(jnp.where(target, student_logits, 0.0), axis=1, keepdims=True),
        ],
        axis=1,
    )
    every = swap(jnp.broadcast_to(stats[None], (shards,) + stats.shape))
    all_top_t = jnp.max(every[:, :, 0], axis=0)
    factor_t = jnp.exp(every[:, :, 0] - all_top_t[None])
    all_top_s = jnp.max(every[:, :, 3], axis=0)
    factor_s = jnp.exp(every[:, :, 3] - all_top_s[None])
    mass_t = jnp.sum(every[:, :, 1] * factor_t, axis=0)
    cross = jnp.sum(every[:, :, 2] * factor_t, axis=0)
    mass_s = jnp.sum(every[:, :, 4] * factor_s, axis=0)
    picked = jnp.sum(every[:, :, 5], axis=0)
    loss = cross / mass_t - all_top_t - jnp.log(mass_t) + 2.0 * (all_top_s + jnp.log(mass_s)) - picked
    token_loss = lax.dynamic_slice_in_dim(loss, lax.axis_index("vocab") * own, own, 0)

    teacher_prob = jnp.exp(teacher_logits - all_top_t[:, None]) / mass_t[:, None]
    student_prob = jnp.exp(student_logits - all_top_s[:, None]) / mass_s[:, None]
    grad_rows = (2.0 * student_prob - teacher_prob - target.astype(F32)).astype(BF16)
    grad_other = lax.ppermute(grad_rows, "rows", other)
    partial = lax.dot_general(grad_rows, student_head, (((1,), (1,)), ((), ())), preferred_element_type=F32)
    arrived = swap(partial.astype(BF16).reshape(shards, own, student_width))
    hidden_grad = jnp.sum(arrived.astype(F32), axis=0)
    head_grad = lax.dot_general(
        jnp.concatenate([student_rows, student_other], axis=0),
        jnp.concatenate([grad_rows, grad_other], axis=0),
        (((0,), (0,)), ((), ())),
        preferred_element_type=F32,
    )
    return (token_loss, hidden_grad, head_grad)


def solution(mesh):
    tokens = ("groups", "vocab", "rows")
    in_specs = (P(tokens, None), P(tokens, None), P(None, "vocab"), P(None, "vocab"), P(tokens))
    out_specs = (P(tokens), P(tokens, None), P("groups", "vocab"))

    def body(*arrays):
        shards = mesh.shape["vocab"]
        own = arrays[4].shape[0]
        small = own == 2 and shards % 4 == 0 and shards * own <= 24
        return (two_exchanges if small else three_exchanges)(*arrays, shards=shards)

    return jax.shard_map(body, mesh=mesh, in_specs=in_specs, out_specs=out_specs, check_vma=False)
```

```python
import jax
import jax.numpy as jnp
from jax import lax
from jax.experimental import pallas as pl
from jax.experimental.pallas import tpu as pltpu
from jax.sharding import PartitionSpec as P

F32 = jnp.float32
BF16 = jnp.bfloat16
CODE = 128


UNROLL = 16
LANES = 128
PIECES = 7
SMEM = pl.BlockSpec(memory_space=pltpu.SMEM)
VMEM = pl.BlockSpec(memory_space=pltpu.VMEM)
ANY = pl.BlockSpec(memory_space=pl.ANY)
SMALL = pltpu.CompilerParams(vmem_limit_bytes=16 * 1024 * 1024)


def over_shards(shards, body):
    if shards <= UNROLL:
        for shard in range(shards):
            body(shard)
    else:
        pl.loop(0, shards)(body)


def swap(blocks):
    return lax.all_to_all(blocks, "vocab", split_axis=0, concat_axis=0, tiled=True)


def payload_kernel(labels_ref, teacher_ref, student_ref, out_ref):
    shards, own, _ = out_ref.shape
    teacher_width, student_width = teacher_ref.shape[1], student_ref.shape[1]
    teacher = teacher_ref[...]
    student = student_ref[...]
    code = label_digits(labels_ref, own)

    def write(shard):
        out_ref[shard, :, :teacher_width] = teacher
        out_ref[shard, :, teacher_width : teacher_width + student_width] = student
        out_ref[shard, :, teacher_width + student_width :] = code

    over_shards(shards, write)


def label_digits(labels_ref, own):
    row = lax.broadcasted_iota(jnp.int32, (own, CODE), 0)
    lane = lax.broadcasted_iota(jnp.int32, (own, CODE), 1)
    digits = jnp.zeros((own, CODE), jnp.int32)
    for token in range(own):
        label = labels_ref[token]
        pair = jnp.where(lane == 0, label >> 7, label & 127)
        digits = jnp.where(row == token, pair, digits)
    return digits.astype(F32).astype(BF16)


def gather_tokens(teacher_hidden, student_hidden, labels, shards):
    own, teacher_width = teacher_hidden.shape
    student_width = student_hidden.shape[1]
    payload = pl.pallas_call(
        payload_kernel,
        out_shape=jax.ShapeDtypeStruct((shards, own, teacher_width + student_width + CODE), BF16),
        in_specs=[SMEM, VMEM, VMEM],
        out_specs=VMEM,
    )(labels, teacher_hidden, student_hidden)
    return swap(payload)


def plain_payload_kernel(teacher_ref, student_ref, out_ref):
    teacher_width = teacher_ref.shape[1]
    for shard in range(out_ref.shape[0]):
        out_ref[shard, :, :teacher_width] = teacher_ref[...]
        out_ref[shard, :, teacher_width:] = student_ref[...]


def raw_partial_kernel(
    first_ref, label_ref, rows_ref, heads_ref, out_hbm, teacher_ref, student_ref, target_ref, out_ref, sems
):
    tokens = rows_ref.shape[0]
    shards = out_ref.shape[0]
    wide = 8 * shards
    columns = heads_ref.shape[1]
    quarter = (out_ref.shape[2] - 128) // 3
    width = 4 * quarter
    teacher_width = heads_ref.shape[0] - width

    def iota(shape, dim):
        return lax.broadcasted_iota(jnp.int32, shape, dim)

    def dot(left, right, dims):
        return lax.dot_general(left, right, (dims, ((), ())), preferred_element_type=F32)

    copies = []

    def send_out(piece, start, size):
        lanes = pl.ds(start, size)
        copies.append(pltpu.make_async_copy(out_ref.at[:, :, lanes], out_hbm.at[:, :, lanes], sems.at[piece]))
        copies[-1].start()

    student = dot(rows_ref[:, teacher_width : teacher_width + width], heads_ref[teacher_width:, :], ((1,), (0,)))
    teacher = dot(rows_ref[:, :teacher_width], heads_ref[:teacher_width, :], ((1,), (0,)))
    target = (label_ref[...] == iota((tokens, columns), 1) + first_ref[...]).astype(F32)
    teacher_ref[...] = teacher
    student_ref[...] = student
    target_ref[...] = target

    def total(array):
        return jnp.sum(array, axis=1, keepdims=True)

    top_t = jnp.max(teacher, axis=1, keepdims=True)
    top_s = jnp.max(student, axis=1, keepdims=True)
    exp_t = jnp.exp(teacher - top_t)
    exp_s = jnp.exp(student - top_s)
    mass_t, mass_s = total(exp_t), total(exp_s)
    guess = jnp.abs(exp_s * (2.0 / mass_s) - exp_t / mass_t)
    lane = iota((tokens, columns), 1)
    largest = jnp.max(guess, axis=1, keepdims=True)
    where_largest = jnp.min(jnp.where(guess == largest, lane, columns), axis=1, keepdims=True)
    has_label = total(target)
    chosen = jnp.where(has_label > 0.5, target, (lane == where_largest).astype(F32))
    stats = [
        top_t,
        mass_t,
        total(exp_t * (teacher - student)),
        top_s,
        mass_s,
        total(chosen * student),
        total(chosen * teacher),
        has_label,
    ]
    lane = iota((tokens, 128), 1)
    table = jnp.zeros((tokens, 128), F32)
    for k, stat in enumerate(stats):
        table = jnp.where(lane % 8 == k, stat, table)
    first = table.astype(BF16).astype(F32)
    second = (table - first).astype(BF16).astype(F32)
    part = (lane % 32) // 8
    parts = jnp.where(
        part == 0, first, jnp.where(part == 1, second, jnp.where(part == 2, table - first - second, 0.0))
    ).astype(BF16)

    row, column = iota((wide, tokens), 0), iota((wide, tokens), 1)
    of_token = (column == (row // 8) * 2 + row % 2).astype(F32).astype(BF16)
    by_row = dot(of_token, parts, ((1,), (0,)))

    lane = iota((8, 128), 1)
    shared = jnp.zeros((8, 128), F32)
    wide_parts = parts.astype(F32)
    for group in range(tokens // 8):
        shared = jnp.where(lane // 32 == group + 1, wide_parts[8 * group : 8 * group + 8], shared)
    for shard in range(shards):
        block = jnp.where(lane < 32, by_row[8 * shard : 8 * shard + 8], shared)
        out_ref[shard, :, 3 * quarter :] = block.astype(BF16)
    send_out(0, 3 * quarter, 128)

    members = jnp.concatenate([exp_s * (1.0 - chosen), exp_t * (1.0 - chosen), chosen], axis=0)
    member_high = members.astype(BF16)
    member_low = (members - member_high.astype(F32)).astype(BF16)
    row, column = iota((wide, 3 * tokens), 0), iota((wide, 3 * tokens), 1)
    place = row % 8
    token = (row // 8) * 2 + row % 2
    pick = ((place < 6) & (column == (place // 2) * tokens + token)).astype(F32).astype(BF16)
    left = dot(pick, jnp.concatenate([member_high, member_low], axis=1), ((1,), (0,))).astype(BF16)
    left = jnp.concatenate([left[:, :columns], left[:, columns:]], axis=0)

    place = iota((wide, 1), 0) % 8
    chunks = quarter // LANES
    first_unsent = 0
    for chunk in range(chunks):
        starts = [teacher_width + j * quarter + chunk * LANES for j in range(4)]
        right = jnp.concatenate([heads_ref[start : start + LANES, :] for start in starts], axis=0)
        both = dot(left, right, ((1,), (1,)))
        exact = [both[:wide, j * LANES : (j + 1) * LANES] + both[wide:, j * LANES : (j + 1) * LANES] for j in range(4)]
        for j in range(3):
            sent = jnp.where(place >= 6, pltpu.roll(exact[3], 6 - 2 * j, 0), exact[j])
            lanes = slice((3 * chunk + j) * LANES, (3 * chunk + j + 1) * LANES)
            for shard in range(shards):
                out_ref[shard, :, lanes] = sent[8 * shard : 8 * shard + 8].astype(BF16)
        if chunk % 3 == 2 or chunk == chunks - 1:
            end = 3 * (chunk + 1) * LANES
            send_out(len(copies), first_unsent, end - first_unsent)
            first_unsent = end
    for copy in copies:
        copy.wait()


def sum_parts(tail):
    shards = tail.shape[0]
    flat = tail.astype(F32).reshape(shards * 8, 128)
    return flat + pltpu.roll(flat, 120, 1) + pltpu.roll(flat, 112, 1)


def fold(flat, lane):
    shards = flat.shape[0] // 8
    stats = [flat[:, lane + k : lane + k + 1].reshape(shards, 8, 1) for k in range(8)]
    top_t = jnp.max(stats[0], axis=0)
    factor_t = jnp.exp(stats[0] - top_t)
    top_s = jnp.max(stats[3], axis=0)
    factor_s = jnp.exp(stats[3] - top_s)
    mass_t = jnp.sum(stats[1] * factor_t, axis=0)
    mass_s = jnp.sum(stats[4] * factor_s, axis=0)
    return stats, top_t, factor_t, mass_t, top_s, factor_s, mass_s


def logit_grad_kernel(tail_ref, teacher_ref, student_ref, target_ref, out_ref):
    flat = sum_parts(tail_ref[...])
    folded = [fold(flat, 32 * group + 32) for group in range(out_ref.shape[0] // 8)]
    top_t, mass_t, top_s, mass_s = [jnp.concatenate([f[i] for f in folded], axis=0) for i in (1, 3, 4, 6)]
    teacher_prob = jnp.exp(teacher_ref[...] - top_t) / mass_t
    student_prob = jnp.exp(student_ref[...] - top_s) / mass_s
    out_ref[...] = (2.0 * student_prob - teacher_prob - target_ref[...]).astype(BF16)


def owner_kernel(arrived_ref, out_ref, loss_ref):
    shards, _, lanes = arrived_ref.shape
    quarter = (lanes - 128) // 3
    stats, top_t, factor_t, mass_t, top_s, factor_s, mass_s = fold(sum_parts(arrived_ref[:, :, 3 * quarter :]), 0)
    cross = jnp.sum(stats[2] * factor_t, axis=0)
    picked = jnp.sum(stats[7] * stats[5], axis=0)
    loss = cross / mass_t - top_t - jnp.log(mass_t) + 2.0 * (top_s + jnp.log(mass_s)) - picked
    token = lax.broadcasted_iota(jnp.int32, (8, 1), 0)
    for t in range(out_ref.shape[0]):
        loss_ref[t] = jnp.sum(jnp.where(token == t, loss, 0.0))
    chosen_s = jnp.exp(stats[5] - top_s) / mass_s
    chosen_t = jnp.exp(stats[6] - top_t) / mass_t
    weight_l = (2.0 * chosen_s - chosen_t - stats[7]).astype(BF16).astype(F32)
    weight_s = 2.0 * (factor_s / mass_s)
    weight_t = -(factor_t / mass_t)
    place = lax.broadcasted_iota(jnp.int32, (shards, 8, 1), 1)
    last = jnp.zeros((8, quarter), F32)
    for j, weight_last in enumerate((weight_s, weight_t, weight_l)):
        weight = jnp.where(
            place < 2, weight_s, jnp.where(place < 4, weight_t, jnp.where(place < 6, weight_l, weight_last))
        )
        piece = []
        for chunk in range(quarter // LANES):
            lanes = slice((3 * chunk + j) * LANES, (3 * chunk + j + 1) * LANES)
            piece.append(sum(weight[shard] * arrived_ref[shard, :, lanes].astype(F32) for shard in range(shards)))
        piece = jnp.concatenate(piece, axis=1)
        last += piece
        out_ref[:, j * quarter : (j + 1) * quarter] = piece[0:2] + piece[2:4] + piece[4:6]
    out_ref[:, 3 * quarter :] = last[6:8]


def head_grad_kernel(hidden_ref, hidden_other_ref, grad_ref, other_ref, out_ref, total_ref, sems):
    grads = jnp.concatenate([grad_ref[...], other_ref[...]], axis=0)
    size = hidden_ref.shape[1] // PIECES
    copies = []
    for piece in range(PIECES):
        rows = pl.ds(piece * size, size)
        hidden = jnp.concatenate([hidden_ref[:, rows], hidden_other_ref[:, rows]], axis=0)
        total_ref[rows, :] = lax.dot_general(hidden, grads, (((0,), (0,)), ((), ())), preferred_element_type=F32)
        copies.append(pltpu.make_async_copy(total_ref.at[rows, :], out_ref.at[rows, :], sems.at[piece]))
        copies[-1].start()
    for copy in copies:
        copy.wait()


def two_exchanges(teacher_hidden, student_hidden, teacher_head, student_head, labels, *, shards):
    own = labels.shape[0]
    teacher_width, width = teacher_hidden.shape[1], student_hidden.shape[1]
    columns_here = student_head.shape[1]
    tokens = shards * own
    quarter = width // 4
    here = lax.axis_index("vocab").astype(jnp.int32)
    payload = pl.pallas_call(
        plain_payload_kernel,
        out_shape=jax.ShapeDtypeStruct((shards, own, teacher_width + width), BF16),
        in_specs=[VMEM, VMEM],
        out_specs=VMEM,
    )(teacher_hidden, student_hidden)
    payload, labels = lax.optimization_barrier((payload, labels))
    rows = swap(payload).reshape(tokens, -1)
    label_rows = lax.all_gather(labels, "vocab", axis=0, tiled=True)[:, None]
    student_rows = rows[:, teacher_width : teacher_width + width]
    other = [(0, 1), (1, 0)]
    student_other = lax.ppermute(student_rows, "rows", other)

    first_column = jnp.full((1, columns_here), here * columns_here, jnp.int32)
    heads = jnp.concatenate([teacher_head, student_head], axis=0)
    square = jax.ShapeDtypeStruct((tokens, columns_here), F32)
    payload, teacher_logits, student_logits, target = pl.pallas_call(
        raw_partial_kernel,
        out_shape=(jax.ShapeDtypeStruct((shards, 8, 3 * quarter + 128), BF16), square, square, square),
        in_specs=[VMEM] * 4,
        out_specs=(ANY, VMEM, VMEM, VMEM),
        scratch_shapes=[pltpu.VMEM((shards, 8, 3 * quarter + 128), BF16), pltpu.SemaphoreType.DMA((2 + quarter // LANES // 3,))],
        compiler_params=SMALL,
    )(first_column, label_rows, rows, heads)
    arrived = swap(payload)
    grad_rows = pl.pallas_call(
        logit_grad_kernel,
        out_shape=jax.ShapeDtypeStruct((tokens, columns_here), BF16),
        in_specs=[VMEM] * 4,
        out_specs=VMEM,
        compiler_params=SMALL,
    )(arrived[:, :, 3 * quarter :], teacher_logits, student_logits, target)
    grad_other = lax.ppermute(grad_rows, "rows", other)
    hidden_grad, token_loss = pl.pallas_call(
        owner_kernel,
        out_shape=(jax.ShapeDtypeStruct((own, width), F32), jax.ShapeDtypeStruct((own,), F32)),
        in_specs=[VMEM],
        out_specs=(VMEM, SMEM),
        compiler_params=SMALL,
    )(arrived)
    head_grad = pl.pallas_call(
        head_grad_kernel,
        out_shape=jax.ShapeDtypeStruct((width, columns_here), F32),
        in_specs=[VMEM] * 4,
        out_specs=ANY,
        scratch_shapes=[pltpu.VMEM((width, columns_here), F32), pltpu.SemaphoreType.DMA((PIECES,))],
        compiler_params=SMALL,
    )(student_rows, student_other, grad_rows, grad_other)
    return (token_loss, hidden_grad, head_grad)


def three_exchanges(teacher_hidden, student_hidden, teacher_head, student_head, labels, *, shards):
    own = labels.shape[0]
    student_width = student_hidden.shape[1]
    columns_here = student_head.shape[1]
    first_column = lax.axis_index("vocab") * columns_here
    rows = gather_tokens(teacher_hidden, student_hidden, labels, shards).reshape(shards * own, -1)
    teacher_width = teacher_hidden.shape[1]
    teacher_rows = rows[:, :teacher_width]
    student_rows = rows[:, teacher_width : teacher_width + student_width]
    code = rows[:, teacher_width + student_width :].astype(jnp.int32)
    label_rows = code[:, 0] * 128 + code[:, 1]
    other = [(0, 1), (1, 0)]
    student_other = lax.ppermute(student_rows, "rows", other)

    teacher_logits = jnp.dot(teacher_rows, teacher_head, preferred_element_type=F32)
    student_logits = jnp.dot(student_rows, student_head, preferred_element_type=F32)
    columns = lax.broadcasted_iota(jnp.int32, student_logits.shape, 1)
    target = (label_rows - first_column)[:, None] == columns
    top_t = jnp.max(teacher_logits, axis=1, keepdims=True)
    exp_t = jnp.exp(teacher_logits - top_t)
    top_s = jnp.max(student_logits, axis=1, keepdims=True)
    exp_s = jnp.exp(student_logits - top_s)
    stats = jnp.concatenate(
        [
            top_t,
            jnp.sum(exp_t, axis=1, keepdims=True),
            jnp.sum(exp_t * (teacher_logits - student_logits), axis=1, keepdims=True),
            top_s,
            jnp.sum(exp_s, axis=1, keepdims=True),
            jnp.sum(jnp.where(target, student_logits, 0.0), axis=1, keepdims=True),
        ],
        axis=1,
    )
    every = swap(jnp.broadcast_to(stats[None], (shards,) + stats.shape))
    all_top_t = jnp.max(every[:, :, 0], axis=0)
    factor_t = jnp.exp(every[:, :, 0] - all_top_t[None])
    all_top_s = jnp.max(every[:, :, 3], axis=0)
    factor_s = jnp.exp(every[:, :, 3] - all_top_s[None])
    mass_t = jnp.sum(every[:, :, 1] * factor_t, axis=0)
    cross = jnp.sum(every[:, :, 2] * factor_t, axis=0)
    mass_s = jnp.sum(every[:, :, 4] * factor_s, axis=0)
    picked = jnp.sum(every[:, :, 5], axis=0)
    loss = cross / mass_t - all_top_t - jnp.log(mass_t) + 2.0 * (all_top_s + jnp.log(mass_s)) - picked
    token_loss = lax.dynamic_slice_in_dim(loss, lax.axis_index("vocab") * own, own, 0)

    teacher_prob = jnp.exp(teacher_logits - all_top_t[:, None]) / mass_t[:, None]
    student_prob = jnp.exp(student_logits - all_top_s[:, None]) / mass_s[:, None]
    grad_rows = (2.0 * student_prob - teacher_prob - target.astype(F32)).astype(BF16)
    grad_other = lax.ppermute(grad_rows, "rows", other)
    partial = lax.dot_general(grad_rows, student_head, (((1,), (1,)), ((), ())), preferred_element_type=F32)
    arrived = swap(partial.astype(BF16).reshape(shards, own, student_width))
    hidden_grad = jnp.sum(arrived.astype(F32), axis=0)
    head_grad = lax.dot_general(
        jnp.concatenate([student_rows, student_other], axis=0),
        jnp.concatenate([grad_rows, grad_other], axis=0),
        (((0,), (0,)), ((), ())),
        preferred_element_type=F32,
    )
    return (token_loss, hidden_grad, head_grad)


def solution(mesh):
    tokens = ("groups", "vocab", "rows")
    in_specs = (P(tokens, None), P(tokens, None), P(None, "vocab"), P(None, "vocab"), P(tokens))
    out_specs = (P(tokens), P(tokens, None), P("groups", "vocab"))

    def body(*arrays):
        shards = mesh.shape["vocab"]
        own = arrays[4].shape[0]
        small = own == 2 and shards % 4 == 0 and shards * own <= 24
        return (two_exchanges if small else three_exchanges)(*arrays, shards=shards)

    return jax.shard_map(body, mesh=mesh, in_specs=in_specs, out_specs=out_specs, check_vma=False)
```

```python
import jax
import jax.numpy as jnp
from jax import lax
from jax.experimental import pallas as pl
from jax.experimental.pallas import tpu as pltpu
from jax.sharding import PartitionSpec as P

F32 = jnp.float32
BF16 = jnp.bfloat16
CODE = 128


UNROLL = 16
LANES = 128
PIECES = 14
SMEM = pl.BlockSpec(memory_space=pltpu.SMEM)
VMEM = pl.BlockSpec(memory_space=pltpu.VMEM)
ANY = pl.BlockSpec(memory_space=pl.ANY)
SMALL = pltpu.CompilerParams(vmem_limit_bytes=16 * 1024 * 1024)


def over_shards(shards, body):
    if shards <= UNROLL:
        for shard in range(shards):
            body(shard)
    else:
        pl.loop(0, shards)(body)


def swap(blocks):
    return lax.all_to_all(blocks, "vocab", split_axis=0, concat_axis=0, tiled=True)


def payload_kernel(labels_ref, teacher_ref, student_ref, out_ref):
    shards, own, _ = out_ref.shape
    teacher_width, student_width = teacher_ref.shape[1], student_ref.shape[1]
    teacher = teacher_ref[...]
    student = student_ref[...]
    code = label_digits(labels_ref, own)

    def write(shard):
        out_ref[shard, :, :teacher_width] = teacher
        out_ref[shard, :, teacher_width : teacher_width + student_width] = student
        out_ref[shard, :, teacher_width + student_width :] = code

    over_shards(shards, write)


def label_digits(labels_ref, own):
    row = lax.broadcasted_iota(jnp.int32, (own, CODE), 0)
    lane = lax.broadcasted_iota(jnp.int32, (own, CODE), 1)
    digits = jnp.zeros((own, CODE), jnp.int32)
    for token in range(own):
        label = labels_ref[token]
        pair = jnp.where(lane == 0, label >> 7, label & 127)
        digits = jnp.where(row == token, pair, digits)
    return digits.astype(F32).astype(BF16)


def gather_tokens(teacher_hidden, student_hidden, labels, shards):
    own, teacher_width = teacher_hidden.shape
    student_width = student_hidden.shape[1]
    payload = pl.pallas_call(
        payload_kernel,
        out_shape=jax.ShapeDtypeStruct((shards, own, teacher_width + student_width + CODE), BF16),
        in_specs=[SMEM, VMEM, VMEM],
        out_specs=VMEM,
    )(labels, teacher_hidden, student_hidden)
    return swap(payload)


def raw_partial_kernel(
    first_ref, rows_ref, heads_ref, out_hbm, teacher_ref, student_ref, target_ref, out_ref, sems
):
    tokens = rows_ref.shape[0]
    shards = out_ref.shape[0]
    wide = 8 * shards
    columns = heads_ref.shape[1]
    quarter = (out_ref.shape[2] - 128) // 3
    width = 4 * quarter
    teacher_width = heads_ref.shape[0] - width

    def iota(shape, dim):
        return lax.broadcasted_iota(jnp.int32, shape, dim)

    def dot(left, right, dims):
        return lax.dot_general(left, right, (dims, ((), ())), preferred_element_type=F32)

    copies = []

    def send_out(piece, start, size):
        lanes = pl.ds(start, size)
        copies.append(pltpu.make_async_copy(out_ref.at[:, :, lanes], out_hbm.at[:, :, lanes], sems.at[piece]))
        copies[-1].start()

    student = dot(rows_ref[:, teacher_width : teacher_width + width], heads_ref[teacher_width:, :], ((1,), (0,)))
    teacher = dot(rows_ref[:, :teacher_width], heads_ref[:teacher_width, :], ((1,), (0,)))
    code = rows_ref[:, teacher_width + width :].astype(F32)
    lane = iota(code.shape, 1)
    label = jnp.sum(jnp.where(lane == 0, code * 128.0, jnp.where(lane == 1, code, 0.0)), axis=1, keepdims=True)
    target = (label.astype(jnp.int32) == iota((tokens, columns), 1) + first_ref[...]).astype(F32)
    teacher_ref[...] = teacher
    student_ref[...] = student
    target_ref[...] = target

    def total(array):
        return jnp.sum(array, axis=1, keepdims=True)

    top_t = jnp.max(teacher, axis=1, keepdims=True)
    top_s = jnp.max(student, axis=1, keepdims=True)
    exp_t = jnp.exp(teacher - top_t)
    exp_s = jnp.exp(student - top_s)
    mass_t, mass_s = total(exp_t), total(exp_s)
    guess = jnp.abs(exp_s * (2.0 / mass_s) - exp_t / mass_t)
    lane = iota((tokens, columns), 1)
    largest = jnp.max(guess, axis=1, keepdims=True)
    where_largest = jnp.min(jnp.where(guess == largest, lane, columns), axis=1, keepdims=True)
    has_label = total(target)
    chosen = jnp.where(has_label > 0.5, target, (lane == where_largest).astype(F32))
    stats = [
        top_t,
        mass_t,
        total(exp_t * (teacher - student)),
        top_s,
        mass_s,
        total(chosen * student),
        total(chosen * teacher),
        has_label,
    ]
    lane = iota((tokens, 128), 1)
    table = jnp.zeros((tokens, 128), F32)
    for k, stat in enumerate(stats):
        table = jnp.where(lane % 8 == k, stat, table)
    first = table.astype(BF16).astype(F32)
    second = (table - first).astype(BF16).astype(F32)
    part = (lane % 32) // 8
    parts = jnp.where(
        part == 0, first, jnp.where(part == 1, second, jnp.where(part == 2, table - first - second, 0.0))
    ).astype(BF16)

    row, column = iota((wide, tokens), 0), iota((wide, tokens), 1)
    of_token = (column == (row // 8) * 2 + row % 2).astype(F32).astype(BF16)
    by_row = dot(of_token, parts, ((1,), (0,)))

    lane = iota((8, 128), 1)
    shared = jnp.zeros((8, 128), F32)
    wide_parts = parts.astype(F32)
    for group in range(tokens // 8):
        shared = jnp.where(lane // 32 == group + 1, wide_parts[8 * group : 8 * group + 8], shared)
    for shard in range(shards):
        block = jnp.where(lane < 32, by_row[8 * shard : 8 * shard + 8], shared)
        out_ref[shard, :, 3 * quarter :] = block.astype(BF16)
    send_out(0, 3 * quarter, 128)

    members = jnp.concatenate([exp_s * (1.0 - chosen), exp_t * (1.0 - chosen), chosen], axis=0)
    member_high = members.astype(BF16)
    member_low = (members - member_high.astype(F32)).astype(BF16)
    row, column = iota((wide, 3 * tokens), 0), iota((wide, 3 * tokens), 1)
    place = row % 8
    token = (row // 8) * 2 + row % 2
    pick = ((place < 6) & (column == (place // 2) * tokens + token)).astype(F32).astype(BF16)
    left = dot(pick, jnp.concatenate([member_high, member_low], axis=1), ((1,), (0,))).astype(BF16)
    left = jnp.concatenate([left[:, :columns], left[:, columns:]], axis=0)

    place = iota((wide, 1), 0) % 8
    chunks = quarter // LANES
    first_unsent = 0
    for chunk in range(chunks):
        starts = [teacher_width + j * quarter + chunk * LANES for j in range(4)]
        right = jnp.concatenate([heads_ref[start : start + LANES, :] for start in starts], axis=0)
        both = dot(left, right, ((1,), (1,)))
        exact = [both[:wide, j * LANES : (j + 1) * LANES] + both[wide:, j * LANES : (j + 1) * LANES] for j in range(4)]
        for j in range(3):
            sent = jnp.where(place >= 6, pltpu.roll(exact[3], 6 - 2 * j, 0), exact[j])
            lanes = slice((3 * chunk + j) * LANES, (3 * chunk + j + 1) * LANES)
            for shard in range(shards):
                out_ref[shard, :, lanes] = sent[8 * shard : 8 * shard + 8].astype(BF16)
        if chunk % 3 == 2 or chunk == chunks - 1:
            end = 3 * (chunk + 1) * LANES
            send_out(len(copies), first_unsent, end - first_unsent)
            first_unsent = end
    for copy in copies:
        copy.wait()


def sum_parts(tail):
    shards = tail.shape[0]
    flat = tail.astype(F32).reshape(shards * 8, 128)
    return flat + pltpu.roll(flat, 120, 1) + pltpu.roll(flat, 112, 1)


def fold(flat, lane):
    shards = flat.shape[0] // 8
    stats = [flat[:, lane + k : lane + k + 1].reshape(shards, 8, 1) for k in range(8)]
    top_t = jnp.max(stats[0], axis=0)
    factor_t = jnp.exp(stats[0] - top_t)
    top_s = jnp.max(stats[3], axis=0)
    factor_s = jnp.exp(stats[3] - top_s)
    mass_t = jnp.sum(stats[1] * factor_t, axis=0)
    mass_s = jnp.sum(stats[4] * factor_s, axis=0)
    return stats, top_t, factor_t, mass_t, top_s, factor_s, mass_s


def logit_grad_kernel(tail_ref, teacher_ref, student_ref, target_ref, out_ref):
    flat = sum_parts(tail_ref[...])
    folded = [fold(flat, 32 * group + 32) for group in range(out_ref.shape[0] // 8)]
    top_t, mass_t, top_s, mass_s = [jnp.concatenate([f[i] for f in folded], axis=0) for i in (1, 3, 4, 6)]
    teacher_prob = jnp.exp(teacher_ref[...] - top_t) / mass_t
    student_prob = jnp.exp(student_ref[...] - top_s) / mass_s
    out_ref[...] = (2.0 * student_prob - teacher_prob - target_ref[...]).astype(BF16)


def owner_kernel(arrived_ref, out_ref, loss_ref):
    shards, _, lanes = arrived_ref.shape
    quarter = (lanes - 128) // 3
    stats, top_t, factor_t, mass_t, top_s, factor_s, mass_s = fold(sum_parts(arrived_ref[:, :, 3 * quarter :]), 0)
    cross = jnp.sum(stats[2] * factor_t, axis=0)
    picked = jnp.sum(stats[7] * stats[5], axis=0)
    loss = cross / mass_t - top_t - jnp.log(mass_t) + 2.0 * (top_s + jnp.log(mass_s)) - picked
    token = lax.broadcasted_iota(jnp.int32, (8, 1), 0)
    for t in range(out_ref.shape[0]):
        loss_ref[t] = jnp.sum(jnp.where(token == t, loss, 0.0))
    chosen_s = jnp.exp(stats[5] - top_s) / mass_s
    chosen_t = jnp.exp(stats[6] - top_t) / mass_t
    weight_l = (2.0 * chosen_s - chosen_t - stats[7]).astype(BF16).astype(F32)
    weight_s = 2.0 * (factor_s / mass_s)
    weight_t = -(factor_t / mass_t)
    place = lax.broadcasted_iota(jnp.int32, (shards, 8, 1), 1)
    last = jnp.zeros((8, quarter), F32)
    for j, weight_last in enumerate((weight_s, weight_t, weight_l)):
        weight = jnp.where(
            place < 2, weight_s, jnp.where(place < 4, weight_t, jnp.where(place < 6, weight_l, weight_last))
        )
        piece = []
        for chunk in range(quarter // LANES):
            lanes = slice((3 * chunk + j) * LANES, (3 * chunk + j + 1) * LANES)
            piece.append(sum(weight[shard] * arrived_ref[shard, :, lanes].astype(F32) for shard in range(shards)))
        piece = jnp.concatenate(piece, axis=1)
        last += piece
        out_ref[:, j * quarter : (j + 1) * quarter] = piece[0:2] + piece[2:4] + piece[4:6]
    out_ref[:, 3 * quarter :] = last[6:8]


def head_grad_kernel(hidden_ref, hidden_other_ref, grad_ref, other_ref, out_ref, total_ref, sems):
    grads = jnp.concatenate([grad_ref[...], other_ref[...]], axis=0)
    size = hidden_ref.shape[1] // PIECES
    copies = []
    for piece in range(PIECES):
        rows = pl.ds(piece * size, size)
        hidden = jnp.concatenate([hidden_ref[:, rows], hidden_other_ref[:, rows]], axis=0)
        total_ref[rows, :] = lax.dot_general(hidden, grads, (((0,), (0,)), ((), ())), preferred_element_type=F32)
        copies.append(pltpu.make_async_copy(total_ref.at[rows, :], out_ref.at[rows, :], sems.at[piece]))
        copies[-1].start()
    for copy in copies:
        copy.wait()


def two_exchanges(teacher_hidden, student_hidden, teacher_head, student_head, labels, *, shards):
    own = labels.shape[0]
    teacher_width, width = teacher_hidden.shape[1], student_hidden.shape[1]
    columns_here = student_head.shape[1]
    tokens = shards * own
    quarter = width // 4
    here = lax.axis_index("vocab").astype(jnp.int32)
    rows = gather_tokens(teacher_hidden, student_hidden, labels, shards).reshape(tokens, -1)
    student_rows = rows[:, teacher_width : teacher_width + width]
    other = [(0, 1), (1, 0)]
    student_other = lax.ppermute(student_rows, "rows", other)

    first_column = jnp.full((1, columns_here), here * columns_here, jnp.int32)
    heads = jnp.concatenate([teacher_head, student_head], axis=0)
    square = jax.ShapeDtypeStruct((tokens, columns_here), F32)
    payload, teacher_logits, student_logits, target = pl.pallas_call(
        raw_partial_kernel,
        out_shape=(jax.ShapeDtypeStruct((shards, 8, 3 * quarter + 128), BF16), square, square, square),
        in_specs=[VMEM, VMEM, VMEM],
        out_specs=(ANY, VMEM, VMEM, VMEM),
        scratch_shapes=[pltpu.VMEM((shards, 8, 3 * quarter + 128), BF16), pltpu.SemaphoreType.DMA((2 + quarter // LANES // 3,))],
        compiler_params=SMALL,
    )(first_column, rows, heads)
    arrived = swap(payload)
    grad_rows = pl.pallas_call(
        logit_grad_kernel,
        out_shape=jax.ShapeDtypeStruct((tokens, columns_here), BF16),
        in_specs=[VMEM] * 4,
        out_specs=VMEM,
        compiler_params=SMALL,
    )(arrived[:, :, 3 * quarter :], teacher_logits, student_logits, target)
    grad_other = lax.ppermute(grad_rows, "rows", other)
    hidden_grad, token_loss = pl.pallas_call(
        owner_kernel,
        out_shape=(jax.ShapeDtypeStruct((own, width), F32), jax.ShapeDtypeStruct((own,), F32)),
        in_specs=[VMEM],
        out_specs=(VMEM, SMEM),
        compiler_params=SMALL,
    )(arrived)
    head_grad = pl.pallas_call(
        head_grad_kernel,
        out_shape=jax.ShapeDtypeStruct((width, columns_here), F32),
        in_specs=[VMEM] * 4,
        out_specs=ANY,
        scratch_shapes=[pltpu.VMEM((width, columns_here), F32), pltpu.SemaphoreType.DMA((PIECES,))],
        compiler_params=SMALL,
    )(student_rows, student_other, grad_rows, grad_other)
    return (token_loss, hidden_grad, head_grad)


def three_exchanges(teacher_hidden, student_hidden, teacher_head, student_head, labels, *, shards):
    own = labels.shape[0]
    student_width = student_hidden.shape[1]
    columns_here = student_head.shape[1]
    first_column = lax.axis_index("vocab") * columns_here
    rows = gather_tokens(teacher_hidden, student_hidden, labels, shards).reshape(shards * own, -1)
    teacher_width = teacher_hidden.shape[1]
    teacher_rows = rows[:, :teacher_width]
    student_rows = rows[:, teacher_width : teacher_width + student_width]
    code = rows[:, teacher_width + student_width :].astype(jnp.int32)
    label_rows = code[:, 0] * 128 + code[:, 1]
    other = [(0, 1), (1, 0)]
    student_other = lax.ppermute(student_rows, "rows", other)

    teacher_logits = jnp.dot(teacher_rows, teacher_head, preferred_element_type=F32)
    student_logits = jnp.dot(student_rows, student_head, preferred_element_type=F32)
    columns = lax.broadcasted_iota(jnp.int32, student_logits.shape, 1)
    target = (label_rows - first_column)[:, None] == columns
    top_t = jnp.max(teacher_logits, axis=1, keepdims=True)
    exp_t = jnp.exp(teacher_logits - top_t)
    top_s = jnp.max(student_logits, axis=1, keepdims=True)
    exp_s = jnp.exp(student_logits - top_s)
    stats = jnp.concatenate(
        [
            top_t,
            jnp.sum(exp_t, axis=1, keepdims=True),
            jnp.sum(exp_t * (teacher_logits - student_logits), axis=1, keepdims=True),
            top_s,
            jnp.sum(exp_s, axis=1, keepdims=True),
            jnp.sum(jnp.where(target, student_logits, 0.0), axis=1, keepdims=True),
        ],
        axis=1,
    )
    every = swap(jnp.broadcast_to(stats[None], (shards,) + stats.shape))
    all_top_t = jnp.max(every[:, :, 0], axis=0)
    factor_t = jnp.exp(every[:, :, 0] - all_top_t[None])
    all_top_s = jnp.max(every[:, :, 3], axis=0)
    factor_s = jnp.exp(every[:, :, 3] - all_top_s[None])
    mass_t = jnp.sum(every[:, :, 1] * factor_t, axis=0)
    cross = jnp.sum(every[:, :, 2] * factor_t, axis=0)
    mass_s = jnp.sum(every[:, :, 4] * factor_s, axis=0)
    picked = jnp.sum(every[:, :, 5], axis=0)
    loss = cross / mass_t - all_top_t - jnp.log(mass_t) + 2.0 * (all_top_s + jnp.log(mass_s)) - picked
    token_loss = lax.dynamic_slice_in_dim(loss, lax.axis_index("vocab") * own, own, 0)

    teacher_prob = jnp.exp(teacher_logits - all_top_t[:, None]) / mass_t[:, None]
    student_prob = jnp.exp(student_logits - all_top_s[:, None]) / mass_s[:, None]
    grad_rows = (2.0 * student_prob - teacher_prob - target.astype(F32)).astype(BF16)
    grad_other = lax.ppermute(grad_rows, "rows", other)
    partial = lax.dot_general(grad_rows, student_head, (((1,), (1,)), ((), ())), preferred_element_type=F32)
    arrived = swap(partial.astype(BF16).reshape(shards, own, student_width))
    hidden_grad = jnp.sum(arrived.astype(F32), axis=0)
    head_grad = lax.dot_general(
        jnp.concatenate([student_rows, student_other], axis=0),
        jnp.concatenate([grad_rows, grad_other], axis=0),
        (((0,), (0,)), ((), ())),
        preferred_element_type=F32,
    )
    return (token_loss, hidden_grad, head_grad)


def solution(mesh):
    tokens = ("groups", "vocab", "rows")
    in_specs = (P(tokens, None), P(tokens, None), P(None, "vocab"), P(None, "vocab"), P(tokens))
    out_specs = (P(tokens), P(tokens, None), P("groups", "vocab"))

    def body(*arrays):
        shards = mesh.shape["vocab"]
        own = arrays[4].shape[0]
        small = own == 2 and shards % 4 == 0 and shards * own <= 24
        return (two_exchanges if small else three_exchanges)(*arrays, shards=shards)

    return jax.shard_map(body, mesh=mesh, in_specs=in_specs, out_specs=out_specs, check_vma=False)
```
